32 devices in a mesh: dp: 8 (over y, x, core), ctx: 4 (over z).
Axes of the slice: x: 2, y: 2, z: 4, core: 2. Of those that a mesh axis runs over, the one named last changes fastest.
Arguments:
- queries: bfloat16 [8, 4096, 512], P('dp', 'ctx'), may hold values from -6 to 6
- keys: bfloat16 [8, 4096, 128], P('dp', 'ctx'), may hold values from -6 to 6
- values: bfloat16 [8, 4096, 128], P('dp', 'ctx'), may hold values from -6 to 6
- dest_replica: int32 [8, 64], P('dp', 'ctx'), may hold values from 0 to 7, as said below
- dest_slot: int32 [8, 64], P('dp', 'ctx'), may hold values from 0 to 63, as said below
- doc_lengths: int32 [8, 16], P('dp'), may hold values from 1 to 32, 64 in all within a row
- tile_mask: int32 [8, 64, 64], P('dp', 'ctx'), may hold values 0 or 1
Outputs:
- attended: bfloat16 [8, 4096, 512], P('dp', 'ctx')
The draws below stay inside these ranges and needn't reach their ends.
Inputs may be any that keep to these rules, and one draw needn't show every extreme that they name: `dest_replica`: every block of a pack receives exactly one arriving block; a block keeps its shard along ctx (dest_slot // 16 equals the arriving block's own b // 16); the 16 blocks of one device go to every pack, 2 to each. `dest_slot`: see dest_replica. `doc_lengths`: they sum to 64 in every pack, and the largest is 32 in every pack.
All inputs are finite; a program needn't handle non-finite values. No bound on the sum of `tile_mask` on one device may be relied on, other than what follows from the above.
Results may differ from the reference program's by a relative error of at most 0.0033.
Values may be sent and summed in bfloat16 or wider, within the bound.
No kernel may reach another device: no remote copies, remote signals or barrier semaphores. Data moves between devices by JAX's collectives and lax.ppermute only.
A program may use at most 64 MiB of HBM per device.

```python
import math
import jax
import jax.numpy as jnp
import numpy as np
from jax import lax

HEAD_WIDTH = 128
QUERY_HEADS = 4
KEY_VALUE_HEADS = 1
TOK_DEV = 1024
BLK = 64
REACH = 2
PACK_COUNT = 8
PACK_TOKENS = 4096
NB_DEV = 16
CAP = 2
NBLK = 64
DOC_MOST = 32
DOCS = 16
N_CTX = 4


def routing_pair(key):
    column_total = NBLK // NB_DEV

    def one_column(column):
        column_key = jax.random.fold_in(jax.random.fold_in(key, 101), column)
        shifts = jax.random.permutation(jax.random.fold_in(column_key, 1), PACK_COUNT)[:NB_DEV // CAP]
        order_key = jax.random.fold_in(column_key, 2)

        def pack_ordering(pack):
            return jax.random.permutation(jax.random.fold_in(order_key, pack), NB_DEV).astype(jnp.int32)
        orderings = jax.vmap(pack_ordering)(jnp.arange(PACK_COUNT, dtype=jnp.int32))
        positions = jnp.arange(NB_DEV, dtype=jnp.int32)
        shift_of = shifts[positions // CAP].astype(jnp.int32)
        replicas = jnp.arange(PACK_COUNT, dtype=jnp.int32)
        target_replica = ((replicas[:, None] + shift_of[None, :]) % PACK_COUNT).astype(jnp.int32)
        chosen = jnp.take_along_axis(orderings, target_replica, axis=0).astype(jnp.int32)
        target_slot = (column * NB_DEV + chosen).astype(jnp.int32)
        return (target_replica, target_slot)
    target_replica, target_slot = jax.vmap(one_column)(jnp.arange(column_total, dtype=jnp.int32))
    target_replica = jnp.transpose(target_replica, (1, 0, 2)).reshape(PACK_COUNT, NBLK).astype(jnp.int32)
    target_slot = jnp.transpose(target_slot, (1, 0, 2)).reshape(PACK_COUNT, NBLK).astype(jnp.int32)
    return (target_replica, target_slot)


def draw_dest_replica(key, part):
    return routing_pair(key)[0]


def draw_dest_slot(key, part):
    return routing_pair(key)[1]


def query_key_pair(key):
    base_q = jax.random.normal(jax.random.fold_in(key, 201), (PACK_COUNT, PACK_TOKENS, QUERY_HEADS * HEAD_WIDTH), jnp.float32)
    starting_key = jax.random.normal(jax.random.fold_in(key, 202), (PACK_COUNT, PACK_TOKENS, KEY_VALUE_HEADS * HEAD_WIDTH), jnp.float32)
    return (jnp.clip(base_q, -6.0, 6.0), jnp.clip(starting_key, -6.0, 6.0))


def draw_queries(key, part):
    return query_key_pair(key)[0].astype(jnp.bfloat16)


def draw_keys(key, part):
    return query_key_pair(key)[1].astype(jnp.bfloat16)


def plant(values, key, low, high):
    index_at = [jax.random.randint(jax.random.fold_in(key, axis), (), 0, length) for axis, length in enumerate(values.shape)]
    widest = values.shape.index(max(values.shape))
    beside = index_at[:widest] + [(index_at[widest] + 1) % values.shape[widest]] + index_at[widest + 1:]
    return values.at[tuple(index_at)].set(low).at[tuple(beside)].set(high)


def level_of(stream_key, extent, split, least, top_value):
    factor_of = 1.0
    for position, parts in split:
        heights = jax.random.uniform(jax.random.fold_in(jax.random.fold_in(stream_key, 6), position), (parts,), jnp.float32, least / len(split), top_value / len(split))
        factor_of = factor_of * jnp.repeat(jnp.exp(heights), extent[position] // parts).reshape((-1,) + (1,) * (len(extent) - 1 - position))
    return factor_of


def profile(number_of, total, reach, skew):
    weights = [(1 << 20) // math.isqrt(grade ** skew) + 1 for grade in range(2, number_of + 1)]
    rest, counts = total - reach - (number_of - 1), [1] * (number_of - 1)
    while rest > 0:
        movable = [i for i in range(number_of - 1) if counts[i] < reach]
        pool, budget = sum([weights[i] for i in movable]), rest
        for i in movable:
            addition = min(reach - counts[i], max(1, budget * weights[i] // pool), rest)
            counts[i] = counts[i] + addition
            rest = rest - addition
    return np.array([reach] + counts)


def uneven(own_key, number_of, total, most, slope):
    if number_of == 2:
        one = jax.random.randint(own_key, (), max(1, total - most), min(most, total - 1) + 1)
        return jnp.stack([one, total - one])
    tallies = jnp.asarray(profile(number_of, total, most, slope), jnp.int32)
    pairs = (number_of - 1) // 2
    donor, receiver = tallies[1:1 + 2 * pairs:2], tallies[2:2 + 2 * pairs:2]
    room = jnp.minimum(donor - 1, most - receiver)
    moved = jax.random.randint(jax.random.fold_in(own_key, 1), (pairs,), 0, 1 << 20) % (room + 1)
    tallies = tallies.at[1:1 + 2 * pairs:2].set(donor - moved).at[2:2 + 2 * pairs:2].set(receiver + moved)
    return tallies[jax.random.permutation(jax.random.fold_in(own_key, 2), number_of)]


def noise(stream_key, shape, spread, limit, cuts=(), held_as=jnp.bfloat16):
    drawn = spread * jax.random.normal(stream_key, shape, jnp.float32)
    if cuts:
        drawn = drawn * level_of(stream_key, shape, cuts, -0.22, 0.18)
    return jnp.clip(drawn, -limit, limit).astype(held_as)


def setup_inputs(seed: int = 0) -> dict:
    key_of = jax.random.split(jax.random.key(seed), 8)
    return {
        "queries": draw_queries(jax.random.fold_in(key_of[7], 71), 0),
        "keys": draw_keys(jax.random.fold_in(key_of[7], 71), 0),
        "values": noise(key_of[2], (PACK_COUNT, PACK_TOKENS, KEY_VALUE_HEADS * HEAD_WIDTH), 1.0, 6.0, ((0, 8), (1, 4))),
        "dest_replica": draw_dest_replica(jax.random.fold_in(key_of[7], 71), 0),
        "dest_slot": draw_dest_slot(jax.random.fold_in(key_of[7], 71), 0),
        "doc_lengths": jax.vmap(lambda own: uneven(own, DOCS, NBLK, DOC_MOST, 2))(jax.random.split(key_of[5], PACK_COUNT)).reshape((PACK_COUNT, DOCS)).astype(jnp.int32),
        "tile_mask": plant((jax.random.randint(key_of[6], (PACK_COUNT, NBLK, NBLK), 0, 4) < 3).astype(jnp.int32), jax.random.fold_in(key_of[6], 1), 0, 1),
    }


def block_docs(ends, block_ids):
    return jnp.sum((ends[None, :] <= block_ids[:, None]).astype(jnp.int32), axis=1).astype(jnp.int32)


def shard_attend(rows_of_queries, rows_of_keys, rows_of_values, allowed):
    count_of_rows = rows_of_queries.shape[0]
    query_group_width = QUERY_HEADS // KEY_VALUE_HEADS
    heads_of_queries = rows_of_queries.astype(jnp.float32).reshape(count_of_rows, KEY_VALUE_HEADS, query_group_width, HEAD_WIDTH)
    heads_of_keys = rows_of_keys.astype(jnp.float32).reshape(count_of_rows, KEY_VALUE_HEADS, HEAD_WIDTH)
    heads_of_values = rows_of_values.astype(jnp.float32).reshape(count_of_rows, KEY_VALUE_HEADS, HEAD_WIDTH)
    scores = jnp.einsum("qhgd,khd->hgqk", heads_of_queries, heads_of_keys) * (HEAD_WIDTH ** -0.5)
    masked = jnp.where(allowed, scores, -jnp.inf)
    row_max = jnp.max(masked, axis=-1)
    present = jnp.any(allowed, axis=-1)
    safe_max = jnp.where(present, row_max, jnp.float32(0.0))
    weights = jnp.where(allowed, jnp.exp(scores - safe_max[..., None]), jnp.float32(0.0))
    row_sum = jnp.sum(weights, axis=-1)
    rounded = lax.optimization_barrier(weights.astype(jnp.bfloat16))
    partial_value = jnp.einsum("hgqk,khd->qhgd", rounded.astype(jnp.float32), heads_of_values)
    return row_max, row_sum, partial_value


def combine(portions):
    overall = portions[0][0]
    for portion in portions[1:]:
        overall = jnp.maximum(overall, portion[0])
    denominator = jnp.zeros_like(overall)
    numerator = jnp.zeros_like(portions[0][2])
    for portion in portions:
        factor = jnp.exp(portion[0] - overall)
        denominator = denominator + factor * portion[1]
        numerator = numerator + jnp.transpose(factor, (2, 0, 1))[..., None] * portion[2]
    result = numerator / jnp.transpose(denominator, (2, 0, 1))[..., None]
    return result.reshape(result.shape[0], -1).astype(jnp.bfloat16)


def reference(queries, keys, values, dest_replica, dest_slot, doc_lengths, tile_mask):
    targets = (dest_replica * NBLK + dest_slot).reshape(-1).astype(jnp.int32)

    def route(array):
        blocks = array.reshape(PACK_COUNT * NBLK, BLK, array.shape[-1])
        placed = jnp.zeros_like(blocks).at[targets].set(blocks)
        return placed.reshape(PACK_COUNT, PACK_TOKENS, array.shape[-1])

    routed_q = route(queries)
    routed_k = route(keys)
    routed_v = route(values)
    ends = jnp.cumsum(doc_lengths, axis=1).astype(jnp.int32)
    block_index = jnp.arange(NB_DEV, dtype=jnp.int32)
    token_index = jnp.arange(TOK_DEV, dtype=jnp.int32)

    def one_shard(index):
        replica = (index // N_CTX).astype(jnp.int32)
        column = (index % N_CTX).astype(jnp.int32)
        pack_q = lax.dynamic_index_in_dim(routed_q, replica, 0, keepdims=False)
        pack_k = lax.dynamic_index_in_dim(routed_k, replica, 0, keepdims=False)
        pack_v = lax.dynamic_index_in_dim(routed_v, replica, 0, keepdims=False)
        pack_ends = lax.dynamic_index_in_dim(ends, replica, 0, keepdims=False)
        pack_mask = lax.dynamic_index_in_dim(tile_mask, replica, 0, keepdims=False)
        mask_rows = lax.dynamic_slice_in_dim(pack_mask, (column * NB_DEV).astype(jnp.int32), NB_DEV, 0)
        rows_of_queries = lax.dynamic_slice_in_dim(pack_q, (column * TOK_DEV).astype(jnp.int32), TOK_DEV, 0)
        query_blocks = column * NB_DEV + block_index
        query_docs = block_docs(pack_ends, query_blocks)
        query_pos = column * TOK_DEV + token_index
        portions = []
        for offset in range(REACH + 1):
            source = jnp.maximum(column - offset, 0).astype(jnp.int32)
            rows_of_keys = lax.dynamic_slice_in_dim(pack_k, (source * TOK_DEV).astype(jnp.int32), TOK_DEV, 0)
            rows_of_values = lax.dynamic_slice_in_dim(pack_v, (source * TOK_DEV).astype(jnp.int32), TOK_DEV, 0)
            key_blocks = (column - offset) * NB_DEV + block_index
            key_docs = block_docs(pack_ends, key_blocks)
            mask_cols = lax.dynamic_slice_in_dim(mask_rows, (source * NB_DEV).astype(jnp.int32), NB_DEV, 1)
            tile_ok = (query_docs[:, None] == key_docs[None, :]) & (key_blocks[None, :] <= query_blocks[:, None])
            tile_ok = tile_ok & ((mask_cols == 1) | (key_blocks[None, :] == query_blocks[:, None]))
            tile_ok = tile_ok & (key_blocks[None, :] >= 0)
            expanded = jnp.repeat(jnp.repeat(tile_ok, BLK, axis=0), BLK, axis=1)
            key_pos = (column - offset) * TOK_DEV + token_index
            allowed = expanded & (key_pos[None, :] <= query_pos[:, None])
            portions.append(shard_attend(rows_of_queries, rows_of_keys, rows_of_values, allowed))
        return combine(portions)

    shards = lax.map(one_shard, jnp.arange(PACK_COUNT * N_CTX, dtype=jnp.int32))
    return shards.reshape(PACK_COUNT, PACK_TOKENS, QUERY_HEADS * HEAD_WIDTH)
```

```python
import functools

import jax
import jax.numpy as jnp
from jax import lax
from jax.experimental import pallas as pl
from jax.experimental.pallas import tpu as pltpu
from jax.sharding import PartitionSpec as P

HEAD_WIDTH = 128
QUERY_HEADS = 4
SCALE = HEAD_WIDTH ** (-0.5) * 1.4426950408889634
NEVER = -1e30
FLOOR = -5e29
VMEM_LIMIT = 48 * 1024 * 1024

ANY = pl.BlockSpec(memory_space=pl.ANY)
SMEM = pl.BlockSpec(memory_space=pltpu.SMEM)
VMEM = pl.BlockSpec(memory_space=pltpu.VMEM)


def shifted(value, axis):
    count = lax.axis_size(axis)
    return lax.ppermute(value, axis, [(source, source + 1) for source in range(count - 1)])


def pack_kv_kernel(cap, targets, slots, keys, values, send, table, counts, sem):
    packs = send.shape[0]
    blocks = targets.shape[1]
    size = keys.shape[1] // blocks
    for t in range(packs):
        counts[t] = 0

    def step(j, carry):
        t = targets[0, j]
        rank = counts[t]
        counts[t] = rank + 1
        table[0, t * cap + rank] = lax.rem(slots[0, j], blocks)
        rows = pl.ds(pl.multiple_of(j * size, size), size)
        to = pl.ds(pl.multiple_of(rank * size, size), size)
        pltpu.make_async_copy(keys.at[0, rows], send.at[t, 0, to], sem).start()
        pltpu.make_async_copy(values.at[0, rows], send.at[t, 1, to], sem).start()
        return carry

    lax.fori_loop(0, blocks, step, 0, unroll=True)
    pltpu.make_async_copy(send, send, sem).wait()


def pack_q_kernel(cap, targets, queries, send, counts, sem):
    packs = send.shape[0]
    blocks = targets.shape[1]
    size = queries.shape[1] // blocks
    for t in range(packs):
        counts[t] = 0

    def step(j, carry):
        t = targets[0, j]
        rank = counts[t]
        counts[t] = rank + 1
        rows = pl.ds(pl.multiple_of(j * size, size), size)
        to = pl.ds(pl.multiple_of(rank * size, size), size)
        pltpu.make_async_copy(queries.at[0, rows], send.at[t, to], sem).start()
        return carry

    lax.fori_loop(0, blocks, step, 0, unroll=True)
    pltpu.make_async_copy(send, send, sem).wait()


def first_document(lengths, position):
    start, end = jnp.int32(0), jnp.int32(0)
    total = jnp.int32(0)
    for j in range(lengths.shape[1]):
        after = total + lengths[0, j]
        inside = (total <= position) & (position < after)
        start = jnp.where(inside, total, start)
        end = jnp.where(inside, after, end)
        total = after
    return start, end


def reach_of(lengths, place, offset, blocks):
    start, end = first_document(lengths, place * blocks)
    low = (place - offset) * blocks
    rows = jnp.where(start < low + blocks, jnp.minimum(end - place * blocks, blocks), 0)
    return jnp.where(low >= 0, rows, 0), jnp.maximum(start - low, 0)


def fill_bias(bias, lengths, tiles, place, offset, blocks, size):
    tokens = blocks * size
    total_blocks = tiles.shape[2]
    key_block = (place - offset) * blocks + lax.broadcasted_iota(jnp.int32, (1, tokens), 1) // size
    query_block = place * blocks + lax.broadcasted_iota(jnp.int32, (blocks, 1), 0)
    key_doc = jnp.zeros((1, tokens), jnp.int32)
    query_doc = jnp.zeros((blocks, 1), jnp.int32)
    end = jnp.int32(0)
    for j in range(lengths.shape[1]):
        end = end + lengths[0, j]
        key_doc = key_doc + (key_block >= end).astype(jnp.int32)
        query_doc = query_doc + (query_block >= end).astype(jnp.int32)
    spread = lax.broadcasted_iota(jnp.int32, (total_blocks, tokens), 0) == key_block
    listed = jnp.dot(
        tiles[0].astype(jnp.float32).astype(jnp.bfloat16),
        spread.astype(jnp.float32).astype(jnp.bfloat16),
        preferred_element_type=jnp.float32,
    )
    allowed = (query_doc == key_doc) & (key_block <= query_block) & (key_block >= 0)
    allowed = allowed & ((listed > 0.5) | (key_block == query_block))
    bias[...] = jnp.where(allowed, 0.0, NEVER)


def place_kv(table, received, pack, place, offset, cap, keys, values, sem):
    packs = received.shape[0]
    ranks = lax.axis_size("ctx")
    size = received.shape[2] // cap
    source_place = jnp.maximum(place - offset, 0)
    for s in range(packs):
        for i in range(cap):
            slot = table[s * ranks + source_place, pack * cap + i]
            rows = pl.ds(pl.multiple_of(slot * size, size), size)
            block = pl.ds(i * size, size)
            pltpu.make_async_copy(received.at[s, 0, block], keys.at[rows], sem.at[0]).start()
            pltpu.make_async_copy(
                received.at[s, 1, block], values.at[rows, pl.ds(0, HEAD_WIDTH)], sem.at[1]
            ).start()
    values[:, HEAD_WIDTH:] = jnp.ones((values.shape[0], HEAD_WIDTH), jnp.bfloat16)


def wait_kv(keys, values, sem):
    half = values.at[:, pl.ds(0, HEAD_WIDTH)]
    pltpu.make_async_copy(keys, keys, sem.at[0]).wait()
    pltpu.make_async_copy(half, half, sem.at[1]).wait()


def place_q(table, received, pack, place, cap, queries, sem):
    packs = received.shape[0]
    ranks = lax.axis_size("ctx")
    size = received.shape[1] // cap
    for s in range(packs):
        for i in range(cap):
            slot = table[s * ranks + place, pack * cap + i]
            rows = pl.ds(pl.multiple_of(slot * size, size), size)
            pltpu.make_async_copy(
                received.at[s, pl.ds(i * size, size)], queries.at[rows], sem
            ).start()


def heads_as_rows(block):
    return jnp.concatenate(
        [block[:, h * HEAD_WIDTH:(h + 1) * HEAD_WIDTH] for h in range(QUERY_HEADS)], axis=0
    )


def heads_as_columns(rows, size):
    return jnp.concatenate(
        [rows[h * size:(h + 1) * size] for h in range(QUERY_HEADS)], axis=1
    )


def attend(query_rows, keys, values, bias):
    scores = lax.dot_general(
        query_rows, keys, (((1,), (1,)), ((), ())), preferred_element_type=jnp.float32
    )
    scores = scores * SCALE + bias
    top = jnp.maximum(jnp.max(scores, axis=1, keepdims=True), FLOOR)
    weights = jnp.exp2(scores - top).astype(jnp.bfloat16)
    return top, jnp.dot(weights, values, preferred_element_type=jnp.float32)


def own_kernel(
    cap, table, lengths, tiles, q_recv, kv_recv,
    out, state_o, state_l,
    queries, keys, values, bias, tri, stage, stage_o, stage_l, sem_in, sem_out, sem_state,
):
    place = lax.axis_index("ctx")
    pack = lax.axis_index("dp")
    tokens = queries.shape[0]
    blocks = bias.shape[0]
    size = tokens // blocks
    place_kv(table, kv_recv, pack, place, 0, cap, keys, values, sem_in)
    place_q(table, q_recv, pack, place, cap, queries, sem_in.at[2])
    fill_bias(bias, lengths, tiles, place, 0, blocks, size)
    row = lax.rem(lax.broadcasted_iota(jnp.int32, tri.shape[1:], 0), size)
    lane = lax.broadcasted_iota(jnp.int32, tri.shape[1:], 1)
    for parity in range(2):
        tri[parity] = jnp.where(lane - parity * size <= row, 0.0, NEVER)
    reads, _ = reach_of(lengths, place, 1, blocks)
    wait_kv(keys, values, sem_in)
    pltpu.make_async_copy(queries, queries, sem_in.at[2]).wait()

    copies = []
    for i in range(blocks):
        rows = slice(i * size, (i + 1) * size)
        width = (i // 2 + 1) * 2 * size
        query_rows = heads_as_rows(queries[rows, :])
        last = bias[i:i + 1, width - 2 * size:width] + tri[i % 2]
        scores = lax.dot_general(
            query_rows, keys[:width, :], (((1,), (1,)), ((), ())),
            preferred_element_type=jnp.float32,
        ) * SCALE
        tail = scores[:, width - 2 * size:] + last
        if width > 2 * size:
            head = scores[:, :width - 2 * size] + bias[i:i + 1, :width - 2 * size]
            scores = jnp.concatenate([head, tail], axis=1)
        else:
            scores = tail
        top = jnp.max(scores, axis=1, keepdims=True)
        weights = jnp.exp2(scores - top).astype(jnp.bfloat16)
        sums = jnp.dot(weights, values[:width, :], preferred_element_type=jnp.float32)
        denominator = sums[:, HEAD_WIDTH:]
        result = sums[:, :HEAD_WIDTH] / denominator
        stage[rows, :] = heads_as_columns(result, size).astype(jnp.bfloat16)
        group = pl.ds(i * QUERY_HEADS * size, QUERY_HEADS * size)
        stage_o[group, :] = result
        stage_l[group, :] = top + jnp.log2(denominator)
        copy = pltpu.make_async_copy(stage.at[rows], out.at[0, rows], sem_out.at[i])
        copy.start()
        copies.append(copy)

    @pl.when(reads > 0)
    def _():
        first = pltpu.make_async_copy(stage_o, state_o, sem_state.at[0])
        second = pltpu.make_async_copy(stage_l, state_l, sem_state.at[1])
        first.start()
        second.start()
        first.wait()
        second.wait()

    for copy in copies:
        copy.wait()


def hop_kernel(
    cap, offset, table, lengths, tiles, q_recv, kv_recv, out_in, state_o_in, state_l_in,
    out, state_o, state_l,
    queries, keys, values, bias, stage, stage_o, stage_l, sem_in, sem_state, sem_out, sem_back,
):
    place = lax.axis_index("ctx")
    pack = lax.axis_index("dp")
    tokens = queries.shape[0]
    blocks = bias.shape[0]
    size = tokens // blocks
    group = QUERY_HEADS * size
    reads, first = reach_of(lengths, place, offset, blocks)

    @pl.when(reads > 0)
    def _():
        place_kv(table, kv_recv, pack, place, offset, cap, keys, values, sem_in)
        place_q(table, q_recv, pack, place, cap, queries, sem_in.at[2])
        load_o = pltpu.make_async_copy(state_o_in, stage_o, sem_state.at[0])
        load_l = pltpu.make_async_copy(state_l_in, stage_l, sem_state.at[1])
        load_o.start()
        load_l.start()
        fill_bias(bias, lengths, tiles, place, offset, blocks, size)
        wait_kv(keys, values, sem_in)
        pltpu.make_async_copy(queries, queries, sem_in.at[2]).wait()
        load_o.wait()
        load_l.wait()

        def over(low):
            def step(i, carry):
                rows = pl.ds(pl.multiple_of(i * size, size), size)
                span = pl.ds(pl.multiple_of(i * group, group), group)
                query_rows = heads_as_rows(queries[rows, :])
                top, sums = attend(
                    query_rows, keys[low:, :], values[low:, :], bias[pl.ds(i, 1), low:]
                )
                before = stage_l[span, :]
                most = jnp.maximum(before, top)
                old = jnp.exp2(before - most)
                new = jnp.exp2(top - most)
                denominator = old + new * sums[:, HEAD_WIDTH:]
                result = (
                    old * stage_o[span, :] + new * sums[:, :HEAD_WIDTH]
                ) / denominator
                stage[rows, :] = heads_as_columns(result, size).astype(jnp.bfloat16)
                stage_o[span, :] = result
                stage_l[span, :] = most + jnp.log2(denominator)
                pltpu.make_async_copy(stage.at[rows], out.at[0, rows], sem_out).start()
                return carry

            lax.fori_loop(0, reads, step, 0)

        quarter = tokens // 4
        part = first // (blocks // 4)
        for n in range(4):
            pl.when(part == n)(functools.partial(over, n * quarter))

        def finish(i, carry):
            rows = pl.ds(pl.multiple_of(i * size, size), size)
            pltpu.make_async_copy(stage.at[rows], out.at[0, rows], sem_out).wait()
            return carry

        lax.fori_loop(0, reads, finish, 0)
        if offset == 1:
            store_o = pltpu.make_async_copy(stage_o, state_o, sem_back.at[0])
            store_l = pltpu.make_async_copy(stage_l, state_l, sem_back.at[1])
            store_o.start()
            store_l.start()
            store_o.wait()
            store_l.wait()


def per_device(queries, keys, values, dest_replica, dest_slot, doc_lengths, tile_mask):
    tokens = queries.shape[1]
    width = queries.shape[2]
    blocks = dest_replica.shape[1]
    size = tokens // blocks
    packs = lax.axis_size("dp")
    cap = blocks // packs
    bf16, f32 = jnp.bfloat16, jnp.float32
    rows = tokens * QUERY_HEADS
    params = pltpu.CompilerParams(vmem_limit_bytes=VMEM_LIMIT)

    def cost(flops, moved):
        return pl.CostEstimate(flops=flops, bytes_accessed=moved, transcendentals=0)

    kv_send, table = pl.pallas_call(
        functools.partial(pack_kv_kernel, cap),
        out_shape=(
            jax.ShapeDtypeStruct((packs, 2, cap * size, HEAD_WIDTH), bf16),
            jax.ShapeDtypeStruct((1, blocks), jnp.int32),
        ),
        in_specs=[SMEM, SMEM, ANY, ANY],
        out_specs=(ANY, SMEM),
        scratch_shapes=[pltpu.SMEM((packs,), jnp.int32), pltpu.SemaphoreType.DMA],
        cost_estimate=cost(0, 4 * tokens * HEAD_WIDTH * 2),
        name="pack_kv",
    )(dest_replica, dest_slot, keys, values)
    kv_recv = lax.all_to_all(kv_send, "dp", split_axis=0, concat_axis=0, tiled=True)
    table = lax.all_gather(table, ("dp", "ctx"), axis=0, tiled=True)
    q_send = pl.pallas_call(
        functools.partial(pack_q_kernel, cap),
        out_shape=jax.ShapeDtypeStruct((packs, cap * size, width), bf16),
        in_specs=[SMEM, ANY],
        out_specs=ANY,
        scratch_shapes=[pltpu.SMEM((packs,), jnp.int32), pltpu.SemaphoreType.DMA],
        cost_estimate=cost(0, 2 * tokens * width * 2),
        name="pack_q",
    )(dest_replica, queries)
    q_recv = lax.all_to_all(q_send, "dp", split_axis=0, concat_axis=0, tiled=True)

    state_shapes = (
        jax.ShapeDtypeStruct((1, tokens, width), bf16),
        jax.ShapeDtypeStruct((rows, HEAD_WIDTH), f32),
        jax.ShapeDtypeStruct((rows, HEAD_WIDTH), f32),
    )
    inputs = [
        pltpu.VMEM((tokens, width), bf16),
        pltpu.VMEM((tokens, HEAD_WIDTH), bf16),
        pltpu.VMEM((tokens, 2 * HEAD_WIDTH), bf16),
        pltpu.VMEM((blocks, tokens), f32),
    ]
    staged = [
        pltpu.VMEM((tokens, width), bf16),
        pltpu.VMEM((rows, HEAD_WIDTH), f32),
        pltpu.VMEM((rows, HEAD_WIDTH), f32),
    ]
    dma = pltpu.SemaphoreType.DMA
    state = pl.pallas_call(
        functools.partial(own_kernel, cap),
        out_shape=state_shapes,
        in_specs=[SMEM, SMEM, VMEM, ANY, ANY],
        out_specs=(ANY, ANY, ANY),
        scratch_shapes=inputs
        + [pltpu.VMEM((2, QUERY_HEADS * size, 2 * size), f32)]
        + staged
        + [dma((3,)), dma((blocks,)), dma((2,))],
        compiler_params=params,
        cost_estimate=cost(2 * 2 * rows * tokens * HEAD_WIDTH, 8 * tokens * width),
        name="attend_own",
    )(table, doc_lengths, tile_mask, q_recv, kv_recv)
    moving = kv_recv
    for offset in (1, 2):
        moving = shifted(moving, "ctx")
        state = pl.pallas_call(
            functools.partial(hop_kernel, cap, offset),
            out_shape=state_shapes,
            in_specs=[SMEM, SMEM, VMEM, ANY, ANY, ANY, ANY, ANY],
            out_specs=(ANY, ANY, ANY),
            scratch_shapes=inputs + staged + [dma((3,)), dma((2,)), dma, dma((2,))],
            input_output_aliases={5: 0, 6: 1, 7: 2},
            compiler_params=params,
            cost_estimate=cost(2 * 2 * rows * tokens * HEAD_WIDTH, 8 * tokens * width),
            name=f"attend_back_{offset}",
        )(table, doc_lengths, tile_mask, q_recv, moving, *state)
    return state[0]


def solution(mesh):
    return jax.shard_map(
        per_device,
        mesh=mesh,
        in_specs=(
            P("dp", "ctx", None),
            P("dp", "ctx", None),
            P("dp", "ctx", None),
            P("dp", "ctx"),
            P("dp", "ctx"),
            P("dp", None),
            P("dp", "ctx", None),
        ),
        out_specs=P("dp", "ctx", None),
        check_vma=False,
    )
```

```python
import functools

import jax
import jax.numpy as jnp
from jax import lax
from jax.experimental import pallas as pl
from jax.experimental.pallas import tpu as pltpu
from jax.sharding import PartitionSpec as P

HEAD_WIDTH = 128
QUERY_HEADS = 4
SCALE = HEAD_WIDTH ** (-0.5) * 1.4426950408889634
NEVER = -1e30
FLOOR = -5e29
SLOT_ROWS = 16
VMEM_LIMIT = 48 * 1024 * 1024

ANY = pl.BlockSpec(memory_space=pl.ANY)
SMEM = pl.BlockSpec(memory_space=pltpu.SMEM)
VMEM = pl.BlockSpec(memory_space=pltpu.VMEM)


def shifted(value, axis):
    count = lax.axis_size(axis)
    return lax.ppermute(value, axis, [(source, source + 1) for source in range(count - 1)])


def pack_kv_kernel(cap, targets, slots, keys, values, send, counts, slot_of):
    packs = send.shape[0]
    blocks = targets.shape[1]
    size = keys.shape[1] // blocks
    half = cap * size
    for t in range(packs):
        counts[t] = 0
    for j in range(blocks):
        t = targets[0, j]
        rank = counts[t]
        counts[t] = rank + 1
        slot_of[t * cap + rank] = lax.rem(slots[0, j], blocks)
        rows = slice(j * size, (j + 1) * size)
        to = pl.multiple_of(rank * size, size)
        send[t, pl.ds(to, size), :] = keys[0, rows, :]
        send[t, pl.ds(to + half, size), :] = values[0, rows, :]
    row = lax.broadcasted_iota(jnp.int32, (SLOT_ROWS, HEAD_WIDTH), 0)
    for t in range(packs):
        listed = jnp.zeros(row.shape, jnp.int32)
        for i in range(cap):
            listed = jnp.where(row == i, slot_of[t * cap + i], listed)
        send[t, 2 * half:, :] = listed.astype(jnp.float32).astype(jnp.bfloat16)


def pack_q_kernel(cap, targets, queries, send, counts):
    packs = send.shape[0]
    blocks = targets.shape[1]
    size = queries.shape[1] // blocks
    for t in range(packs):
        counts[t] = 0
    for j in range(blocks):
        t = targets[0, j]
        rank = counts[t]
        counts[t] = rank + 1
        to = pl.multiple_of(rank * size, size)
        send[t, pl.ds(to, size), :] = queries[0, j * size:(j + 1) * size, :]


def place_kernel(cap, received, placed, order):
    packs = received.shape[0]
    size = placed.shape[1] // (packs * cap)
    half = cap * size
    for s in range(packs):
        listed = received[s, 2 * half:, :].astype(jnp.float32).astype(jnp.int32)
        for i in range(cap):
            slot = listed[i, 0]
            order[0, slot] = s * cap + i
            rows = pl.ds(pl.multiple_of(slot * size, size), size)
            placed[0, rows, :] = received[s, i * size:(i + 1) * size, :]
            placed[1, rows, :] = received[s, half + i * size:half + (i + 1) * size, :]


def first_document(lengths, position):
    start, end = jnp.int32(0), jnp.int32(0)
    total = jnp.int32(0)
    for j in range(lengths.shape[1]):
        after = total + lengths[0, j]
        inside = (total <= position) & (position < after)
        start = jnp.where(inside, total, start)
        end = jnp.where(inside, after, end)
        total = after
    return start, end


def reach_of(lengths, place, offset, blocks):
    start, end = first_document(lengths, place * blocks)
    low = (place - offset) * blocks
    rows = jnp.where(start < low + blocks, jnp.minimum(end - place * blocks, blocks), 0)
    return jnp.where(low >= 0, rows, 0), jnp.maximum(start - low, 0)


def fill_bias(bias, lengths, tiles, place, offset, blocks, size):
    tokens = blocks * size
    total_blocks = tiles.shape[2]
    key_block = (place - offset) * blocks + lax.broadcasted_iota(jnp.int32, (1, tokens), 1) // size
    query_block = place * blocks + lax.broadcasted_iota(jnp.int32, (blocks, 1), 0)
    key_doc = jnp.zeros((1, tokens), jnp.int32)
    query_doc = jnp.zeros((blocks, 1), jnp.int32)
    end = jnp.int32(0)
    for j in range(lengths.shape[1]):
        end = end + lengths[0, j]
        key_doc = key_doc + (key_block >= end).astype(jnp.int32)
        query_doc = query_doc + (query_block >= end).astype(jnp.int32)
    spread = lax.broadcasted_iota(jnp.int32, (total_blocks, tokens), 0) == key_block
    listed = jnp.dot(
        tiles[0].astype(jnp.float32).astype(jnp.bfloat16),
        spread.astype(jnp.float32).astype(jnp.bfloat16),
        preferred_element_type=jnp.float32,
    )
    allowed = (query_doc == key_doc) & (key_block <= query_block) & (key_block >= 0)
    allowed = allowed & ((listed > 0.5) | (key_block == query_block))
    bias[...] = jnp.where(allowed, 0.0, NEVER)


def heads_as_rows(block):
    return jnp.concatenate(
        [block[:, h * HEAD_WIDTH:(h + 1) * HEAD_WIDTH] for h in range(QUERY_HEADS)], axis=0
    )


def heads_as_columns(rows, size):
    return jnp.concatenate(
        [rows[h * size:(h + 1) * size] for h in range(QUERY_HEADS)], axis=1
    )


def attend(query_rows, keys, values, bias):
    scores = lax.dot_general(
        query_rows, keys, (((1,), (1,)), ((), ())), preferred_element_type=jnp.float32
    )
    scores = scores * SCALE + bias
    top = jnp.maximum(jnp.max(scores, axis=1, keepdims=True), FLOOR)
    weights = jnp.exp2(scores - top).astype(jnp.bfloat16)
    return top, jnp.dot(weights, values, preferred_element_type=jnp.float32)


def with_ones(values):
    return jnp.concatenate([values, jnp.ones(values.shape, values.dtype)], axis=1)


def own_kernel(
    order, lengths, tiles, received, kv,
    out, state_o, state_l,
    bias, tri, stage, sem,
):
    place = lax.axis_index("ctx")
    blocks, tokens = bias.shape
    size = tokens // blocks
    group = QUERY_HEADS * size
    fill_bias(bias, lengths, tiles, place, 0, blocks, size)
    row = lax.rem(lax.broadcasted_iota(jnp.int32, tri.shape[1:], 0), size)
    lane = lax.broadcasted_iota(jnp.int32, tri.shape[1:], 1)
    for parity in range(2):
        tri[parity] = jnp.where(lane - parity * size <= row, 0.0, NEVER)

    copies = []
    for i in range(blocks):
        rows = slice(i * size, (i + 1) * size)
        width = (i // 2 + 1) * 2 * size
        edge = width - 2 * size
        source = pl.ds(pl.multiple_of(order[0, i] * size, size), size)
        query_rows = heads_as_rows(received[source, :])
        scores = lax.dot_general(
            query_rows, kv[0, :width, :], (((1,), (1,)), ((), ())),
            preferred_element_type=jnp.float32,
        ) * SCALE
        tail = scores[:, edge:] + (bias[i:i + 1, edge:width] + tri[i % 2])
        if edge:
            head = scores[:, :edge] + bias[i:i + 1, :edge]
            scores = jnp.concatenate([head, tail], axis=1)
        else:
            scores = tail
        top = jnp.max(scores, axis=1, keepdims=True)
        weights = jnp.exp2(scores - top).astype(jnp.bfloat16)
        sums = jnp.dot(weights, with_ones(kv[1, :width, :]), preferred_element_type=jnp.float32)
        denominator = sums[:, HEAD_WIDTH:]
        result = sums[:, :HEAD_WIDTH] / denominator
        stage[rows, :] = heads_as_columns(result, size).astype(jnp.bfloat16)
        state_o[i * group:(i + 1) * group, :] = result
        state_l[i * group:(i + 1) * group, :] = top + jnp.log2(denominator)
        copy = pltpu.make_async_copy(stage.at[rows], out.at[0, rows], sem.at[i])
        copy.start()
        copies.append(copy)
    for copy in copies:
        copy.wait()


def hop_kernel(
    offset, order, lengths, tiles, received, kv, out_in, state_o_in, state_l_in,
    out, state_o, state_l,
    bias, stage, sem,
):
    place = lax.axis_index("ctx")
    blocks, tokens = bias.shape
    size = tokens // blocks
    group = QUERY_HEADS * size
    reads, first = reach_of(lengths, place, offset, blocks)

    @pl.when(reads > 0)
    def _():
        fill_bias(bias, lengths, tiles, place, offset, blocks, size)

        def over(low):
            def step(i, carry):
                rows = pl.ds(pl.multiple_of(i * size, size), size)
                span = pl.ds(pl.multiple_of(i * group, group), group)
                source = pl.ds(pl.multiple_of(order[0, i] * size, size), size)
                top, sums = attend(
                    heads_as_rows(received[source, :]),
                    kv[0, low:, :],
                    with_ones(kv[1, low:, :]),
                    bias[pl.ds(i, 1), low:],
                )
                before = state_l_in[span, :]
                most = jnp.maximum(before, top)
                old = jnp.exp2(before - most)
                new = jnp.exp2(top - most)
                denominator = old + new * sums[:, HEAD_WIDTH:]
                result = (
                    old * state_o_in[span, :] + new * sums[:, :HEAD_WIDTH]
                ) / denominator
                stage[rows, :] = heads_as_columns(result, size).astype(jnp.bfloat16)
                if offset == 1:
                    state_o[span, :] = result
                    state_l[span, :] = most + jnp.log2(denominator)
                pltpu.make_async_copy(stage.at[rows], out.at[0, rows], sem).start()
                return carry

            lax.fori_loop(0, reads, step, 0)

        part = first // (blocks // 4)
        for n in range(4):
            pl.when(part == n)(functools.partial(over, n * (tokens // 4)))

        def finish(i, carry):
            rows = pl.ds(pl.multiple_of(i * size, size), size)
            pltpu.make_async_copy(stage.at[rows], out.at[0, rows], sem).wait()
            return carry

        lax.fori_loop(0, reads, finish, 0)


def per_device(queries, keys, values, dest_replica, dest_slot, doc_lengths, tile_mask):
    tokens = queries.shape[1]
    width = queries.shape[2]
    blocks = dest_replica.shape[1]
    size = tokens // blocks
    packs = lax.axis_size("dp")
    cap = blocks // packs
    bf16, f32 = jnp.bfloat16, jnp.float32
    rows = tokens * QUERY_HEADS
    params = pltpu.CompilerParams(vmem_limit_bytes=VMEM_LIMIT)

    def cost(flops, moved):
        return pl.CostEstimate(flops=flops, bytes_accessed=moved, transcendentals=0)

    def route(sent):
        return lax.all_to_all(sent, "dp", split_axis=0, concat_axis=0, tiled=True)

    counts = pltpu.SMEM((packs,), jnp.int32)
    kv_send = pl.pallas_call(
        functools.partial(pack_kv_kernel, cap),
        out_shape=jax.ShapeDtypeStruct((packs, 2 * cap * size + SLOT_ROWS, HEAD_WIDTH), bf16),
        in_specs=[SMEM, SMEM, VMEM, VMEM],
        out_specs=VMEM,
        scratch_shapes=[counts, pltpu.SMEM((blocks,), jnp.int32)],
        cost_estimate=cost(0, 4 * tokens * HEAD_WIDTH * 2),
        name="pack_kv",
    )(dest_replica, dest_slot, keys, values)
    kv_recv = route(kv_send)
    q_send = pl.pallas_call(
        functools.partial(pack_q_kernel, cap),
        out_shape=jax.ShapeDtypeStruct((packs, cap * size, width), bf16),
        in_specs=[SMEM, VMEM],
        out_specs=VMEM,
        scratch_shapes=[counts],
        cost_estimate=cost(0, 2 * tokens * width * 2),
        name="pack_q",
    )(dest_replica, queries)
    q_recv = route(q_send).reshape(tokens, width)
    kv, order = pl.pallas_call(
        functools.partial(place_kernel, cap),
        out_shape=(
            jax.ShapeDtypeStruct((2, tokens, HEAD_WIDTH), bf16),
            jax.ShapeDtypeStruct((1, blocks), jnp.int32),
        ),
        in_specs=[VMEM],
        out_specs=(VMEM, SMEM),
        cost_estimate=cost(0, 4 * tokens * HEAD_WIDTH * 2),
        name="place_kv",
    )(kv_recv)

    state_shapes = (
        jax.ShapeDtypeStruct((1, tokens, width), bf16),
        jax.ShapeDtypeStruct((rows, HEAD_WIDTH), f32),
        jax.ShapeDtypeStruct((rows, HEAD_WIDTH), f32),
    )
    bias = pltpu.VMEM((blocks, tokens), f32)
    stage = pltpu.VMEM((tokens, width), bf16)
    dma = pltpu.SemaphoreType.DMA
    state = pl.pallas_call(
        own_kernel,
        out_shape=state_shapes,
        in_specs=[SMEM, SMEM, VMEM, VMEM, VMEM],
        out_specs=(ANY, VMEM, VMEM),
        scratch_shapes=[
            bias, pltpu.VMEM((2, QUERY_HEADS * size, 2 * size), f32), stage, dma((blocks,))
        ],
        compiler_params=params,
        cost_estimate=cost(2 * 2 * rows * tokens * HEAD_WIDTH, 8 * tokens * width),
        name="attend_own",
    )(order, doc_lengths, tile_mask, q_recv, kv)
    for offset in (1, 2):
        kv = shifted(kv, "ctx")
        state = pl.pallas_call(
            functools.partial(hop_kernel, offset),
            out_shape=state_shapes,
            in_specs=[SMEM, SMEM, VMEM, VMEM, VMEM, ANY, VMEM, VMEM],
            out_specs=(ANY, VMEM, VMEM),
            scratch_shapes=[bias, stage, dma],
            input_output_aliases={5: 0, 6: 1, 7: 2},
            compiler_params=params,
            cost_estimate=cost(2 * 2 * rows * tokens * HEAD_WIDTH, 8 * tokens * width),
            name=f"attend_back_{offset}",
        )(order, doc_lengths, tile_mask, q_recv, kv, *state)
    return state[0]


def solution(mesh):
    return jax.shard_map(
        per_device,
        mesh=mesh,
        in_specs=(
            P("dp", "ctx", None),
            P("dp", "ctx", None),
            P("dp", "ctx", None),
            P("dp", "ctx"),
            P("dp", "ctx"),
            P("dp", None),
            P("dp", "ctx", None),
        ),
        out_specs=P("dp", "ctx", None),
        check_vma=False,
    )
```

```python
import functools

import jax
import jax.numpy as jnp
from jax import lax
from jax.experimental import pallas as pl
from jax.experimental.pallas import tpu as pltpu
from jax.sharding import PartitionSpec as P

HEAD_WIDTH = 128
QUERY_HEADS = 4
SCALE = HEAD_WIDTH ** (-0.5) * 1.4426950408889634
NEVER = -1e30
FLOOR = -5e29
SLOT_ROWS = 16
VMEM_LIMIT = 32 * 1024 * 1024
VMEM_SMALL = 8 * 1024 * 1024

ANY = pl.BlockSpec(memory_space=pl.ANY)
SMEM = pl.BlockSpec(memory_space=pltpu.SMEM)
VMEM = pl.BlockSpec(memory_space=pltpu.VMEM)


def shifted(value, axis):
    count = lax.axis_size(axis)
    return lax.ppermute(value, axis, [(source, source + 1) for source in range(count - 1)])


def pack_kv_kernel(cap, targets, slots, keys, values, send, counts, slot_of):
    packs = send.shape[0]
    blocks = targets.shape[1]
    size = keys.shape[1] // blocks
    half = cap * size
    for t in range(packs):
        counts[t] = 0
    for j in range(blocks):
        t = targets[0, j]
        rank = counts[t]
        counts[t] = rank + 1
        slot_of[t * cap + rank] = lax.rem(slots[0, j], blocks)
        rows = slice(j * size, (j + 1) * size)
        to = pl.multiple_of(rank * size, size)
        send[t, pl.ds(to, size), :] = keys[0, rows, :]
        send[t, pl.ds(to + half, size), :] = values[0, rows, :]
    row = lax.broadcasted_iota(jnp.int32, (SLOT_ROWS, HEAD_WIDTH), 0)
    for t in range(packs):
        listed = jnp.zeros(row.shape, jnp.int32)
        for i in range(cap):
            listed = jnp.where(row == i, slot_of[t * cap + i], listed)
        send[t, 2 * half:, :] = listed.astype(jnp.float32).astype(jnp.bfloat16)


def pack_q_kernel(cap, targets, queries, send, counts):
    packs = send.shape[0]
    blocks = targets.shape[1]
    size = queries.shape[1] // blocks
    for t in range(packs):
        counts[t] = 0
    for j in range(blocks):
        t = targets[0, j]
        rank = counts[t]
        counts[t] = rank + 1
        to = pl.multiple_of(rank * size, size)
        send[t, pl.ds(to, size), :] = queries[0, j * size:(j + 1) * size, :]


def place_kernel(cap, received, placed, order):
    packs = received.shape[0]
    size = placed.shape[1] // (packs * cap)
    half = cap * size
    for s in range(packs):
        listed = received[s, 2 * half:, :].astype(jnp.float32).astype(jnp.int32)
        for i in range(cap):
            slot = listed[i, 0]
            order[0, slot] = s * cap + i
            rows = pl.ds(pl.multiple_of(slot * size, size), size)
            placed[0, rows, :] = received[s, i * size:(i + 1) * size, :]
            placed[1, rows, :] = received[s, half + i * size:half + (i + 1) * size, :]


def first_document(lengths, position):
    start, end = jnp.int32(0), jnp.int32(0)
    total = jnp.int32(0)
    for j in range(lengths.shape[1]):
        after = total + lengths[0, j]
        inside = (total <= position) & (position < after)
        start = jnp.where(inside, total, start)
        end = jnp.where(inside, after, end)
        total = after
    return start, end


def reach_of(lengths, place, offset, blocks):
    start, end = first_document(lengths, place * blocks)
    low = (place - offset) * blocks
    rows = jnp.where(start < low + blocks, jnp.minimum(end - place * blocks, blocks), 0)
    return jnp.where(low >= 0, rows, 0), jnp.maximum(start - low, 0)


def fill_bias(bias, lengths, tiles, place, offset, blocks, size):
    tokens = blocks * size
    total_blocks = tiles.shape[2]
    key_block = (place - offset) * blocks + lax.broadcasted_iota(jnp.int32, (1, tokens), 1) // size
    query_block = place * blocks + lax.broadcasted_iota(jnp.int32, (blocks, 1), 0)
    key_doc = jnp.zeros((1, tokens), jnp.int32)
    query_doc = jnp.zeros((blocks, 1), jnp.int32)
    end = jnp.int32(0)
    for j in range(lengths.shape[1]):
        end = end + lengths[0, j]
        key_doc = key_doc + (key_block >= end).astype(jnp.int32)
        query_doc = query_doc + (query_block >= end).astype(jnp.int32)
    spread = lax.broadcasted_iota(jnp.int32, (total_blocks, tokens), 0) == key_block
    listed = jnp.dot(
        tiles[0].astype(jnp.float32).astype(jnp.bfloat16),
        spread.astype(jnp.float32).astype(jnp.bfloat16),
        preferred_element_type=jnp.float32,
    )
    allowed = (query_doc == key_doc) & (key_block <= query_block) & (key_block >= 0)
    allowed = allowed & ((listed > 0.5) | (key_block == query_block))
    bias[...] = jnp.where(allowed, 0.0, NEVER)


def heads_as_rows(block):
    return jnp.concatenate(
        [block[:, h * HEAD_WIDTH:(h + 1) * HEAD_WIDTH] for h in range(QUERY_HEADS)], axis=0
    )


def heads_as_columns(rows, size):
    return jnp.concatenate(
        [rows[h * size:(h + 1) * size] for h in range(QUERY_HEADS)], axis=1
    )


def attend(query_rows, keys, values, bias):
    scores = lax.dot_general(
        query_rows, keys, (((1,), (1,)), ((), ())), preferred_element_type=jnp.float32
    )
    scores = scores * SCALE + bias
    top = jnp.maximum(jnp.max(scores, axis=1, keepdims=True), FLOOR)
    weights = jnp.exp2(scores - top).astype(jnp.bfloat16)
    return top, jnp.dot(weights, values, preferred_element_type=jnp.float32)


def with_ones(values):
    return jnp.concatenate([values, jnp.ones(values.shape, values.dtype)], axis=1)


def own_kernel(
    order, lengths, tiles, received, kv,
    out, state_o, state_l,
    bias, tri, stage, sem,
):
    place = lax.axis_index("ctx")
    blocks, tokens = bias.shape
    size = tokens // blocks
    group = QUERY_HEADS * size
    fill_bias(bias, lengths, tiles, place, 0, blocks, size)
    row = lax.rem(lax.broadcasted_iota(jnp.int32, tri.shape[1:], 0), size)
    lane = lax.broadcasted_iota(jnp.int32, tri.shape[1:], 1)
    for parity in range(2):
        tri[parity] = jnp.where(lane - parity * size <= row, 0.0, NEVER)

    copies = []
    for i in range(blocks):
        rows = slice(i * size, (i + 1) * size)
        width = (i // 2 + 1) * 2 * size
        edge = width - 2 * size
        source = pl.ds(pl.multiple_of(order[0, i] * size, size), size)
        query_rows = heads_as_rows(received[source, :])
        scores = lax.dot_general(
            query_rows, kv[0, :width, :], (((1,), (1,)), ((), ())),
            preferred_element_type=jnp.float32,
        ) * SCALE
        tail = scores[:, edge:] + (bias[i:i + 1, edge:width] + tri[i % 2])
        if edge:
            head = scores[:, :edge] + bias[i:i + 1, :edge]
            scores = jnp.concatenate([head, tail], axis=1)
        else:
            scores = tail
        top = jnp.max(scores, axis=1, keepdims=True)
        weights = jnp.exp2(scores - top).astype(jnp.bfloat16)
        sums = jnp.dot(weights, with_ones(kv[1, :width, :]), preferred_element_type=jnp.float32)
        denominator = sums[:, HEAD_WIDTH:]
        result = sums[:, :HEAD_WIDTH] / denominator
        stage[rows, :] = heads_as_columns(result, size).astype(jnp.bfloat16)
        state_o[i * group:(i + 1) * group, :] = result
        state_l[i * group:(i + 1) * group, :] = top + jnp.log2(denominator)
        copy = pltpu.make_async_copy(stage.at[rows], out.at[0, rows], sem.at[i])
        copy.start()
        copies.append(copy)
    for copy in copies:
        copy.wait()


def hop_kernel(
    offset, order, lengths, tiles, received, kv, out_in, state_o_in, state_l_in,
    out, state_o, state_l,
    bias, stage, sem,
):
    place = lax.axis_index("ctx")
    blocks, tokens = bias.shape
    size = tokens // blocks
    group = QUERY_HEADS * size
    reads, first = reach_of(lengths, place, offset, blocks)

    @pl.when(reads > 0)
    def _():
        fill_bias(bias, lengths, tiles, place, offset, blocks, size)

        def over(low, together):
            def one(i):
                rows = pl.ds(pl.multiple_of(i * size, size), size)
                span = pl.ds(pl.multiple_of(i * group, group), group)
                source = pl.ds(pl.multiple_of(order[0, i] * size, size), size)
                top, sums = attend(
                    heads_as_rows(received[source, :]),
                    kv[0, low:, :],
                    with_ones(kv[1, low:, :]),
                    bias[pl.ds(i, 1), low:],
                )
                before = state_l_in[span, :]
                most = jnp.maximum(before, top)
                old = jnp.exp2(before - most)
                new = jnp.exp2(top - most)
                denominator = old + new * sums[:, HEAD_WIDTH:]
                result = (
                    old * state_o_in[span, :] + new * sums[:, :HEAD_WIDTH]
                ) / denominator
                stage[rows, :] = heads_as_columns(result, size).astype(jnp.bfloat16)
                if offset == 1:
                    state_o[span, :] = result
                    state_l[span, :] = most + jnp.log2(denominator)

            def step(n, carry):
                for u in range(together):
                    one(n * together + u)
                rows = pl.ds(pl.multiple_of(n * together * size, size), together * size)
                pltpu.make_async_copy(stage.at[rows], out.at[0, rows], sem).start()
                return carry

            def finish(n, carry):
                rows = pl.ds(pl.multiple_of(n * together * size, size), together * size)
                pltpu.make_async_copy(stage.at[rows], out.at[0, rows], sem).wait()
                return carry

            steps = pl.cdiv(reads, together)
            lax.fori_loop(0, steps, step, 0)
            lax.fori_loop(0, steps, finish, 0)

        part = first // (blocks // 4)
        for n, together in enumerate((2, 2, 4, 4)):
            pl.when(part == n)(functools.partial(over, n * (tokens // 4), together))


def per_device(queries, keys, values, dest_replica, dest_slot, doc_lengths, tile_mask):
    tokens = queries.shape[1]
    width = queries.shape[2]
    blocks = dest_replica.shape[1]
    size = tokens // blocks
    packs = lax.axis_size("dp")
    cap = blocks // packs
    bf16, f32 = jnp.bfloat16, jnp.float32
    rows = tokens * QUERY_HEADS
    params = pltpu.CompilerParams(vmem_limit_bytes=VMEM_LIMIT)
    small = pltpu.CompilerParams(vmem_limit_bytes=VMEM_SMALL)

    def cost(flops, moved):
        return pl.CostEstimate(flops=flops, bytes_accessed=moved, transcendentals=0)

    def route(sent):
        return lax.all_to_all(sent, "dp", split_axis=0, concat_axis=0, tiled=True)

    counts = pltpu.SMEM((packs,), jnp.int32)
    kv_send = pl.pallas_call(
        functools.partial(pack_kv_kernel, cap),
        out_shape=jax.ShapeDtypeStruct((packs, 2 * cap * size + SLOT_ROWS, HEAD_WIDTH), bf16),
        in_specs=[SMEM, SMEM, VMEM, VMEM],
        out_specs=VMEM,
        scratch_shapes=[counts, pltpu.SMEM((blocks,), jnp.int32)],
        compiler_params=small,
        cost_estimate=cost(0, 4 * tokens * HEAD_WIDTH * 2),
        name="pack_kv",
    )(dest_replica, dest_slot, keys, values)
    kv_recv = route(kv_send)
    q_send = pl.pallas_call(
        functools.partial(pack_q_kernel, cap),
        out_shape=jax.ShapeDtypeStruct((packs, cap * size, width), bf16),
        in_specs=[SMEM, VMEM],
        out_specs=VMEM,
        scratch_shapes=[counts],
        compiler_params=small,
        cost_estimate=cost(0, 2 * tokens * width * 2),
        name="pack_q",
    )(dest_replica, queries)
    kv, order = pl.pallas_call(
        functools.partial(place_kernel, cap),
        out_shape=(
            jax.ShapeDtypeStruct((2, tokens, HEAD_WIDTH), bf16),
            jax.ShapeDtypeStruct((1, blocks), jnp.int32),
        ),
        in_specs=[VMEM],
        out_specs=(VMEM, SMEM),
        compiler_params=small,
        cost_estimate=cost(0, 4 * tokens * HEAD_WIDTH * 2),
        name="place_kv",
    )(kv_recv)

    q_send, kv = lax.optimization_barrier((q_send, kv))
    q_recv = route(q_send).reshape(tokens, width)

    state_shapes = (
        jax.ShapeDtypeStruct((1, tokens, width), bf16),
        jax.ShapeDtypeStruct((rows, HEAD_WIDTH), f32),
        jax.ShapeDtypeStruct((rows, HEAD_WIDTH), f32),
    )
    bias = pltpu.VMEM((blocks, tokens), f32)
    stage = pltpu.VMEM((tokens, width), bf16)
    dma = pltpu.SemaphoreType.DMA
    state = pl.pallas_call(
        own_kernel,
        out_shape=state_shapes,
        in_specs=[SMEM, SMEM, VMEM, VMEM, VMEM],
        out_specs=(ANY, VMEM, VMEM),
        scratch_shapes=[
            bias, pltpu.VMEM((2, QUERY_HEADS * size, 2 * size), f32), stage, dma((blocks,))
        ],
        compiler_params=params,
        cost_estimate=cost(2 * 2 * rows * tokens * HEAD_WIDTH, 8 * tokens * width),
        name="attend_own",
    )(order, doc_lengths, tile_mask, q_recv, kv)
    for offset in (1, 2):
        kv = shifted(kv, "ctx")
        state = pl.pallas_call(
            functools.partial(hop_kernel, offset),
            out_shape=state_shapes,
            in_specs=[SMEM, SMEM, VMEM, VMEM, VMEM, ANY, VMEM, VMEM],
            out_specs=(ANY, VMEM, VMEM),
            scratch_shapes=[bias, stage, dma],
            input_output_aliases={5: 0, 6: 1, 7: 2},
            compiler_params=params,
            cost_estimate=cost(2 * 2 * rows * tokens * HEAD_WIDTH, 8 * tokens * width),
            name=f"attend_back_{offset}",
        )(order, doc_lengths, tile_mask, q_recv, kv, *state)
    return state[0]


def solution(mesh):
    return jax.shard_map(
        per_device,
        mesh=mesh,
        in_specs=(
            P("dp", "ctx", None),
            P("dp", "ctx", None),
            P("dp", "ctx", None),
            P("dp", "ctx"),
            P("dp", "ctx"),
            P("dp", None),
            P("dp", "ctx", None),
        ),
        out_specs=P("dp", "ctx", None),
        check_vma=False,
    )
```

```python
import functools

import jax
import jax.numpy as jnp
from jax import lax
from jax.experimental import pallas as pl
from jax.experimental.pallas import tpu as pltpu
from jax.sharding import PartitionSpec as P

HEAD_WIDTH = 128
QUERY_HEADS = 4
SCALE = HEAD_WIDTH ** (-0.5) * 1.4426950408889634
NEVER = -1e30
FLOOR = -5e29
SLOT_ROWS = 16
VMEM_LIMIT = 32 * 1024 * 1024
VMEM_SMALL = 8 * 1024 * 1024

ANY = pl.BlockSpec(memory_space=pl.ANY)
SMEM = pl.BlockSpec(memory_space=pltpu.SMEM)
VMEM = pl.BlockSpec(memory_space=pltpu.VMEM)


def shifted(value, axis):
    count = lax.axis_size(axis)
    return lax.ppermute(value, axis, [(source, source + 1) for source in range(count - 1)])


def pack_kv_kernel(cap, targets, slots, keys_in, values_in, send_out,
                   keys, values, send, counts, slot_of, sem):
    packs = send.shape[0]
    blocks = targets.shape[1]
    size = keys.shape[1] // blocks
    half = cap * size
    loads = [
        pltpu.make_async_copy(keys_in, keys, sem.at[0]),
        pltpu.make_async_copy(values_in, values, sem.at[1]),
    ]
    for load in loads:
        load.start()
    for t in range(packs):
        counts[t] = 0
    places = []
    for j in range(blocks):
        t = targets[0, j]
        rank = counts[t]
        counts[t] = rank + 1
        slot_of[t * cap + rank] = lax.rem(slots[0, j], blocks)
        places.append((t, pl.multiple_of(rank * size, size)))
    row = lax.broadcasted_iota(jnp.int32, (SLOT_ROWS, HEAD_WIDTH), 0)
    for t in range(packs):
        listed = jnp.zeros(row.shape, jnp.int32)
        for i in range(cap):
            listed = jnp.where(row == i, slot_of[t * cap + i], listed)
        send[t, 2 * half:, :] = listed.astype(jnp.float32).astype(jnp.bfloat16)
    for load, held, shift in zip(loads, (keys, values), (0, half)):
        load.wait()
        for j, (t, to) in enumerate(places):
            send[t, pl.ds(to + shift, size), :] = held[0, j * size:(j + 1) * size, :]
    store = pltpu.make_async_copy(send, send_out, sem.at[2])
    store.start()
    store.wait()


def pack_q_kernel(cap, targets, queries, send, counts):
    packs = send.shape[0]
    blocks = targets.shape[1]
    size = queries.shape[1] // blocks
    for t in range(packs):
        counts[t] = 0
    for j in range(blocks):
        t = targets[0, j]
        rank = counts[t]
        counts[t] = rank + 1
        to = pl.multiple_of(rank * size, size)
        send[t, pl.ds(to, size), :] = queries[0, j * size:(j + 1) * size, :]


def place_kernel(cap, received, placed, order):
    packs = received.shape[0]
    size = placed.shape[1] // (packs * cap)
    half = cap * size
    for s in range(packs):
        listed = received[s, 2 * half:, :].astype(jnp.float32).astype(jnp.int32)
        for i in range(cap):
            slot = listed[i, 0]
            order[0, slot] = s * cap + i
            rows = pl.ds(pl.multiple_of(slot * size, size), size)
            placed[0, rows, :] = received[s, i * size:(i + 1) * size, :]
            placed[1, rows, :] = received[s, half + i * size:half + (i + 1) * size, :]


def first_document(lengths, position):
    start, end = jnp.int32(0), jnp.int32(0)
    total = jnp.int32(0)
    for j in range(lengths.shape[1]):
        after = total + lengths[0, j]
        inside = (total <= position) & (position < after)
        start = jnp.where(inside, total, start)
        end = jnp.where(inside, after, end)
        total = after
    return start, end


def reach_of(lengths, place, offset, blocks):
    start, end = first_document(lengths, place * blocks)
    low = (place - offset) * blocks
    rows = jnp.where(start < low + blocks, jnp.minimum(end - place * blocks, blocks), 0)
    return jnp.where(low >= 0, rows, 0), jnp.maximum(start - low, 0)


def prepare(keys, values, bias, kv, lengths, tiles, place, offset):
    blocks = bias.shape[0]
    tokens = kv.shape[1]
    size = tokens // blocks
    keys[:HEAD_WIDTH, :] = kv[0].T
    block = lax.broadcasted_iota(jnp.int32, (HEAD_WIDTH, tokens), 0)
    of_key = lax.broadcasted_iota(jnp.int32, (HEAD_WIDTH, tokens), 1) // size
    keys[HEAD_WIDTH:, :] = (block == of_key).astype(jnp.float32).astype(jnp.bfloat16)
    values[:, :HEAD_WIDTH] = kv[1]
    values[:, HEAD_WIDTH:] = jnp.ones((tokens, HEAD_WIDTH), jnp.bfloat16)

    low = (place - offset) * blocks
    key_block = low + lax.broadcasted_iota(jnp.int32, (1, HEAD_WIDTH), 1)
    query_block = place * blocks + lax.broadcasted_iota(jnp.int32, (blocks, 1), 0)
    key_doc = jnp.zeros((1, HEAD_WIDTH), jnp.int32)
    query_doc = jnp.zeros((blocks, 1), jnp.int32)
    end = jnp.int32(0)
    for j in range(lengths.shape[1]):
        end = end + lengths[0, j]
        key_doc = key_doc + (key_block >= end).astype(jnp.int32)
        query_doc = query_doc + (query_block >= end).astype(jnp.int32)
    spread = lax.broadcasted_iota(jnp.int32, (tiles.shape[2], HEAD_WIDTH), 0) == key_block
    listed = jnp.dot(
        tiles[0].astype(jnp.float32).astype(jnp.bfloat16),
        spread.astype(jnp.float32).astype(jnp.bfloat16),
        preferred_element_type=jnp.float32,
    )
    allowed = (query_doc == key_doc) & (key_block <= query_block) & (key_block >= 0)
    allowed = allowed & ((listed > 0.5) | (key_block == query_block))
    bias[...] = jnp.where(allowed, 0.0, NEVER)


def query_operand(received, order, bias, first, count, size):
    rows = []
    for u in range(count):
        source = pl.ds(pl.multiple_of(order[0, first + u] * size, size), size)
        barred = jnp.broadcast_to(bias[pl.ds(first + u, 1), :], (QUERY_HEADS * size, HEAD_WIDTH))
        rows.append(jnp.concatenate(
            [heads_as_rows(received[source, :]), barred.astype(jnp.bfloat16)], axis=1
        ))
    return jnp.concatenate(rows, axis=0)


def heads_as_rows(block):
    return jnp.concatenate(
        [block[:, h * HEAD_WIDTH:(h + 1) * HEAD_WIDTH] for h in range(QUERY_HEADS)], axis=0
    )


def heads_as_columns(rows, size):
    return jnp.concatenate(
        [rows[h * size:(h + 1) * size] for h in range(QUERY_HEADS)], axis=1
    )


def own_kernel(
    order, lengths, tiles, received, kv,
    out, state_o, state_l,
    keys, values, bias, stage, sem,
):
    place = lax.axis_index("ctx")
    blocks = bias.shape[0]
    tokens = kv.shape[1]
    size = tokens // blocks
    group = QUERY_HEADS * size
    prepare(keys, values, bias, kv, lengths, tiles, place, 0)
    row = lax.broadcasted_iota(jnp.int32, (2 * group, 2 * size), 0)
    lane = lax.broadcasted_iota(jnp.int32, (2 * group, 2 * size), 1)
    later = lane - (row // group) * size > lax.rem(row, size)

    copies = []
    for i in range(0, blocks, 2):
        rows = slice(i * size, (i + 2) * size)
        span = slice(i * group, (i + 2) * group)
        width = (i + 2) * size
        edge = i * size
        scores = jnp.dot(
            query_operand(received, order, bias, i, 2, size), keys[:, :width],
            preferred_element_type=jnp.float32,
        )
        tail = jnp.where(later, NEVER, scores[:, edge:])
        scores = jnp.concatenate([scores[:, :edge], tail], axis=1) if edge else tail
        top = jnp.max(scores, axis=1, keepdims=True) * SCALE
        weights = jnp.exp2(scores * SCALE - top).astype(jnp.bfloat16)
        sums = jnp.dot(weights, values[:width, :], preferred_element_type=jnp.float32)
        denominator = sums[:, HEAD_WIDTH:]
        result = sums[:, :HEAD_WIDTH] / denominator
        for u in range(2):
            stage[(i + u) * size:(i + u + 1) * size, :] = heads_as_columns(
                result[u * group:(u + 1) * group], size
            ).astype(jnp.bfloat16)
        state_o[span, :] = result
        state_l[span, :] = top + jnp.log2(denominator)
        copy = pltpu.make_async_copy(stage.at[rows], out.at[0, rows], sem.at[i])
        copy.start()
        copies.append(copy)
    for copy in copies:
        copy.wait()


def hop_kernel(
    offset, order, lengths, tiles, received, kv, out_in, state_o_in, state_l_in,
    out, state_o, state_l,
    keys, values, bias, stage, sem,
):
    place = lax.axis_index("ctx")
    blocks = bias.shape[0]
    tokens = kv.shape[1]
    size = tokens // blocks
    group = QUERY_HEADS * size
    reads, first = reach_of(lengths, place, offset, blocks)

    @pl.when(reads > 0)
    def _():
        prepare(keys, values, bias, kv, lengths, tiles, place, offset)

        def over(low, together):
            def step(n, carry):
                i = n * together
                rows = pl.ds(pl.multiple_of(i * size, size), together * size)
                span = pl.ds(pl.multiple_of(i * group, group), together * group)
                scores = jnp.dot(
                    query_operand(received, order, bias, i, together, size), keys[:, low:],
                    preferred_element_type=jnp.float32,
                )
                top = jnp.maximum(jnp.max(scores, axis=1, keepdims=True), FLOOR) * SCALE
                weights = jnp.exp2(scores * SCALE - top).astype(jnp.bfloat16)
                sums = jnp.dot(weights, values[low:, :], preferred_element_type=jnp.float32)
                before = state_l_in[span, :]
                most = jnp.maximum(before, top)
                old = jnp.exp2(before - most)
                new = jnp.exp2(top - most)
                denominator = old + new * sums[:, HEAD_WIDTH:]
                result = (
                    old * state_o_in[span, :] + new * sums[:, :HEAD_WIDTH]
                ) / denominator
                for u in range(together):
                    stage[pl.ds(pl.multiple_of((i + u) * size, size), size), :] = heads_as_columns(
                        result[u * group:(u + 1) * group], size
                    ).astype(jnp.bfloat16)
                if offset == 1:
                    state_o[span, :] = result
                    state_l[span, :] = most + jnp.log2(denominator)
                pltpu.make_async_copy(stage.at[rows], out.at[0, rows], sem).start()
                return carry

            def finish(n, carry):
                rows = pl.ds(pl.multiple_of(n * together * size, size), together * size)
                pltpu.make_async_copy(stage.at[rows], out.at[0, rows], sem).wait()
                return carry

            steps = pl.cdiv(reads, together)
            lax.fori_loop(0, steps, step, 0)
            lax.fori_loop(0, steps, finish, 0)

        part = first // (blocks // 4)
        for n, together in enumerate((2, 2, 4, 4)):
            pl.when(part == n)(functools.partial(over, n * (tokens // 4), together))


def per_device(queries, keys, values, dest_replica, dest_slot, doc_lengths, tile_mask):
    tokens = queries.shape[1]
    width = queries.shape[2]
    blocks = dest_replica.shape[1]
    size = tokens // blocks
    packs = lax.axis_size("dp")
    cap = blocks // packs
    bf16, f32 = jnp.bfloat16, jnp.float32
    rows = tokens * QUERY_HEADS
    params = pltpu.CompilerParams(vmem_limit_bytes=VMEM_LIMIT)
    small = pltpu.CompilerParams(vmem_limit_bytes=VMEM_SMALL)

    def cost(flops, moved):
        return pl.CostEstimate(flops=flops, bytes_accessed=moved, transcendentals=0)

    def route(sent):
        return lax.all_to_all(sent, "dp", split_axis=0, concat_axis=0, tiled=True)

    dma = pltpu.SemaphoreType.DMA
    counts = pltpu.SMEM((packs,), jnp.int32)
    kv_send = pl.pallas_call(
        functools.partial(pack_kv_kernel, cap),
        out_shape=jax.ShapeDtypeStruct((packs, 2 * cap * size + SLOT_ROWS, HEAD_WIDTH), bf16),
        in_specs=[SMEM, SMEM, ANY, ANY],
        out_specs=ANY,
        scratch_shapes=[
            pltpu.VMEM(keys.shape, bf16),
            pltpu.VMEM(values.shape, bf16),
            pltpu.VMEM((packs, 2 * cap * size + SLOT_ROWS, HEAD_WIDTH), bf16),
            counts,
            pltpu.SMEM((blocks,), jnp.int32),
            dma((3,)),
        ],
        cost_estimate=cost(0, 4 * tokens * HEAD_WIDTH * 2),
        name="pack_kv",
    )(dest_replica, dest_slot, keys, values)
    kv_recv = route(kv_send)
    q_send = pl.pallas_call(
        functools.partial(pack_q_kernel, cap),
        out_shape=jax.ShapeDtypeStruct((packs, cap * size, width), bf16),
        in_specs=[SMEM, VMEM],
        out_specs=VMEM,
        scratch_shapes=[counts],
        compiler_params=small,
        cost_estimate=cost(0, 2 * tokens * width * 2),
        name="pack_q",
    )(dest_replica, queries)
    kv, order = pl.pallas_call(
        functools.partial(place_kernel, cap),
        out_shape=(
            jax.ShapeDtypeStruct((2, tokens, HEAD_WIDTH), bf16),
            jax.ShapeDtypeStruct((1, blocks), jnp.int32),
        ),
        in_specs=[VMEM],
        out_specs=(VMEM, SMEM),
        compiler_params=small,
        cost_estimate=cost(0, 4 * tokens * HEAD_WIDTH * 2),
        name="place_kv",
    )(kv_recv)

    q_send, kv = lax.optimization_barrier((q_send, kv))
    q_recv = route(q_send).reshape(tokens, width)

    state_shapes = (
        jax.ShapeDtypeStruct((1, tokens, width), bf16),
        jax.ShapeDtypeStruct((rows, HEAD_WIDTH), f32),
        jax.ShapeDtypeStruct((rows, HEAD_WIDTH), f32),
    )
    operands = [
        pltpu.VMEM((2 * HEAD_WIDTH, tokens), bf16),
        pltpu.VMEM((tokens, 2 * HEAD_WIDTH), bf16),
        pltpu.VMEM((blocks, HEAD_WIDTH), f32),
    ]
    stage = pltpu.VMEM((tokens, width), bf16)
    state = pl.pallas_call(
        own_kernel,
        out_shape=state_shapes,
        in_specs=[SMEM, SMEM, VMEM, VMEM, VMEM],
        out_specs=(ANY, VMEM, VMEM),
        scratch_shapes=operands + [stage, dma((blocks,))],
        compiler_params=params,
        cost_estimate=cost(2 * 2 * rows * tokens * HEAD_WIDTH, 8 * tokens * width),
        name="attend_own",
    )(order, doc_lengths, tile_mask, q_recv, kv)
    later = kv
    for offset in (1, 2):
        kv = shifted(later, "ctx")
        if offset == 1:
            later, *state = lax.optimization_barrier((kv, *state))
        state = pl.pallas_call(
            functools.partial(hop_kernel, offset),
            out_shape=state_shapes,
            in_specs=[SMEM, SMEM, VMEM, VMEM, VMEM, ANY, VMEM, VMEM],
            out_specs=(ANY, VMEM, VMEM),
            scratch_shapes=operands + [stage, dma],
            input_output_aliases={5: 0, 6: 1, 7: 2},
            compiler_params=params,
            cost_estimate=cost(2 * 2 * rows * tokens * HEAD_WIDTH, 8 * tokens * width),
            name=f"attend_back_{offset}",
        )(order, doc_lengths, tile_mask, q_recv, kv, *state)
    return state[0]


def solution(mesh):
    return jax.shard_map(
        per_device,
        mesh=mesh,
        in_specs=(
            P("dp", "ctx", None),
            P("dp", "ctx", None),
            P("dp", "ctx", None),
            P("dp", "ctx"),
            P("dp", "ctx"),
            P("dp", None),
            P("dp", "ctx", None),
        ),
        out_specs=P("dp", "ctx", None),
        check_vma=False,
    )
```

```python
import functools

import jax
import jax.numpy as jnp
from jax import lax
from jax.experimental import pallas as pl
from jax.experimental.pallas import tpu as pltpu
from jax.sharding import PartitionSpec as P

HEAD_WIDTH = 128
QUERY_HEADS = 4
SCALE = HEAD_WIDTH ** (-0.5)
NEVER = -1e30
FLOOR = -5e29
SLOT_ROWS = 16
VMEM_LIMIT = 32 * 1024 * 1024
VMEM_SMALL = 8 * 1024 * 1024

ANY = pl.BlockSpec(memory_space=pl.ANY)
SMEM = pl.BlockSpec(memory_space=pltpu.SMEM)
VMEM = pl.BlockSpec(memory_space=pltpu.VMEM)


def shifted(value, axis):
    count = lax.axis_size(axis)
    return lax.ppermute(value, axis, [(source, source + 1) for source in range(count - 1)])


def pack_kv_kernel(cap, targets, slots, keys_in, values_in, send_out,
                   keys, values, send, counts, slot_of, sem):
    packs = send.shape[0]
    blocks = targets.shape[1]
    size = keys.shape[1] // blocks
    half = cap * size
    loads = [
        pltpu.make_async_copy(keys_in, keys, sem.at[0]),
        pltpu.make_async_copy(values_in, values, sem.at[1]),
    ]
    for load in loads:
        load.start()
    for t in range(packs):
        counts[t] = 0
    places = []
    for j in range(blocks):
        t = targets[0, j]
        rank = counts[t]
        counts[t] = rank + 1
        slot_of[t * cap + rank] = lax.rem(slots[0, j], blocks)
        places.append((t, pl.multiple_of(rank * size, size)))
    row = lax.broadcasted_iota(jnp.int32, (SLOT_ROWS, HEAD_WIDTH), 0)
    for t in range(packs):
        listed = jnp.zeros(row.shape, jnp.int32)
        for i in range(cap):
            listed = jnp.where(row == i, slot_of[t * cap + i], listed)
        send[t, 2 * half:, :] = listed.astype(jnp.float32).astype(jnp.bfloat16)
    for load, held, shift in zip(loads, (keys, values), (0, half)):
        load.wait()
        for j, (t, to) in enumerate(places):
            send[t, pl.ds(to + shift, size), :] = held[0, j * size:(j + 1) * size, :]
    store = pltpu.make_async_copy(send, send_out, sem.at[2])
    store.start()
    store.wait()


def pack_q_kernel(cap, targets, queries, send, counts):
    packs = send.shape[0]
    blocks = targets.shape[1]
    size = queries.shape[1] // blocks
    for t in range(packs):
        counts[t] = 0
    for j in range(blocks):
        t = targets[0, j]
        rank = counts[t]
        counts[t] = rank + 1
        to = pl.multiple_of(rank * size, size)
        send[t, pl.ds(to, size), :] = queries[0, j * size:(j + 1) * size, :]


def place_kernel(cap, received, placed, order):
    packs = received.shape[0]
    size = placed.shape[1] // (packs * cap)
    half = cap * size
    for s in range(packs):
        listed = received[s, 2 * half:, :].astype(jnp.float32).astype(jnp.int32)
        for i in range(cap):
            slot = listed[i, 0]
            order[0, slot] = s * cap + i
            rows = pl.ds(pl.multiple_of(slot * size, size), size)
            placed[0, rows, :] = received[s, i * size:(i + 1) * size, :]
            placed[1, rows, :] = received[s, half + i * size:half + (i + 1) * size, :]


def first_document(lengths, position):
    start, end = jnp.int32(0), jnp.int32(0)
    total = jnp.int32(0)
    for j in range(lengths.shape[1]):
        after = total + lengths[0, j]
        inside = (total <= position) & (position < after)
        start = jnp.where(inside, total, start)
        end = jnp.where(inside, after, end)
        total = after
    return start, end


def reach_of(lengths, place, offset, blocks):
    start, end = first_document(lengths, place * blocks)
    low = (place - offset) * blocks
    rows = jnp.where(start < low + blocks, jnp.minimum(end - place * blocks, blocks), 0)
    return jnp.where(low >= 0, rows, 0), jnp.maximum(start - low, 0)


def prepare(keys, values, bias, kv, lengths, tiles, place, offset):
    blocks = bias.shape[0]
    tokens = kv.shape[1]
    size = tokens // blocks
    block = lax.broadcasted_iota(jnp.int32, (tokens, HEAD_WIDTH), 1)
    of_key = lax.broadcasted_iota(jnp.int32, (tokens, HEAD_WIDTH), 0) // size
    keys[:, :HEAD_WIDTH] = kv[0]
    keys[:, HEAD_WIDTH:] = (block == of_key).astype(jnp.float32).astype(jnp.bfloat16)
    values[:, :HEAD_WIDTH] = kv[1]
    values[:, HEAD_WIDTH:] = jnp.ones((tokens, HEAD_WIDTH), jnp.bfloat16)

    low = (place - offset) * blocks
    key_block = low + lax.broadcasted_iota(jnp.int32, (1, HEAD_WIDTH), 1)
    query_block = place * blocks + lax.broadcasted_iota(jnp.int32, (blocks, 1), 0)
    key_doc = jnp.zeros((1, HEAD_WIDTH), jnp.int32)
    query_doc = jnp.zeros((blocks, 1), jnp.int32)
    end = jnp.int32(0)
    for j in range(lengths.shape[1]):
        end = end + lengths[0, j]
        key_doc = key_doc + (key_block >= end).astype(jnp.int32)
        query_doc = query_doc + (query_block >= end).astype(jnp.int32)
    spread = lax.broadcasted_iota(jnp.int32, (tiles.shape[2], HEAD_WIDTH), 0) == key_block
    listed = jnp.dot(
        tiles[0].astype(jnp.float32).astype(jnp.bfloat16),
        spread.astype(jnp.float32).astype(jnp.bfloat16),
        preferred_element_type=jnp.float32,
    )
    allowed = (query_doc == key_doc) & (key_block <= query_block) & (key_block >= 0)
    allowed = allowed & ((listed > 0.5) | (key_block == query_block))
    bias[...] = jnp.where(allowed, 0.0, NEVER)


def score(received, order, bias, i, keys, size):
    source = pl.ds(pl.multiple_of(order[0, i] * size, size), size)
    barred = jnp.broadcast_to(bias[pl.ds(i, 1), :], (QUERY_HEADS * size, HEAD_WIDTH))
    rows = jnp.concatenate(
        [heads_as_rows(received[source, :]), barred.astype(jnp.bfloat16)], axis=1
    )
    return lax.dot_general(
        rows, keys, (((1,), (1,)), ((), ())), preferred_element_type=jnp.float32
    )


def heads_as_rows(block):
    return jnp.concatenate(
        [block[:, h * HEAD_WIDTH:(h + 1) * HEAD_WIDTH] for h in range(QUERY_HEADS)], axis=0
    )


def heads_as_columns(rows, size):
    return jnp.concatenate(
        [rows[h * size:(h + 1) * size] for h in range(QUERY_HEADS)], axis=1
    )


def own_kernel(
    order, lengths, tiles, received, kv,
    out, state_o, state_l,
    keys, values, bias, stage, sem,
):
    place = lax.axis_index("ctx")
    blocks = bias.shape[0]
    tokens = kv.shape[1]
    size = tokens // blocks
    group = QUERY_HEADS * size
    prepare(keys, values, bias, kv, lengths, tiles, place, 0)
    row = lax.rem(lax.broadcasted_iota(jnp.int32, (group, 2 * size), 0), size)
    lane = lax.broadcasted_iota(jnp.int32, (group, 2 * size), 1)

    def start(i):
        return score(received, order, bias, i, keys[:(i // 2 + 1) * 2 * size, :], size)

    copies = []
    scores = start(0)
    for i in range(blocks):
        ahead = start(i + 1) if i + 1 < blocks else None
        rows = slice(i * size, (i + 1) * size)
        span = slice(i * group, (i + 1) * group)
        width = scores.shape[1]
        edge = width - 2 * size
        tail = jnp.where(lane - (i % 2) * size > row, NEVER, scores[:, edge:])
        scores = jnp.concatenate([scores[:, :edge], tail], axis=1) if edge else tail
        top = jnp.max(scores, axis=1, keepdims=True) * SCALE
        weights = jnp.exp(scores * SCALE - top).astype(jnp.bfloat16)
        sums = jnp.dot(weights, values[:width, :], preferred_element_type=jnp.float32)
        denominator = sums[:, HEAD_WIDTH:]
        result = sums[:, :HEAD_WIDTH] / denominator
        stage[rows, :] = heads_as_columns(result, size).astype(jnp.bfloat16)
        state_o[span, :] = result
        state_l[span, :] = top + jnp.log(denominator)
        copy = pltpu.make_async_copy(stage.at[rows], out.at[0, rows], sem.at[i])
        copy.start()
        copies.append(copy)
        scores = ahead
    for copy in copies:
        copy.wait()


def hop_kernel(
    offset, order, lengths, tiles, received, kv, out_in, state_o_in, state_l_in,
    out, state_o, state_l,
    keys, values, bias, stage, sem,
):
    place = lax.axis_index("ctx")
    blocks = bias.shape[0]
    tokens = kv.shape[1]
    size = tokens // blocks
    group = QUERY_HEADS * size
    reads, first = reach_of(lengths, place, offset, blocks)

    @pl.when(reads > 0)
    def _():
        prepare(keys, values, bias, kv, lengths, tiles, place, offset)

        def over(low, together):
            def start(i):
                return score(received, order, bias, i, keys[low:, :], size)

            def end(i, scores):
                span = pl.ds(pl.multiple_of(i * group, group), group)
                top = jnp.maximum(jnp.max(scores, axis=1, keepdims=True), FLOOR) * SCALE
                weights = jnp.exp(scores * SCALE - top).astype(jnp.bfloat16)
                sums = jnp.dot(weights, values[low:, :], preferred_element_type=jnp.float32)
                before = state_l_in[span, :]
                most = jnp.maximum(before, top)
                old = jnp.exp(before - most)
                new = jnp.exp(top - most)
                denominator = old + new * sums[:, HEAD_WIDTH:]
                result = (
                    old * state_o_in[span, :] + new * sums[:, :HEAD_WIDTH]
                ) / denominator
                rows = pl.ds(pl.multiple_of(i * size, size), size)
                stage[rows, :] = heads_as_columns(result, size).astype(jnp.bfloat16)
                if offset == 1:
                    state_o[span, :] = result
                    state_l[span, :] = most + jnp.log(denominator)

            def step(n, carry):
                i = n * together
                scores = start(i)
                for u in range(together):
                    ahead = start(i + u + 1) if u + 1 < together else None
                    end(i + u, scores)
                    scores = ahead
                rows = pl.ds(pl.multiple_of(i * size, size), together * size)
                pltpu.make_async_copy(stage.at[rows], out.at[0, rows], sem).start()
                return carry

            def finish(n, carry):
                rows = pl.ds(pl.multiple_of(n * together * size, size), together * size)
                pltpu.make_async_copy(stage.at[rows], out.at[0, rows], sem).wait()
                return carry

            steps = pl.cdiv(reads, together)
            lax.fori_loop(0, steps, step, 0)
            lax.fori_loop(0, steps, finish, 0)

        part = first // (blocks // 4)
        for n, together in enumerate((4, 4, 4, 4)):
            pl.when(part == n)(functools.partial(over, n * (tokens // 4), together))


def per_device(queries, keys, values, dest_replica, dest_slot, doc_lengths, tile_mask):
    tokens = queries.shape[1]
    width = queries.shape[2]
    blocks = dest_replica.shape[1]
    size = tokens // blocks
    packs = lax.axis_size("dp")
    cap = blocks // packs
    bf16, f32 = jnp.bfloat16, jnp.float32
    rows = tokens * QUERY_HEADS
    params = pltpu.CompilerParams(vmem_limit_bytes=VMEM_LIMIT)
    small = pltpu.CompilerParams(vmem_limit_bytes=VMEM_SMALL)

    def cost(flops, moved):
        return pl.CostEstimate(flops=flops, bytes_accessed=moved, transcendentals=0)

    def route(sent):
        return lax.all_to_all(sent, "dp", split_axis=0, concat_axis=0, tiled=True)

    dma = pltpu.SemaphoreType.DMA
    counts = pltpu.SMEM((packs,), jnp.int32)
    kv_send = pl.pallas_call(
        functools.partial(pack_kv_kernel, cap),
        out_shape=jax.ShapeDtypeStruct((packs, 2 * cap * size + SLOT_ROWS, HEAD_WIDTH), bf16),
        in_specs=[SMEM, SMEM, ANY, ANY],
        out_specs=ANY,
        scratch_shapes=[
            pltpu.VMEM(keys.shape, bf16),
            pltpu.VMEM(values.shape, bf16),
            pltpu.VMEM((packs, 2 * cap * size + SLOT_ROWS, HEAD_WIDTH), bf16),
            counts,
            pltpu.SMEM((blocks,), jnp.int32),
            dma((3,)),
        ],
        cost_estimate=cost(0, 4 * tokens * HEAD_WIDTH * 2),
        name="pack_kv",
    )(dest_replica, dest_slot, keys, values)
    kv_recv = route(kv_send)
    q_send = pl.pallas_call(
        functools.partial(pack_q_kernel, cap),
        out_shape=jax.ShapeDtypeStruct((packs, cap * size, width), bf16),
        in_specs=[SMEM, VMEM],
        out_specs=VMEM,
        scratch_shapes=[counts],
        compiler_params=small,
        cost_estimate=cost(0, 2 * tokens * width * 2),
        name="pack_q",
    )(dest_replica, queries)
    kv, order = pl.pallas_call(
        functools.partial(place_kernel, cap),
        out_shape=(
            jax.ShapeDtypeStruct((2, tokens, HEAD_WIDTH), bf16),
            jax.ShapeDtypeStruct((1, blocks), jnp.int32),
        ),
        in_specs=[VMEM],
        out_specs=(VMEM, SMEM),
        compiler_params=small,
        cost_estimate=cost(0, 4 * tokens * HEAD_WIDTH * 2),
        name="place_kv",
    )(kv_recv)

    q_send, kv = lax.optimization_barrier((q_send, kv))
    q_recv = route(q_send).reshape(tokens, width)

    state_shapes = (
        jax.ShapeDtypeStruct((1, tokens, width), bf16),
        jax.ShapeDtypeStruct((rows, HEAD_WIDTH), f32),
        jax.ShapeDtypeStruct((rows, HEAD_WIDTH), f32),
    )
    operands = [
        pltpu.VMEM((tokens, 2 * HEAD_WIDTH), bf16),
        pltpu.VMEM((tokens, 2 * HEAD_WIDTH), bf16),
        pltpu.VMEM((blocks, HEAD_WIDTH), f32),
    ]
    stage = pltpu.VMEM((tokens, width), bf16)
    state = pl.pallas_call(
        own_kernel,
        out_shape=state_shapes,
        in_specs=[SMEM, SMEM, VMEM, VMEM, VMEM],
        out_specs=(ANY, VMEM, VMEM),
        scratch_shapes=operands + [stage, dma((blocks,))],
        compiler_params=params,
        cost_estimate=cost(2 * 2 * rows * tokens * HEAD_WIDTH, 8 * tokens * width),
        name="attend_own",
    )(order, doc_lengths, tile_mask, q_recv, kv)
    later = kv
    for offset in (1, 2):
        kv = shifted(later, "ctx")
        if offset == 1:
            later, *state = lax.optimization_barrier((kv, *state))
        state = pl.pallas_call(
            functools.partial(hop_kernel, offset),
            out_shape=state_shapes,
            in_specs=[SMEM, SMEM, VMEM, VMEM, VMEM, ANY, VMEM, VMEM],
            out_specs=(ANY, VMEM, VMEM),
            scratch_shapes=operands + [stage, dma],
            input_output_aliases={5: 0, 6: 1, 7: 2},
            compiler_params=params,
            cost_estimate=cost(2 * 2 * rows * tokens * HEAD_WIDTH, 8 * tokens * width),
            name=f"attend_back_{offset}",
        )(order, doc_lengths, tile_mask, q_recv, kv, *state)
    return state[0]


def solution(mesh):
    return jax.shard_map(
        per_device,
        mesh=mesh,
        in_specs=(
            P("dp", "ctx", None),
            P("dp", "ctx", None),
            P("dp", "ctx", None),
            P("dp", "ctx"),
            P("dp", "ctx"),
            P("dp", None),
            P("dp", "ctx", None),
        ),
        out_specs=P("dp", "ctx", None),
        check_vma=False,
    )
```

```python
import functools

import jax
import jax.numpy as jnp
from jax import lax
from jax.experimental import pallas as pl
from jax.experimental.pallas import tpu as pltpu
from jax.sharding import PartitionSpec as P

HEAD_WIDTH = 128
QUERY_HEADS = 4
SCALE = HEAD_WIDTH ** (-0.5) * 1.4426950408889634
NEVER = -1e30
FLOOR = -5e29
SLOT_ROWS = 16
REACH = 2
VMEM_LIMIT = 32 * 1024 * 1024
VMEM_SMALL = 8 * 1024 * 1024

ANY = pl.BlockSpec(memory_space=pl.ANY)
SMEM = pl.BlockSpec(memory_space=pltpu.SMEM)
VMEM = pl.BlockSpec(memory_space=pltpu.VMEM)


def shifted(value, axis):
    count = lax.axis_size(axis)
    return lax.ppermute(value, axis, [(source, source + 1) for source in range(count - 1)])


def pack_kv_kernel(cap, targets, slots, keys, values, send, counts, slot_of):
    packs = send.shape[0]
    blocks = targets.shape[1]
    size = keys.shape[1] // blocks
    half = cap * size
    for t in range(packs):
        counts[t] = 0
    for j in range(blocks):
        t = targets[0, j]
        rank = counts[t]
        counts[t] = rank + 1
        slot_of[t * cap + rank] = lax.rem(slots[0, j], blocks)
        rows = slice(j * size, (j + 1) * size)
        to = pl.multiple_of(rank * size, size)
        send[t, pl.ds(to, size), :] = keys[0, rows, :]
        send[t, pl.ds(to + half, size), :] = values[0, rows, :]
    row = lax.broadcasted_iota(jnp.int32, (SLOT_ROWS, HEAD_WIDTH), 0)
    for t in range(packs):
        listed = jnp.zeros(row.shape, jnp.int32)
        for i in range(cap):
            listed = jnp.where(row == i, slot_of[t * cap + i], listed)
        send[t, 2 * half:, :] = listed.astype(jnp.float32).astype(jnp.bfloat16)


def pack_q_kernel(cap, targets, lengths, tiles, queries, send, bias, block_of, counts):
    packs = send.shape[0]
    blocks = targets.shape[1]
    tokens = queries.shape[1]
    size = tokens // blocks
    place = lax.axis_index("ctx")
    for t in range(packs):
        counts[t] = 0
    for j in range(blocks):
        t = targets[0, j]
        rank = counts[t]
        counts[t] = rank + 1
        to = pl.multiple_of(rank * size, size)
        send[t, pl.ds(to, size), :] = queries[0, j * size:(j + 1) * size, :]

    block = lax.broadcasted_iota(jnp.int32, (tokens, HEAD_WIDTH), 1)
    of_key = lax.broadcasted_iota(jnp.int32, (tokens, HEAD_WIDTH), 0) // size
    block_of[...] = (block == of_key).astype(jnp.float32).astype(jnp.bfloat16)
    query_block = place * blocks + lax.broadcasted_iota(jnp.int32, (blocks, 1), 0)
    listed_tiles = tiles[0].astype(jnp.float32).astype(jnp.bfloat16)
    for offset in range(bias.shape[0]):
        low = (place - offset) * blocks
        key_block = low + lax.broadcasted_iota(jnp.int32, (1, HEAD_WIDTH), 1)
        key_doc = jnp.zeros((1, HEAD_WIDTH), jnp.int32)
        query_doc = jnp.zeros((blocks, 1), jnp.int32)
        end = jnp.int32(0)
        for j in range(lengths.shape[1]):
            end = end + lengths[0, j]
            key_doc = key_doc + (key_block >= end).astype(jnp.int32)
            query_doc = query_doc + (query_block >= end).astype(jnp.int32)
        spread = lax.broadcasted_iota(jnp.int32, (tiles.shape[2], HEAD_WIDTH), 0) == key_block
        listed = jnp.dot(
            listed_tiles, spread.astype(jnp.float32).astype(jnp.bfloat16),
            preferred_element_type=jnp.float32,
        )
        allowed = (query_doc == key_doc) & (key_block <= query_block) & (key_block >= 0)
        allowed = allowed & ((listed > 0.5) | (key_block == query_block))
        bias[offset] = jnp.where(allowed, 0.0, NEVER)


def place_kernel(cap, received, keys, values, order):
    packs = received.shape[0]
    size = keys.shape[0] // (packs * cap)
    half = cap * size
    for s in range(packs):
        listed = received[s, 2 * half:, :].astype(jnp.float32).astype(jnp.int32)
        for i in range(cap):
            slot = listed[i, 0]
            order[0, slot] = s * cap + i
            rows = pl.ds(pl.multiple_of(slot * size, size), size)
            keys[rows, :] = received[s, i * size:(i + 1) * size, :]
            values[rows, :] = received[s, half + i * size:half + (i + 1) * size, :]


def first_document(lengths, position):
    start, end = jnp.int32(0), jnp.int32(0)
    total = jnp.int32(0)
    for j in range(lengths.shape[1]):
        after = total + lengths[0, j]
        inside = (total <= position) & (position < after)
        start = jnp.where(inside, total, start)
        end = jnp.where(inside, after, end)
        total = after
    return start, end


def reach_of(lengths, place, offset, blocks):
    start, end = first_document(lengths, place * blocks)
    low = (place - offset) * blocks
    rows = jnp.where(start < low + blocks, jnp.minimum(end - place * blocks, blocks), 0)
    return jnp.where(low >= 0, rows, 0), jnp.maximum(start - low, 0)


def beside_ones(values):
    return jnp.concatenate([values, jnp.ones(values.shape, values.dtype)], axis=1)


def score(received, order, bias, i, keys, block_of, size):
    source = pl.ds(pl.multiple_of(order[0, i] * size, size), size)
    barred = jnp.broadcast_to(bias[pl.ds(i, 1), :], (QUERY_HEADS * size, HEAD_WIDTH))
    rows = jnp.concatenate(
        [heads_as_rows(received[source, :]), barred.astype(jnp.bfloat16)], axis=1
    )
    return lax.dot_general(
        rows, jnp.concatenate([keys, block_of], axis=1), (((1,), (1,)), ((), ())), preferred_element_type=jnp.float32
    )


def heads_as_rows(block):
    return jnp.concatenate(
        [block[:, h * HEAD_WIDTH:(h + 1) * HEAD_WIDTH] for h in range(QUERY_HEADS)], axis=0
    )


def heads_as_columns(rows, size):
    return jnp.concatenate(
        [rows[h * size:(h + 1) * size] for h in range(QUERY_HEADS)], axis=1
    )


def own_kernel(first, last, order, bias_in, block_of, received, keys, values, *refs):
    out, state_o, state_l, stage, sem = refs[-5:]
    bias = bias_in.at[0]
    blocks = bias.shape[0]
    tokens = keys.shape[0]
    size = tokens // blocks
    group = QUERY_HEADS * size
    row = lax.rem(lax.broadcasted_iota(jnp.int32, (group, 2 * size), 0), size)
    lane = lax.broadcasted_iota(jnp.int32, (group, 2 * size), 1)

    def start(i):
        width = (i // 2 + 1) * 2 * size
        return score(received, order, bias, i, keys[:width, :], block_of[:width, :], size)

    copies = []
    scores = start(first)
    for i in range(first, last):
        ahead = start(i + 1) if i + 1 < last else None
        rows = slice(i * size, (i + 1) * size)
        span = slice(i * group, (i + 1) * group)
        width = scores.shape[1]
        edge = width - 2 * size
        tail = jnp.where(lane - (i % 2) * size > row, NEVER, scores[:, edge:])
        scores = jnp.concatenate([scores[:, :edge], tail], axis=1) if edge else tail
        top = jnp.max(scores, axis=1, keepdims=True) * SCALE
        weights = jnp.exp2(scores * SCALE - top).astype(jnp.bfloat16)
        sums = jnp.dot(weights, beside_ones(values[:width, :]), preferred_element_type=jnp.float32)
        denominator = sums[:, HEAD_WIDTH:]
        result = sums[:, :HEAD_WIDTH] / denominator
        stage[rows, :] = heads_as_columns(result, size).astype(jnp.bfloat16)
        state_o[span, :] = result
        state_l[span, :] = top + jnp.log2(denominator)
        copy = pltpu.make_async_copy(stage.at[rows], out.at[0, rows], sem.at[i])
        copy.start()
        copies.append(copy)
        scores = ahead
    for copy in copies:
        copy.wait()


def hop_kernel(
    offset, order, lengths, bias_in, block_of, received, keys, values,
    out_in, state_o_in, state_l_in,
    out, state_o, state_l,
    stage, sem,
):
    place = lax.axis_index("ctx")
    bias = bias_in.at[offset]
    blocks = bias.shape[0]
    tokens = keys.shape[0]
    size = tokens // blocks
    group = QUERY_HEADS * size
    reads, first = reach_of(lengths, place, offset, blocks)

    @pl.when(reads > 0)
    def _():
        def over(low, together):
            def start(i):
                return score(received, order, bias, i, keys[low:, :], block_of[low:, :], size)

            def end(i, scores):
                span = pl.ds(pl.multiple_of(i * group, group), group)
                top = jnp.maximum(jnp.max(scores, axis=1, keepdims=True), FLOOR) * SCALE
                weights = jnp.exp2(scores * SCALE - top).astype(jnp.bfloat16)
                sums = jnp.dot(weights, beside_ones(values[low:, :]), preferred_element_type=jnp.float32)
                before = state_l_in[span, :]
                most = jnp.maximum(before, top)
                old = jnp.exp2(before - most)
                new = jnp.exp2(top - most)
                denominator = old + new * sums[:, HEAD_WIDTH:]
                result = (
                    old * state_o_in[span, :] + new * sums[:, :HEAD_WIDTH]
                ) / denominator
                rows = pl.ds(pl.multiple_of(i * size, size), size)
                stage[rows, :] = heads_as_columns(result, size).astype(jnp.bfloat16)
                if offset == 1:
                    state_o[span, :] = result
                    state_l[span, :] = most + jnp.log2(denominator)

            def step(n, carry):
                i = n * together
                scores = start(i)
                for u in range(together):
                    ahead = start(i + u + 1) if u + 1 < together else None
                    end(i + u, scores)
                    scores = ahead
                rows = pl.ds(pl.multiple_of(i * size, size), together * size)
                pltpu.make_async_copy(stage.at[rows], out.at[0, rows], sem).start()
                return carry

            def finish(n, carry):
                rows = pl.ds(pl.multiple_of(n * together * size, size), together * size)
                pltpu.make_async_copy(stage.at[rows], out.at[0, rows], sem).wait()
                return carry

            steps = pl.cdiv(reads, together)
            lax.fori_loop(0, steps, step, 0)
            lax.fori_loop(0, steps, finish, 0)

        part = first // (blocks // 4)
        for n in range(4):
            pl.when(part == n)(functools.partial(over, n * (tokens // 4), 4))


def per_device(queries, keys, values, dest_replica, dest_slot, doc_lengths, tile_mask):
    tokens = queries.shape[1]
    width = queries.shape[2]
    blocks = dest_replica.shape[1]
    size = tokens // blocks
    packs = lax.axis_size("dp")
    cap = blocks // packs
    bf16, f32 = jnp.bfloat16, jnp.float32
    rows = tokens * QUERY_HEADS
    params = pltpu.CompilerParams(vmem_limit_bytes=VMEM_LIMIT)
    small = pltpu.CompilerParams(vmem_limit_bytes=VMEM_SMALL)

    def cost(flops, moved):
        return pl.CostEstimate(flops=flops, bytes_accessed=moved, transcendentals=0)

    def route(sent):
        return lax.all_to_all(sent, "dp", split_axis=0, concat_axis=0, tiled=True)

    dma = pltpu.SemaphoreType.DMA
    counts = pltpu.SMEM((packs,), jnp.int32)
    kv_send = pl.pallas_call(
        functools.partial(pack_kv_kernel, cap),
        out_shape=jax.ShapeDtypeStruct((packs, 2 * cap * size + SLOT_ROWS, HEAD_WIDTH), bf16),
        in_specs=[SMEM, SMEM, VMEM, VMEM],
        out_specs=VMEM,
        scratch_shapes=[counts, pltpu.SMEM((blocks,), jnp.int32)],
        cost_estimate=cost(0, 4 * tokens * HEAD_WIDTH * 2),
        name="pack_kv",
    )(dest_replica, dest_slot, keys, values)
    kv_recv = route(kv_send)
    q_send, bias, block_of = pl.pallas_call(
        functools.partial(pack_q_kernel, cap),
        out_shape=(
            jax.ShapeDtypeStruct((packs, cap * size, width), bf16),
            jax.ShapeDtypeStruct((REACH + 1, blocks, HEAD_WIDTH), f32),
            jax.ShapeDtypeStruct((tokens, HEAD_WIDTH), bf16),
        ),
        in_specs=[SMEM, SMEM, VMEM, VMEM],
        out_specs=(VMEM, VMEM, VMEM),
        scratch_shapes=[counts],
        compiler_params=small,
        cost_estimate=cost(0, 2 * tokens * width * 2),
        name="pack_q",
    )(dest_replica, doc_lengths, tile_mask, queries)
    q_recv = route(q_send).reshape(tokens, width)
    moving_k, moving_v, order = pl.pallas_call(
        functools.partial(place_kernel, cap),
        out_shape=(
            jax.ShapeDtypeStruct((tokens, HEAD_WIDTH), bf16),
            jax.ShapeDtypeStruct((tokens, HEAD_WIDTH), bf16),
            jax.ShapeDtypeStruct((1, blocks), jnp.int32),
        ),
        in_specs=[VMEM],
        out_specs=(VMEM, VMEM, SMEM),
        compiler_params=small,
        cost_estimate=cost(0, 4 * tokens * HEAD_WIDTH * 2),
        name="place_kv",
    )(kv_recv)

    state_shapes = (
        jax.ShapeDtypeStruct((1, tokens, width), bf16),
        jax.ShapeDtypeStruct((rows, HEAD_WIDTH), f32),
        jax.ShapeDtypeStruct((rows, HEAD_WIDTH), f32),
    )
    stage = pltpu.VMEM((tokens, width), bf16)

    def attend_own(first, last, *state):
        return pl.pallas_call(
            functools.partial(own_kernel, first, last),
            out_shape=state_shapes,
            in_specs=[SMEM] + [VMEM] * 5 + [ANY, VMEM, VMEM][:len(state)],
            out_specs=(ANY, VMEM, VMEM),
            scratch_shapes=[stage, dma((blocks,))],
            input_output_aliases={6 + n: n for n in range(len(state))},
            compiler_params=params,
            cost_estimate=cost(2 * rows * tokens * HEAD_WIDTH, 8 * tokens * width),
            name=f"attend_own_{first}",
        )(order, bias, block_of, q_recv, moving_k, moving_v, *state)

    def attend_back(offset, keys, values, *state):
        return pl.pallas_call(
            functools.partial(hop_kernel, offset),
            out_shape=state_shapes,
            in_specs=[SMEM, SMEM] + [VMEM] * 5 + [ANY, VMEM, VMEM],
            out_specs=(ANY, VMEM, VMEM),
            scratch_shapes=[stage, dma],
            input_output_aliases={7: 0, 8: 1, 9: 2},
            compiler_params=params,
            cost_estimate=cost(2 * 2 * rows * tokens * HEAD_WIDTH, 8 * tokens * width),
            name=f"attend_back_{offset}",
        )(order, doc_lengths, bias, block_of, q_recv, keys, values, *state)

    middle = blocks * 5 // 16 * 2
    back_k = shifted(moving_k, "ctx")
    back_v = shifted(moving_v, "ctx")
    state = attend_own(0, middle)
    far_v, *state = lax.optimization_barrier((back_v, *state))
    far_k = shifted(back_k, "ctx")
    far_v = shifted(far_v, "ctx")
    state = attend_own(middle, blocks, *state)
    state = attend_back(1, back_k, back_v, *state)
    state = attend_back(2, far_k, far_v, *state)
    return state[0]


def solution(mesh):
    return jax.shard_map(
        per_device,
        mesh=mesh,
        in_specs=(
            P("dp", "ctx", None),
            P("dp", "ctx", None),
            P("dp", "ctx", None),
            P("dp", "ctx"),
            P("dp", "ctx"),
            P("dp", None),
            P("dp", "ctx", None),
        ),
        out_specs=P("dp", "ctx", None),
        check_vma=False,
    )
```

```python
import functools

import jax
import jax.numpy as jnp
from jax import lax
from jax.experimental import pallas as pl
from jax.experimental.pallas import tpu as pltpu
from jax.sharding import PartitionSpec as P

HEAD_WIDTH = 128
QUERY_HEADS = 4
SCALE = HEAD_WIDTH ** (-0.5) * 1.4426950408889634
NEVER = -1e30
MOST = 1e30
CHUNK = 256
SLOT_ROWS = 16
REACH = 2
VMEM_LIMIT = 32 * 1024 * 1024
VMEM_SMALL = 8 * 1024 * 1024

ANY = pl.BlockSpec(memory_space=pl.ANY)
SMEM = pl.BlockSpec(memory_space=pltpu.SMEM)
VMEM = pl.BlockSpec(memory_space=pltpu.VMEM)


def shifted(value, axis):
    count = lax.axis_size(axis)
    return lax.ppermute(value, axis, [(source, source + 1) for source in range(count - 1)])


def pack_kv_kernel(cap, targets, slots, keys, values, send, counts, slot_of):
    packs = send.shape[0]
    blocks = targets.shape[1]
    size = keys.shape[1] // blocks
    half = cap * size
    for t in range(packs):
        counts[t] = 0
    for j in range(blocks):
        t = targets[0, j]
        rank = counts[t]
        counts[t] = rank + 1
        slot_of[t * cap + rank] = lax.rem(slots[0, j], blocks)
        rows = slice(j * size, (j + 1) * size)
        to = pl.multiple_of(rank * size, size)
        send[t, pl.ds(to, size), :] = keys[0, rows, :]
        send[t, pl.ds(to + half, size), :] = values[0, rows, :]
    row = lax.broadcasted_iota(jnp.int32, (SLOT_ROWS, HEAD_WIDTH), 0)
    for t in range(packs):
        listed = jnp.zeros(row.shape, jnp.int32)
        for i in range(cap):
            listed = jnp.where(row == i, slot_of[t * cap + i], listed)
        send[t, 2 * half:, :] = listed.astype(jnp.float32).astype(jnp.bfloat16)


def pack_q_kernel(cap, targets, lengths, tiles, queries, send, bias, block_of, counts):
    packs = send.shape[0]
    blocks = targets.shape[1]
    tokens = queries.shape[1]
    size = tokens // blocks
    place = lax.axis_index("ctx")
    for t in range(packs):
        counts[t] = 0
    for j in range(blocks):
        t = targets[0, j]
        rank = counts[t]
        counts[t] = rank + 1
        to = pl.multiple_of(rank * size, size)
        send[t, pl.ds(to, size), :] = queries[0, j * size:(j + 1) * size, :]

    block = lax.broadcasted_iota(jnp.int32, (tokens, HEAD_WIDTH), 1)
    of_key = lax.broadcasted_iota(jnp.int32, (tokens, HEAD_WIDTH), 0) // size
    block_of[...] = (block == of_key).astype(jnp.float32).astype(jnp.bfloat16)
    query_block = place * blocks + lax.broadcasted_iota(jnp.int32, (blocks, 1), 0)
    listed_tiles = tiles[0].astype(jnp.float32).astype(jnp.bfloat16)
    for offset in range(bias.shape[0]):
        low = (place - offset) * blocks
        key_block = low + lax.broadcasted_iota(jnp.int32, (1, HEAD_WIDTH), 1)
        key_doc = jnp.zeros((1, HEAD_WIDTH), jnp.int32)
        query_doc = jnp.zeros((blocks, 1), jnp.int32)
        end = jnp.int32(0)
        for j in range(lengths.shape[1]):
            end = end + lengths[0, j]
            key_doc = key_doc + (key_block >= end).astype(jnp.int32)
            query_doc = query_doc + (query_block >= end).astype(jnp.int32)
        spread = lax.broadcasted_iota(jnp.int32, (tiles.shape[2], HEAD_WIDTH), 0) == key_block
        listed = jnp.dot(
            listed_tiles, spread.astype(jnp.float32).astype(jnp.bfloat16),
            preferred_element_type=jnp.float32,
        )
        allowed = (query_doc == key_doc) & (key_block <= query_block) & (key_block >= 0)
        allowed = allowed & ((listed > 0.5) | (key_block == query_block))
        bias[offset] = jnp.where(allowed, 0.0, NEVER)


def place_kernel(cap, received, keys, values, order):
    packs = received.shape[0]
    size = keys.shape[0] // (packs * cap)
    half = cap * size
    for s in range(packs):
        listed = received[s, 2 * half:, :].astype(jnp.float32).astype(jnp.int32)
        for i in range(cap):
            slot = listed[i, 0]
            order[0, slot] = s * cap + i
            rows = pl.ds(pl.multiple_of(slot * size, size), size)
            keys[rows, :] = received[s, i * size:(i + 1) * size, :]
            values[rows, :] = received[s, half + i * size:half + (i + 1) * size, :]


def first_document(lengths, position):
    start, end = jnp.int32(0), jnp.int32(0)
    total = jnp.int32(0)
    for j in range(lengths.shape[1]):
        after = total + lengths[0, j]
        inside = (total <= position) & (position < after)
        start = jnp.where(inside, total, start)
        end = jnp.where(inside, after, end)
        total = after
    return start, end


def reach_of(lengths, place, offset, blocks):
    start, end = first_document(lengths, place * blocks)
    low = (place - offset) * blocks
    rows = jnp.where(start < low + blocks, jnp.minimum(end - place * blocks, blocks), 0)
    return jnp.where(low >= 0, rows, 0), jnp.maximum(start - low, 0)


def beside_ones(values):
    return jnp.concatenate([values, jnp.ones(values.shape, values.dtype)], axis=1)


def query_rows(received, order, bias, i, size):
    source = pl.ds(pl.multiple_of(order[0, i] * size, size), size)
    barred = jnp.broadcast_to(bias[pl.ds(i, 1), :], (QUERY_HEADS * size, HEAD_WIDTH))
    return jnp.concatenate(
        [heads_as_rows(received[source, :]), barred.astype(jnp.bfloat16)], axis=1
    )


def score(rows, keys, block_of):
    return lax.dot_general(
        rows, jnp.concatenate([keys, block_of], axis=1), (((1,), (1,)), ((), ())),
        preferred_element_type=jnp.float32,
    )


def weigh(scores, level):
    return jnp.exp2(scores * SCALE - level).astype(jnp.bfloat16)


def largest(sums, so_far):
    parts = sums[:, HEAD_WIDTH:]
    return jnp.maximum(so_far, jnp.max(parts.reshape(-1, 8, HEAD_WIDTH), axis=0))


def divided(sums, size):
    return heads_as_columns(sums[:, :HEAD_WIDTH] / sums[:, HEAD_WIDTH:], size).astype(jnp.bfloat16)


def heads_as_rows(block):
    return jnp.concatenate(
        [block[:, h * HEAD_WIDTH:(h + 1) * HEAD_WIDTH] for h in range(QUERY_HEADS)], axis=0
    )


def heads_as_columns(rows, size):
    return jnp.concatenate(
        [rows[h * size:(h + 1) * size] for h in range(QUERY_HEADS)], axis=1
    )


def own_kernel(
    order, bias_in, block_of, received, keys, values,
    out, state, level,
    stage, sem,
):
    bias = bias_in.at[0]
    blocks = bias.shape[0]
    tokens = keys.shape[0]
    size = tokens // blocks
    group = QUERY_HEADS * size
    row = lax.rem(lax.broadcasted_iota(jnp.int32, (group, 2 * size), 0), size)
    lane = lax.broadcasted_iota(jnp.int32, (group, 2 * size), 1)

    work = []
    for i in range(blocks):
        width = (i // 2 + 1) * 2 * size
        spans = [(low, min(low + CHUNK, width)) for low in range(0, width, CHUNK)]
        for n, span in enumerate(spans[-1:] + spans[:-1]):
            work.append((i, span, n == 0, n == len(spans) - 1))

    rows = {}

    def start(i, span):
        if i not in rows:
            rows[i] = query_rows(received, order, bias, i, size)
        return score(rows[i], keys[span[0]:span[1], :], block_of[span[0]:span[1], :])

    worst = jnp.zeros((8, HEAD_WIDTH), jnp.float32)
    copies = []
    scores = start(*work[0][:2])
    for n, (i, span, opening, closing) in enumerate(work):
        ahead = start(*work[n + 1][:2]) if n + 1 < len(work) else None
        if opening:
            cut = span[1] - span[0] - 2 * size
            tail = jnp.where(lane - (i % 2) * size > row, NEVER, scores[:, cut:])
            scores = jnp.concatenate([scores[:, :cut], tail], axis=1) if cut else tail
            top = jnp.max(scores, axis=1, keepdims=True) * SCALE
            weights = []
            width = span[1]
        weights.append(weigh(scores, top))
        if closing:
            ordered = weights[1:] + weights[:1]
            joined = jnp.concatenate(ordered, axis=1) if len(ordered) > 1 else ordered[0]
            sums = jnp.dot(
                joined, beside_ones(values[:width, :]), preferred_element_type=jnp.float32
            )
            worst = largest(sums, worst)
            where = slice(i * group, (i + 1) * group)
            held = slice(i * size, (i + 1) * size)
            state[where, :] = sums
            level[where, :] = jnp.broadcast_to(top, (group, HEAD_WIDTH))
            stage[held, :] = divided(sums, size)
            copy = pltpu.make_async_copy(stage.at[held], out.at[0, held], sem.at[i])
            copy.start()
            copies.append(copy)
        scores = ahead
    for copy in copies:
        copy.wait()

    @pl.when(jnp.logical_not(jnp.max(worst) < MOST))
    def _():
        def again(i, carry):
            where = pl.ds(pl.multiple_of(i * group, group), group)
            held = pl.ds(pl.multiple_of(i * size, size), size)
            scores = score(
                query_rows(received, order, bias, i, size), keys[...], block_of[...]
            )
            query = i * size + lax.rem(lax.broadcasted_iota(jnp.int32, scores.shape, 0), size)
            key = lax.broadcasted_iota(jnp.int32, scores.shape, 1)
            scores = jnp.where(key > query, NEVER, scores)
            top = jnp.max(scores, axis=1, keepdims=True) * SCALE
            sums = jnp.dot(
                weigh(scores, top), beside_ones(values[...]), preferred_element_type=jnp.float32
            )
            state[where, :] = sums
            level[where, :] = jnp.broadcast_to(top, (group, HEAD_WIDTH))
            stage[held, :] = divided(sums, size)
            copy = pltpu.make_async_copy(stage.at[held], out.at[0, held], sem.at[0])
            copy.start()
            copy.wait()
            return carry

        lax.fori_loop(0, blocks, again, 0)


def hop_kernel(
    offset, order, lengths, bias_in, block_of, received, keys, values,
    out_in, level_in, state_in, *refs,
):
    together = 4
    stage, sem = refs[-2:]
    out, level = refs[0], refs[1]
    place = lax.axis_index("ctx")
    bias = bias_in.at[offset]
    blocks = bias.shape[0]
    tokens = keys.shape[0]
    size = tokens // blocks
    group = QUERY_HEADS * size
    reads, first = reach_of(lengths, place, offset, blocks)

    def keep(i, sums):
        held = pl.ds(pl.multiple_of(i * size, size), size)
        stage[held, :] = divided(sums, size)
        if offset < REACH:
            refs[2][pl.ds(pl.multiple_of(i * group, group), group), :] = sums

    def over(low):
        spans = [(at, at + CHUNK) for at in range(low, tokens, CHUNK)]
        work = [(u, span) for u in range(together) for span in spans]

        def step(n, worst):
            i = n * together
            rows = {}

            def start(u, span):
                if u not in rows:
                    rows[u] = query_rows(received, order, bias, i + u, size)
                return score(rows[u], keys[span[0]:span[1], :], block_of[span[0]:span[1], :])

            scores = start(*work[0])
            for m, (u, span) in enumerate(work):
                ahead = start(*work[m + 1]) if m + 1 < len(work) else None
                where = pl.ds(pl.multiple_of((i + u) * group, group), group)
                if span is spans[0]:
                    base = level_in[where, :]
                    base = jnp.concatenate([base] * (CHUNK // HEAD_WIDTH), axis=1)
                    weights = []
                weights.append(weigh(scores, base))
                if span is spans[-1]:
                    joined = jnp.concatenate(weights, axis=1) if len(weights) > 1 else weights[0]
                    sums = state_in[where, :] + jnp.dot(
                        joined, beside_ones(values[low:, :]), preferred_element_type=jnp.float32
                    )
                    worst = largest(sums, worst)
                    keep(i + u, sums)
                scores = ahead
            held = pl.ds(pl.multiple_of(i * size, size), together * size)
            pltpu.make_async_copy(stage.at[held], out.at[0, held], sem).start()
            return worst

        def finish(n, carry):
            held = pl.ds(pl.multiple_of(n * together * size, size), together * size)
            pltpu.make_async_copy(stage.at[held], out.at[0, held], sem).wait()
            return carry

        steps = pl.cdiv(reads, together)
        worst = lax.fori_loop(0, steps, step, jnp.zeros((8, HEAD_WIDTH), jnp.float32))
        lax.fori_loop(0, steps, finish, 0)

        @pl.when(jnp.logical_not(jnp.max(worst) < MOST))
        def _():
            def again(i, carry):
                where = pl.ds(pl.multiple_of(i * group, group), group)
                held = pl.ds(pl.multiple_of(i * size, size), size)
                scores = score(
                    query_rows(received, order, bias, i, size), keys[...], block_of[...]
                )
                before = level_in[where, :]
                top = jnp.max(scores, axis=1, keepdims=True) * SCALE
                now = jnp.maximum(before, top)
                factor = jnp.exp2(before - now)
                sums = jnp.concatenate([factor, factor], axis=1) * state_in[where, :] + jnp.dot(
                    weigh(scores, now[:, :1]), beside_ones(values[...]),
                    preferred_element_type=jnp.float32,
                )
                level[where, :] = now
                keep(i, sums)
                copy = pltpu.make_async_copy(stage.at[held], out.at[0, held], sem)
                copy.start()
                copy.wait()
                return carry

            lax.fori_loop(0, steps * together, again, 0)

    part = first // (blocks // 4)
    for n in range(4):
        pl.when((reads > 0) & (part == n))(functools.partial(over, n * (tokens // 4)))


def per_device(queries, keys, values, dest_replica, dest_slot, doc_lengths, tile_mask):
    tokens = queries.shape[1]
    width = queries.shape[2]
    blocks = dest_replica.shape[1]
    size = tokens // blocks
    packs = lax.axis_size("dp")
    cap = blocks // packs
    bf16, f32 = jnp.bfloat16, jnp.float32
    rows = tokens * QUERY_HEADS
    params = pltpu.CompilerParams(vmem_limit_bytes=VMEM_LIMIT)
    small = pltpu.CompilerParams(vmem_limit_bytes=VMEM_SMALL)

    def cost(flops, moved):
        return pl.CostEstimate(flops=flops, bytes_accessed=moved, transcendentals=0)

    def route(sent):
        return lax.all_to_all(sent, "dp", split_axis=0, concat_axis=0, tiled=True)

    dma = pltpu.SemaphoreType.DMA
    counts = pltpu.SMEM((packs,), jnp.int32)
    kv_send = pl.pallas_call(
        functools.partial(pack_kv_kernel, cap),
        out_shape=jax.ShapeDtypeStruct((packs, 2 * cap * size + SLOT_ROWS, HEAD_WIDTH), bf16),
        in_specs=[SMEM, SMEM, VMEM, VMEM],
        out_specs=VMEM,
        scratch_shapes=[counts, pltpu.SMEM((blocks,), jnp.int32)],
        cost_estimate=cost(0, 4 * tokens * HEAD_WIDTH * 2),
        name="pack_kv",
    )(dest_replica, dest_slot, keys, values)
    kv_recv = route(kv_send)
    q_send, bias, block_of = pl.pallas_call(
        functools.partial(pack_q_kernel, cap),
        out_shape=(
            jax.ShapeDtypeStruct((packs, cap * size, width), bf16),
            jax.ShapeDtypeStruct((REACH + 1, blocks, HEAD_WIDTH), f32),
            jax.ShapeDtypeStruct((tokens, HEAD_WIDTH), bf16),
        ),
        in_specs=[SMEM, SMEM, VMEM, VMEM],
        out_specs=(VMEM, VMEM, VMEM),
        scratch_shapes=[counts],
        compiler_params=small,
        cost_estimate=cost(0, 2 * tokens * width * 2),
        name="pack_q",
    )(dest_replica, doc_lengths, tile_mask, queries)
    q_recv = route(q_send).reshape(tokens, width)
    moving_k, moving_v, order = pl.pallas_call(
        functools.partial(place_kernel, cap),
        out_shape=(
            jax.ShapeDtypeStruct((tokens, HEAD_WIDTH), bf16),
            jax.ShapeDtypeStruct((tokens, HEAD_WIDTH), bf16),
            jax.ShapeDtypeStruct((1, blocks), jnp.int32),
        ),
        in_specs=[VMEM],
        out_specs=(VMEM, VMEM, SMEM),
        compiler_params=small,
        cost_estimate=cost(0, 4 * tokens * HEAD_WIDTH * 2),
        name="place_kv",
    )(kv_recv)

    out_shape = jax.ShapeDtypeStruct((1, tokens, width), bf16)
    level_shape = jax.ShapeDtypeStruct((rows, HEAD_WIDTH), f32)
    sums_shape = jax.ShapeDtypeStruct((rows, 2 * HEAD_WIDTH), f32)
    stage = pltpu.VMEM((tokens, width), bf16)

    def attend_back(offset, keys, values, out, level, sums):
        last = offset == REACH
        return pl.pallas_call(
            functools.partial(hop_kernel, offset),
            out_shape=(out_shape, level_shape) + (() if last else (sums_shape,)),
            in_specs=[SMEM, SMEM] + [VMEM] * 5 + [ANY, VMEM, VMEM],
            out_specs=(ANY, VMEM) + (() if last else (VMEM,)),
            scratch_shapes=[stage, dma],
            input_output_aliases={7: 0, 8: 1},
            compiler_params=params,
            cost_estimate=cost(2 * 2 * rows * tokens * HEAD_WIDTH, 8 * tokens * width),
            name=f"attend_back_{offset}",
        )(order, doc_lengths, bias, block_of, q_recv, keys, values, out, level, sums)

    back_k = shifted(moving_k, "ctx")
    back_v = shifted(moving_v, "ctx")
    out, sums, level = pl.pallas_call(
        own_kernel,
        out_shape=(out_shape, sums_shape, level_shape),
        in_specs=[SMEM] + [VMEM] * 5,
        out_specs=(ANY, VMEM, VMEM),
        scratch_shapes=[stage, dma((blocks,))],
        compiler_params=params,
        cost_estimate=cost(2 * rows * tokens * HEAD_WIDTH, 8 * tokens * width),
        name="attend_own",
    )(order, bias, block_of, q_recv, moving_k, moving_v)
    far_v, out, sums, level = lax.optimization_barrier((back_v, out, sums, level))
    far_k = shifted(back_k, "ctx")
    far_v = shifted(far_v, "ctx")
    out, level, sums = attend_back(1, back_k, back_v, out, level, sums)
    return attend_back(2, far_k, far_v, out, level, sums)[0]


def solution(mesh):
    return jax.shard_map(
        per_device,
        mesh=mesh,
        in_specs=(
            P("dp", "ctx", None),
            P("dp", "ctx", None),
            P("dp", "ctx", None),
            P("dp", "ctx"),
            P("dp", "ctx"),
            P("dp", None),
            P("dp", "ctx", None),
        ),
        out_specs=P("dp", "ctx", None),
        check_vma=False,
    )
```

```python
import functools

import jax
import jax.numpy as jnp
from jax import lax
from jax.experimental import pallas as pl
from jax.experimental.pallas import tpu as pltpu
from jax.sharding import PartitionSpec as P

HEAD_WIDTH = 128
QUERY_HEADS = 4
SCALE = HEAD_WIDTH ** (-0.5) * 1.4426950408889634
NEVER = -1e30
MOST = 1e30
CHUNK = 256
SLOT_ROWS = 16
REACH = 2
VMEM_LIMIT = 32 * 1024 * 1024
VMEM_SMALL = 8 * 1024 * 1024

ANY = pl.BlockSpec(memory_space=pl.ANY)
SMEM = pl.BlockSpec(memory_space=pltpu.SMEM)
VMEM = pl.BlockSpec(memory_space=pltpu.VMEM)


def shifted(value, axis):
    count = lax.axis_size(axis)
    return lax.ppermute(value, axis, [(source, source + 1) for source in range(count - 1)])


def pack_kv_kernel(cap, targets, slots, keys, values, send, counts, slot_of):
    packs = send.shape[0]
    blocks = targets.shape[1]
    size = keys.shape[1] // blocks
    half = cap * size
    for t in range(packs):
        counts[t] = 0
    for j in range(blocks):
        t = targets[0, j]
        rank = counts[t]
        counts[t] = rank + 1
        slot_of[t * cap + rank] = lax.rem(slots[0, j], blocks)
        rows = slice(j * size, (j + 1) * size)
        to = pl.multiple_of(rank * size, size)
        send[t, pl.ds(to, size), :] = keys[0, rows, :]
        send[t, pl.ds(to + half, size), :] = values[0, rows, :]
    row = lax.broadcasted_iota(jnp.int32, (SLOT_ROWS, HEAD_WIDTH), 0)
    for t in range(packs):
        listed = jnp.zeros(row.shape, jnp.int32)
        for i in range(cap):
            listed = jnp.where(row == i, slot_of[t * cap + i], listed)
        send[t, 2 * half:, :] = listed.astype(jnp.float32).astype(jnp.bfloat16)


def pack_q_kernel(cap, targets, lengths, tiles, queries, send, bias, block_of, counts):
    packs = send.shape[0]
    blocks = targets.shape[1]
    tokens = queries.shape[1]
    size = tokens // blocks
    place = lax.axis_index("ctx")
    for t in range(packs):
        counts[t] = 0
    for j in range(blocks):
        t = targets[0, j]
        rank = counts[t]
        counts[t] = rank + 1
        to = pl.multiple_of(rank * size, size)
        send[t, pl.ds(to, size), :] = queries[0, j * size:(j + 1) * size, :]

    block = lax.broadcasted_iota(jnp.int32, (tokens, HEAD_WIDTH), 1)
    of_key = lax.broadcasted_iota(jnp.int32, (tokens, HEAD_WIDTH), 0) // size
    block_of[...] = (block == of_key).astype(jnp.float32).astype(jnp.bfloat16)
    query_block = place * blocks + lax.broadcasted_iota(jnp.int32, (blocks, 1), 0)
    listed_tiles = tiles[0].astype(jnp.float32).astype(jnp.bfloat16)
    for offset in range(bias.shape[0]):
        low = (place - offset) * blocks
        key_block = low + lax.broadcasted_iota(jnp.int32, (1, HEAD_WIDTH), 1)
        key_doc = jnp.zeros((1, HEAD_WIDTH), jnp.int32)
        query_doc = jnp.zeros((blocks, 1), jnp.int32)
        end = jnp.int32(0)
        for j in range(lengths.shape[1]):
            end = end + lengths[0, j]
            key_doc = key_doc + (key_block >= end).astype(jnp.int32)
            query_doc = query_doc + (query_block >= end).astype(jnp.int32)
        spread = lax.broadcasted_iota(jnp.int32, (tiles.shape[2], HEAD_WIDTH), 0) == key_block
        listed = jnp.dot(
            listed_tiles, spread.astype(jnp.float32).astype(jnp.bfloat16),
            preferred_element_type=jnp.float32,
        )
        allowed = (query_doc == key_doc) & (key_block <= query_block) & (key_block >= 0)
        allowed = allowed & ((listed > 0.5) | (key_block == query_block))
        bias[offset] = jnp.where(allowed, 0.0, NEVER)


def place_kernel(cap, received, early, rest, order, placed):
    packs = received.shape[0]
    tokens = placed.shape[0] // 2
    size = tokens // (packs * cap)
    half = cap * size
    for s in range(packs):
        listed = received[s, 2 * half:, :].astype(jnp.float32).astype(jnp.int32)
        for i in range(cap):
            slot = listed[i, 0]
            order[0, slot] = s * cap + i
            to = pl.multiple_of(slot * size, size)
            placed[pl.ds(to, size), :] = received[s, i * size:(i + 1) * size, :]
            placed[pl.ds(to + tokens, size), :] = (
                received[s, half + i * size:half + (i + 1) * size, :]
            )
    early[...] = placed[:tokens // 2, :]
    rest[...] = placed[tokens // 2:, :]


def first_document(lengths, position):
    start, end = jnp.int32(0), jnp.int32(0)
    total = jnp.int32(0)
    for j in range(lengths.shape[1]):
        after = total + lengths[0, j]
        inside = (total <= position) & (position < after)
        start = jnp.where(inside, total, start)
        end = jnp.where(inside, after, end)
        total = after
    return start, end


def reach_of(lengths, place, offset, blocks):
    start, end = first_document(lengths, place * blocks)
    low = (place - offset) * blocks
    rows = jnp.where(start < low + blocks, jnp.minimum(end - place * blocks, blocks), 0)
    return jnp.where(low >= 0, rows, 0), jnp.maximum(start - low, 0)


def keys_of(early, rest, low, high):
    half = early.shape[0]
    if high <= half:
        return early[low:high, :]
    if low >= half:
        return rest[low - half:high - half, :]
    return jnp.concatenate([early[low:, :], rest[:high - half, :]], axis=0)


def values_of(early, rest, low, high):
    half = early.shape[0]
    return beside_ones(rest[half + low:half + high, :])


def beside_ones(values):
    return jnp.concatenate([values, jnp.ones(values.shape, values.dtype)], axis=1)


def query_rows(received, order, bias, i, size):
    source = pl.ds(pl.multiple_of(order[0, i] * size, size), size)
    barred = jnp.broadcast_to(bias[pl.ds(i, 1), :], (QUERY_HEADS * size, HEAD_WIDTH))
    return jnp.concatenate(
        [heads_as_rows(received[source, :]), barred.astype(jnp.bfloat16)], axis=1
    )


def score(rows, keys, block_of):
    return lax.dot_general(
        rows, jnp.concatenate([keys, block_of], axis=1), (((1,), (1,)), ((), ())),
        preferred_element_type=jnp.float32,
    )


def weigh(scores, level):
    return jnp.exp2(scores * SCALE - level).astype(jnp.bfloat16)


def largest(sums, so_far):
    parts = sums[:, HEAD_WIDTH:]
    return jnp.maximum(so_far, jnp.max(parts.reshape(-1, 8, HEAD_WIDTH), axis=0))


def divided(sums, size):
    return heads_as_columns(sums[:, :HEAD_WIDTH] / sums[:, HEAD_WIDTH:], size).astype(jnp.bfloat16)


def heads_as_rows(block):
    return jnp.concatenate(
        [block[:, h * HEAD_WIDTH:(h + 1) * HEAD_WIDTH] for h in range(QUERY_HEADS)], axis=0
    )


def heads_as_columns(rows, size):
    return jnp.concatenate(
        [rows[h * size:(h + 1) * size] for h in range(QUERY_HEADS)], axis=1
    )


def own_kernel(
    order, bias_in, block_of, received, early, rest,
    out, state, level,
    stage, sem,
):
    bias = bias_in.at[0]
    blocks = bias.shape[0]
    tokens = 2 * early.shape[0]
    size = tokens // blocks
    group = QUERY_HEADS * size
    row = lax.rem(lax.broadcasted_iota(jnp.int32, (group, 2 * size), 0), size)
    lane = lax.broadcasted_iota(jnp.int32, (group, 2 * size), 1)

    work = []
    for i in range(blocks):
        width = (i // 2 + 1) * 2 * size
        spans = [(low, min(low + CHUNK, width)) for low in range(0, width, CHUNK)]
        for n, span in enumerate(spans[-1:] + spans[:-1]):
            work.append((i, span, n == 0, n == len(spans) - 1))

    rows = {}

    def start(i, span):
        if i not in rows:
            rows[i] = query_rows(received, order, bias, i, size)
        return score(rows[i], keys_of(early, rest, *span), block_of[span[0]:span[1], :])

    worst = jnp.zeros((8, HEAD_WIDTH), jnp.float32)
    copies = []
    scores = start(*work[0][:2])
    for n, (i, span, opening, closing) in enumerate(work):
        ahead = start(*work[n + 1][:2]) if n + 1 < len(work) else None
        if opening:
            cut = span[1] - span[0] - 2 * size
            tail = jnp.where(lane - (i % 2) * size > row, NEVER, scores[:, cut:])
            scores = jnp.concatenate([scores[:, :cut], tail], axis=1) if cut else tail
            top = jnp.max(scores, axis=1, keepdims=True) * SCALE
            weights = []
            width = span[1]
        weights.append(weigh(scores, top))
        if closing:
            ordered = weights[1:] + weights[:1]
            joined = jnp.concatenate(ordered, axis=1) if len(ordered) > 1 else ordered[0]
            sums = jnp.dot(
                joined, values_of(early, rest, 0, width), preferred_element_type=jnp.float32
            )
            worst = largest(sums, worst)
            where = slice(i * group, (i + 1) * group)
            held = slice(i * size, (i + 1) * size)
            state[where, :] = sums
            level[where, :] = jnp.broadcast_to(top, (group, HEAD_WIDTH))
            stage[held, :] = divided(sums, size)
            copy = pltpu.make_async_copy(stage.at[held], out.at[0, held], sem.at[i])
            copy.start()
            copies.append(copy)
        scores = ahead
    for copy in copies:
        copy.wait()

    @pl.when(jnp.logical_not(jnp.max(worst) < MOST))
    def _():
        def again(i, carry):
            where = pl.ds(pl.multiple_of(i * group, group), group)
            held = pl.ds(pl.multiple_of(i * size, size), size)
            scores = score(
                query_rows(received, order, bias, i, size),
                keys_of(early, rest, 0, tokens), block_of[...],
            )
            query = i * size + lax.rem(lax.broadcasted_iota(jnp.int32, scores.shape, 0), size)
            key = lax.broadcasted_iota(jnp.int32, scores.shape, 1)
            scores = jnp.where(key > query, NEVER, scores)
            top = jnp.max(scores, axis=1, keepdims=True) * SCALE
            sums = jnp.dot(
                weigh(scores, top), values_of(early, rest, 0, tokens),
                preferred_element_type=jnp.float32,
            )
            state[where, :] = sums
            level[where, :] = jnp.broadcast_to(top, (group, HEAD_WIDTH))
            stage[held, :] = divided(sums, size)
            copy = pltpu.make_async_copy(stage.at[held], out.at[0, held], sem.at[0])
            copy.start()
            copy.wait()
            return carry

        lax.fori_loop(0, blocks, again, 0)


def hop_kernel(
    offset, order, lengths, bias_in, block_of, received, early, rest,
    out_in, level_in, state_in, *refs,
):
    stage, sem = refs[-2:]
    out, level = refs[0], refs[1]
    place = lax.axis_index("ctx")
    bias = bias_in.at[offset]
    blocks = bias.shape[0]
    tokens = 2 * early.shape[0]
    size = tokens // blocks
    group = QUERY_HEADS * size
    reads, first = reach_of(lengths, place, offset, blocks)

    def keep(i, sums):
        held = pl.ds(pl.multiple_of(i * size, size), size)
        stage[held, :] = divided(sums, size)
        if offset < REACH:
            refs[2][pl.ds(pl.multiple_of(i * group, group), group), :] = sums

    def over(low, together):
        spans = [(at, at + CHUNK) for at in range(low, tokens, CHUNK)]
        work = [(u, span) for u in range(together) for span in spans]

        def step(n, worst):
            i = n * together
            rows = {}

            def start(u, span):
                if u not in rows:
                    rows[u] = query_rows(received, order, bias, i + u, size)
                return score(rows[u], keys_of(early, rest, *span), block_of[span[0]:span[1], :])

            scores = start(*work[0])
            for m, (u, span) in enumerate(work):
                ahead = start(*work[m + 1]) if m + 1 < len(work) else None
                where = pl.ds(pl.multiple_of((i + u) * group, group), group)
                if span is spans[0]:
                    base = level_in[where, :]
                    base = jnp.concatenate([base] * (CHUNK // HEAD_WIDTH), axis=1)
                    weights = []
                weights.append(weigh(scores, base))
                if span is spans[-1]:
                    joined = jnp.concatenate(weights, axis=1) if len(weights) > 1 else weights[0]
                    sums = state_in[where, :] + jnp.dot(
                        joined, values_of(early, rest, low, tokens), preferred_element_type=jnp.float32
                    )
                    worst = jnp.where(i + u < reads, largest(sums, worst), worst)
                    keep(i + u, sums)
                scores = ahead
            lax.fori_loop(i, jnp.minimum(i + together, reads), send, 0)
            return worst

        def copy_of(i):
            held = pl.ds(pl.multiple_of(i * size, size), size)
            return pltpu.make_async_copy(stage.at[held], out.at[0, held], sem)

        def send(i, carry):
            copy_of(i).start()
            return carry

        def finish(i, carry):
            copy_of(i).wait()
            return carry

        steps = pl.cdiv(reads, together)
        worst = lax.fori_loop(0, steps, step, jnp.zeros((8, HEAD_WIDTH), jnp.float32))
        lax.fori_loop(0, reads, finish, 0)

        @pl.when(jnp.logical_not(jnp.max(worst) < MOST))
        def _():
            def again(i, carry):
                where = pl.ds(pl.multiple_of(i * group, group), group)
                scores = score(
                    query_rows(received, order, bias, i, size),
                    keys_of(early, rest, 0, tokens), block_of[...],
                )
                before = level_in[where, :]
                top = jnp.max(scores, axis=1, keepdims=True) * SCALE
                now = jnp.maximum(before, top)
                factor = jnp.exp2(before - now)
                sums = jnp.concatenate([factor, factor], axis=1) * state_in[where, :] + jnp.dot(
                    weigh(scores, now[:, :1]), values_of(early, rest, 0, tokens),
                    preferred_element_type=jnp.float32,
                )
                level[where, :] = now
                keep(i, sums)
                copy_of(i).start()
                copy_of(i).wait()
                return carry

            lax.fori_loop(0, reads, again, 0)

    part = first // (blocks // 4)
    for n, together in enumerate((4, 4, 8, 8)):
        pl.when((reads > 0) & (part == n))(functools.partial(over, n * (tokens // 4), together))


def per_device(queries, keys, values, dest_replica, dest_slot, doc_lengths, tile_mask):
    tokens = queries.shape[1]
    width = queries.shape[2]
    blocks = dest_replica.shape[1]
    size = tokens // blocks
    packs = lax.axis_size("dp")
    cap = blocks // packs
    bf16, f32 = jnp.bfloat16, jnp.float32
    rows = tokens * QUERY_HEADS
    params = pltpu.CompilerParams(vmem_limit_bytes=VMEM_LIMIT)
    small = pltpu.CompilerParams(vmem_limit_bytes=VMEM_SMALL)

    def cost(flops, moved):
        return pl.CostEstimate(flops=flops, bytes_accessed=moved, transcendentals=0)

    def route(sent):
        return lax.all_to_all(sent, "dp", split_axis=0, concat_axis=0, tiled=True)

    dma = pltpu.SemaphoreType.DMA
    counts = pltpu.SMEM((packs,), jnp.int32)
    kv_send = pl.pallas_call(
        functools.partial(pack_kv_kernel, cap),
        out_shape=jax.ShapeDtypeStruct((packs, 2 * cap * size + SLOT_ROWS, HEAD_WIDTH), bf16),
        in_specs=[SMEM, SMEM, VMEM, VMEM],
        out_specs=VMEM,
        scratch_shapes=[counts, pltpu.SMEM((blocks,), jnp.int32)],
        cost_estimate=cost(0, 4 * tokens * HEAD_WIDTH * 2),
        name="pack_kv",
    )(dest_replica, dest_slot, keys, values)
    kv_recv = route(kv_send)
    q_send, bias, block_of = pl.pallas_call(
        functools.partial(pack_q_kernel, cap),
        out_shape=(
            jax.ShapeDtypeStruct((packs, cap * size, width), bf16),
            jax.ShapeDtypeStruct((REACH + 1, blocks, HEAD_WIDTH), f32),
            jax.ShapeDtypeStruct((tokens, HEAD_WIDTH), bf16),
        ),
        in_specs=[SMEM, SMEM, VMEM, VMEM],
        out_specs=(VMEM, VMEM, VMEM),
        scratch_shapes=[counts],
        compiler_params=small,
        cost_estimate=cost(0, 2 * tokens * width * 2),
        name="pack_q",
    )(dest_replica, doc_lengths, tile_mask, queries)
    q_recv = route(q_send).reshape(tokens, width)
    early, rest, order = pl.pallas_call(
        functools.partial(place_kernel, cap),
        out_shape=(
            jax.ShapeDtypeStruct((tokens // 2, HEAD_WIDTH), bf16),
            jax.ShapeDtypeStruct((tokens // 2 * 3, HEAD_WIDTH), bf16),
            jax.ShapeDtypeStruct((1, blocks), jnp.int32),
        ),
        in_specs=[VMEM],
        out_specs=(VMEM, VMEM, SMEM),
        scratch_shapes=[pltpu.VMEM((2 * tokens, HEAD_WIDTH), bf16)],
        compiler_params=small,
        cost_estimate=cost(0, 4 * tokens * HEAD_WIDTH * 2),
        name="place_kv",
    )(kv_recv)

    out_shape = jax.ShapeDtypeStruct((1, tokens, width), bf16)
    level_shape = jax.ShapeDtypeStruct((rows, HEAD_WIDTH), f32)
    sums_shape = jax.ShapeDtypeStruct((rows, 2 * HEAD_WIDTH), f32)
    stage = pltpu.VMEM((tokens, width), bf16)

    def attend_back(offset, early, rest, out, level, sums):
        last = offset == REACH
        return pl.pallas_call(
            functools.partial(hop_kernel, offset),
            out_shape=(out_shape, level_shape) + (() if last else (sums_shape,)),
            in_specs=[SMEM, SMEM] + [VMEM] * 5 + [ANY, VMEM, VMEM],
            out_specs=(ANY, VMEM) + (() if last else (VMEM,)),
            scratch_shapes=[stage, dma],
            input_output_aliases={7: 0, 8: 1},
            compiler_params=params,
            cost_estimate=cost(2 * 2 * rows * tokens * HEAD_WIDTH, 8 * tokens * width),
            name=f"attend_back_{offset}",
        )(order, doc_lengths, bias, block_of, q_recv, early, rest, out, level, sums)

    back_early = shifted(early, "ctx")
    back_rest = shifted(rest, "ctx")
    out, sums, level = pl.pallas_call(
        own_kernel,
        out_shape=(out_shape, sums_shape, level_shape),
        in_specs=[SMEM] + [VMEM] * 5,
        out_specs=(ANY, VMEM, VMEM),
        scratch_shapes=[stage, dma((blocks,))],
        compiler_params=params,
        cost_estimate=cost(2 * rows * tokens * HEAD_WIDTH, 8 * tokens * width),
        name="attend_own",
    )(order, bias, block_of, q_recv, early, rest)
    far_rest, out, sums, level = lax.optimization_barrier((back_rest, out, sums, level))
    far_early = shifted(back_early, "ctx")
    far_rest = shifted(far_rest, "ctx")
    out, level, sums = attend_back(1, back_early, back_rest, out, level, sums)
    return attend_back(2, far_early, far_rest, out, level, sums)[0]


def solution(mesh):
    return jax.shard_map(
        per_device,
        mesh=mesh,
        in_specs=(
            P("dp", "ctx", None),
            P("dp", "ctx", None),
            P("dp", "ctx", None),
            P("dp", "ctx"),
            P("dp", "ctx"),
            P("dp", None),
            P("dp", "ctx", None),
        ),
        out_specs=P("dp", "ctx", None),
        check_vma=False,
    )
```

```python
import functools

import jax
import jax.numpy as jnp
from jax import lax
from jax.experimental import pallas as pl
from jax.experimental.pallas import tpu as pltpu
from jax.sharding import PartitionSpec as P

HEAD_WIDTH = 128
QUERY_HEADS = 4
SCALE = HEAD_WIDTH ** (-0.5) * 1.4426950408889634
NEVER = -1e30
MOST = 1e30
CHUNK = 256
SLOT_ROWS = 16
REACH = 2
PIECE = 4
VMEM_LIMIT = 32 * 1024 * 1024
VMEM_SMALL = 8 * 1024 * 1024

ANY = pl.BlockSpec(memory_space=pl.ANY)
SMEM = pl.BlockSpec(memory_space=pltpu.SMEM)
VMEM = pl.BlockSpec(memory_space=pltpu.VMEM)


def shifted(value, axis):
    count = lax.axis_size(axis)
    return lax.ppermute(value, axis, [(source, source + 1) for source in range(count - 1)])


def pack_kv_kernel(cap, targets, slots, keys, values, send, counts, slot_of):
    packs = send.shape[0]
    blocks = targets.shape[1]
    size = keys.shape[1] // blocks
    half = cap * size
    for t in range(packs):
        counts[t] = 0
    for j in range(blocks):
        t = targets[0, j]
        rank = counts[t]
        counts[t] = rank + 1
        slot_of[t * cap + rank] = lax.rem(slots[0, j], blocks)
        rows = slice(j * size, (j + 1) * size)
        to = pl.multiple_of(rank * size, size)
        send[t, pl.ds(to, size), :] = keys[0, rows, :]
        send[t, pl.ds(to + half, size), :] = values[0, rows, :]
    row = lax.broadcasted_iota(jnp.int32, (SLOT_ROWS, HEAD_WIDTH), 0)
    for t in range(packs):
        listed = jnp.zeros(row.shape, jnp.int32)
        for i in range(cap):
            listed = jnp.where(row == i, slot_of[t * cap + i], listed)
        send[t, 2 * half:, :] = listed.astype(jnp.float32).astype(jnp.bfloat16)


def pack_q_kernel(cap, targets, lengths, tiles, queries, send, bias, block_of, counts):
    packs = send.shape[0]
    blocks = targets.shape[1]
    tokens = queries.shape[1]
    size = tokens // blocks
    place = lax.axis_index("ctx")
    for t in range(packs):
        counts[t] = 0
    for j in range(blocks):
        t = targets[0, j]
        rank = counts[t]
        counts[t] = rank + 1
        to = pl.multiple_of(rank * size, size)
        send[t, pl.ds(to, size), :] = queries[0, j * size:(j + 1) * size, :]

    block = lax.broadcasted_iota(jnp.int32, (tokens, HEAD_WIDTH), 1)
    of_key = lax.broadcasted_iota(jnp.int32, (tokens, HEAD_WIDTH), 0) // size
    block_of[...] = (block == of_key).astype(jnp.float32).astype(jnp.bfloat16)
    query_block = place * blocks + lax.broadcasted_iota(jnp.int32, (blocks, 1), 0)
    listed_tiles = tiles[0].astype(jnp.float32).astype(jnp.bfloat16)
    for offset in range(bias.shape[0]):
        low = (place - offset) * blocks
        key_block = low + lax.broadcasted_iota(jnp.int32, (1, HEAD_WIDTH), 1)
        key_doc = jnp.zeros((1, HEAD_WIDTH), jnp.int32)
        query_doc = jnp.zeros((blocks, 1), jnp.int32)
        end = jnp.int32(0)
        for j in range(lengths.shape[1]):
            end = end + lengths[0, j]
            key_doc = key_doc + (key_block >= end).astype(jnp.int32)
            query_doc = query_doc + (query_block >= end).astype(jnp.int32)
        spread = lax.broadcasted_iota(jnp.int32, (tiles.shape[2], HEAD_WIDTH), 0) == key_block
        listed = jnp.dot(
            listed_tiles, spread.astype(jnp.float32).astype(jnp.bfloat16),
            preferred_element_type=jnp.float32,
        )
        allowed = (query_doc == key_doc) & (key_block <= query_block) & (key_block >= 0)
        allowed = allowed & ((listed > 0.5) | (key_block == query_block))
        bias[offset] = jnp.where(allowed, 0.0, NEVER)


def place_kernel(cap, received, early, rest, order, placed):
    packs = received.shape[0]
    tokens = placed.shape[0] // 2
    size = tokens // (packs * cap)
    half = cap * size
    for s in range(packs):
        listed = received[s, 2 * half:, :].astype(jnp.float32).astype(jnp.int32)
        for i in range(cap):
            slot = listed[i, 0]
            order[0, slot] = s * cap + i
            to = pl.multiple_of(slot * size, size)
            placed[pl.ds(to, size), :] = received[s, i * size:(i + 1) * size, :]
            placed[pl.ds(to + tokens, size), :] = (
                received[s, half + i * size:half + (i + 1) * size, :]
            )
    early[...] = placed[:early.shape[0], :]
    rest[...] = placed[early.shape[0]:, :]


def first_document(lengths, position):
    start, end = jnp.int32(0), jnp.int32(0)
    total = jnp.int32(0)
    for j in range(lengths.shape[1]):
        after = total + lengths[0, j]
        inside = (total <= position) & (position < after)
        start = jnp.where(inside, total, start)
        end = jnp.where(inside, after, end)
        total = after
    return start, end


def reach_of(lengths, place, offset, blocks):
    start, end = first_document(lengths, place * blocks)
    low = (place - offset) * blocks
    rows = jnp.where(start < low + blocks, jnp.minimum(end - place * blocks, blocks), 0)
    return jnp.where(low >= 0, rows, 0), jnp.maximum(start - low, 0)


def keys_of(early, rest, low, high):
    half = early.shape[0]
    if high <= half:
        return early[low:high, :]
    if low >= half:
        return rest[low - half:high - half, :]
    return jnp.concatenate([early[low:, :], rest[:high - half, :]], axis=0)


def values_of(early, rest, low, high):
    values = (early.shape[0] + rest.shape[0]) // 2 - early.shape[0]
    return beside_ones(rest[values + low:values + high, :])


def beside_ones(values):
    return jnp.concatenate([values, jnp.ones(values.shape, values.dtype)], axis=1)


def query_rows(received, order, bias, i, size):
    source = pl.ds(pl.multiple_of(order[0, i] * size, size), size)
    barred = jnp.broadcast_to(bias[pl.ds(i, 1), :], (QUERY_HEADS * size, HEAD_WIDTH))
    return jnp.concatenate(
        [heads_as_rows(received[source, :]), barred.astype(jnp.bfloat16)], axis=1
    )


def score(rows, keys, block_of):
    return lax.dot_general(
        rows, jnp.concatenate([keys, block_of], axis=1), (((1,), (1,)), ((), ())),
        preferred_element_type=jnp.float32,
    )


def weigh(scores, level):
    return jnp.exp2(scores * SCALE - level).astype(jnp.bfloat16)


def largest(sums, so_far):
    parts = sums[:, HEAD_WIDTH:]
    return jnp.maximum(so_far, jnp.max(parts.reshape(-1, 8, HEAD_WIDTH), axis=0))


def divided(sums, size):
    return heads_as_columns(sums[:, :HEAD_WIDTH] / sums[:, HEAD_WIDTH:], size).astype(jnp.bfloat16)


def heads_as_rows(block):
    return jnp.concatenate(
        [block[:, h * HEAD_WIDTH:(h + 1) * HEAD_WIDTH] for h in range(QUERY_HEADS)], axis=0
    )


def heads_as_columns(rows, size):
    return jnp.concatenate(
        [rows[h * size:(h + 1) * size] for h in range(QUERY_HEADS)], axis=1
    )


def own_kernel(
    order, bias_in, block_of, received, early, rest,
    out, state, level,
    stage, sem,
):
    bias = bias_in.at[0]
    blocks = bias.shape[0]
    tokens = (early.shape[0] + rest.shape[0]) // 2
    size = tokens // blocks
    group = QUERY_HEADS * size
    row = lax.rem(lax.broadcasted_iota(jnp.int32, (group, 2 * size), 0), size)
    lane = lax.broadcasted_iota(jnp.int32, (group, 2 * size), 1)

    work = []
    for i in range(blocks):
        width = (i // 2 + 1) * 2 * size
        spans = [(low, min(low + CHUNK, width)) for low in range(0, width, CHUNK)]
        for n, span in enumerate(spans[-1:] + spans[:-1]):
            work.append((i, span, n == 0, n == len(spans) - 1))

    rows = {}

    def start(i, span):
        if i not in rows:
            rows[i] = query_rows(received, order, bias, i, size)
        return score(rows[i], keys_of(early, rest, *span), block_of[span[0]:span[1], :])

    worst = jnp.zeros((8, HEAD_WIDTH), jnp.float32)
    copies = []
    scores = start(*work[0][:2])
    for n, (i, span, opening, closing) in enumerate(work):
        ahead = start(*work[n + 1][:2]) if n + 1 < len(work) else None
        if opening:
            cut = span[1] - span[0] - 2 * size
            tail = jnp.where(lane - (i % 2) * size > row, NEVER, scores[:, cut:])
            scores = jnp.concatenate([scores[:, :cut], tail], axis=1) if cut else tail
            top = jnp.max(scores, axis=1, keepdims=True) * SCALE
            weights = []
            width = span[1]
        weights.append(weigh(scores, top))
        if closing:
            ordered = weights[1:] + weights[:1]
            joined = jnp.concatenate(ordered, axis=1) if len(ordered) > 1 else ordered[0]
            sums = jnp.dot(
                joined, values_of(early, rest, 0, width), preferred_element_type=jnp.float32
            )
            worst = largest(sums, worst)
            where = slice(i * group, (i + 1) * group)
            held = slice(i * size, (i + 1) * size)
            state[where, :] = sums
            level[where, :] = jnp.broadcast_to(top, (group, HEAD_WIDTH))
            stage[held, :] = divided(sums, size)
            copy = pltpu.make_async_copy(stage.at[held], out.at[0, held], sem.at[i])
            copy.start()
            copies.append(copy)
        scores = ahead
    for copy in copies:
        copy.wait()

    @pl.when(jnp.logical_not(jnp.max(worst) < MOST))
    def _():
        def again(i, carry):
            where = pl.ds(pl.multiple_of(i * group, group), group)
            held = pl.ds(pl.multiple_of(i * size, size), size)
            scores = score(
                query_rows(received, order, bias, i, size),
                keys_of(early, rest, 0, tokens), block_of[...],
            )
            query = i * size + lax.rem(lax.broadcasted_iota(jnp.int32, scores.shape, 0), size)
            key = lax.broadcasted_iota(jnp.int32, scores.shape, 1)
            scores = jnp.where(key > query, NEVER, scores)
            top = jnp.max(scores, axis=1, keepdims=True) * SCALE
            sums = jnp.dot(
                weigh(scores, top), values_of(early, rest, 0, tokens),
                preferred_element_type=jnp.float32,
            )
            state[where, :] = sums
            level[where, :] = jnp.broadcast_to(top, (group, HEAD_WIDTH))
            stage[held, :] = divided(sums, size)
            copy = pltpu.make_async_copy(stage.at[held], out.at[0, held], sem.at[0])
            copy.start()
            copy.wait()
            return carry

        lax.fori_loop(0, blocks, again, 0)


def hop_kernel(
    offset, order, lengths, bias_in, block_of, received, early, rest,
    out_in, level_in, state_in, *refs,
):
    stage, sem = refs[-2:]
    out, level = refs[0], refs[1]
    place = lax.axis_index("ctx")
    bias = bias_in.at[offset]
    blocks = bias.shape[0]
    tokens = (early.shape[0] + rest.shape[0]) // 2
    size = tokens // blocks
    group = QUERY_HEADS * size
    reads, first = reach_of(lengths, place, offset, blocks)

    def over(low, together, final):
        def keep(i, sums):
            if offset < REACH:
                refs[2][pl.ds(pl.multiple_of(i * group, group), group), :] = sums
            if final:
                stage[pl.ds(pl.multiple_of(i * size, size), size), :] = divided(sums, size)

        spans = [(at, at + CHUNK) for at in range(low, tokens, CHUNK)]
        work = [(u, span) for u in range(together) for span in spans]

        def step(n, worst):
            i = n * together
            rows = {}

            def start(u, span):
                if u not in rows:
                    rows[u] = query_rows(received, order, bias, i + u, size)
                return score(rows[u], keys_of(early, rest, *span), block_of[span[0]:span[1], :])

            scores = start(*work[0])
            for m, (u, span) in enumerate(work):
                ahead = start(*work[m + 1]) if m + 1 < len(work) else None
                where = pl.ds(pl.multiple_of((i + u) * group, group), group)
                if span is spans[0]:
                    base = level_in[where, :]
                    base = jnp.concatenate([base] * (CHUNK // HEAD_WIDTH), axis=1)
                    weights = []
                weights.append(weigh(scores, base))
                if span is spans[-1]:
                    joined = jnp.concatenate(weights, axis=1) if len(weights) > 1 else weights[0]
                    sums = state_in[where, :] + jnp.dot(
                        joined, values_of(early, rest, low, tokens), preferred_element_type=jnp.float32
                    )
                    worst = jnp.where(i + u < reads, largest(sums, worst), worst)
                    keep(i + u, sums)
                scores = ahead
            if final:
                lax.fori_loop(i, jnp.minimum(i + together, reads), send, 0)
            return worst

        def copy_of(i):
            held = pl.ds(pl.multiple_of(i * size, size), size)
            return pltpu.make_async_copy(stage.at[held], out.at[0, held], sem)

        def send(i, carry):
            copy_of(i).start()
            return carry

        def finish(i, carry):
            copy_of(i).wait()
            return carry

        steps = pl.cdiv(reads, together)
        worst = lax.fori_loop(0, steps, step, jnp.zeros((8, HEAD_WIDTH), jnp.float32))
        if final:
            lax.fori_loop(0, reads, finish, 0)

        @pl.when(jnp.logical_not(jnp.max(worst) < MOST))
        def _():
            def again(i, carry):
                where = pl.ds(pl.multiple_of(i * group, group), group)
                scores = score(
                    query_rows(received, order, bias, i, size),
                    keys_of(early, rest, 0, tokens), block_of[...],
                )
                before = level_in[where, :]
                top = jnp.max(scores, axis=1, keepdims=True) * SCALE
                now = jnp.maximum(before, top)
                factor = jnp.exp2(before - now)
                sums = jnp.concatenate([factor, factor], axis=1) * state_in[where, :] + jnp.dot(
                    weigh(scores, now[:, :1]), values_of(early, rest, 0, tokens),
                    preferred_element_type=jnp.float32,
                )
                level[where, :] = now
                keep(i, sums)
                if final:
                    copy_of(i).start()
                    copy_of(i).wait()
                return carry

            lax.fori_loop(0, reads, again, 0)

    part = first // (blocks // 4)
    more = jnp.int32(0)
    if offset < REACH:
        more, _ = reach_of(lengths, place, offset + 1, blocks)
        pl.when((reads > 0) & (more > 0))(functools.partial(over, 0, 4, False))
    for n, together in enumerate((4, 4, 8, 8)):
        pl.when((reads > 0) & (more == 0) & (part == n))(
            functools.partial(over, n * (tokens // 4), together, True)
        )


def per_device(queries, keys, values, dest_replica, dest_slot, doc_lengths, tile_mask):
    tokens = queries.shape[1]
    width = queries.shape[2]
    blocks = dest_replica.shape[1]
    size = tokens // blocks
    packs = lax.axis_size("dp")
    cap = blocks // packs
    bf16, f32 = jnp.bfloat16, jnp.float32
    rows = tokens * QUERY_HEADS
    params = pltpu.CompilerParams(vmem_limit_bytes=VMEM_LIMIT)
    small = pltpu.CompilerParams(vmem_limit_bytes=VMEM_SMALL)

    def cost(flops, moved):
        return pl.CostEstimate(flops=flops, bytes_accessed=moved, transcendentals=0)

    def route(sent):
        return lax.all_to_all(sent, "dp", split_axis=0, concat_axis=0, tiled=True)

    dma = pltpu.SemaphoreType.DMA
    counts = pltpu.SMEM((packs,), jnp.int32)
    kv_send = pl.pallas_call(
        functools.partial(pack_kv_kernel, cap),
        out_shape=jax.ShapeDtypeStruct((packs, 2 * cap * size + SLOT_ROWS, HEAD_WIDTH), bf16),
        in_specs=[SMEM, SMEM, VMEM, VMEM],
        out_specs=VMEM,
        scratch_shapes=[counts, pltpu.SMEM((blocks,), jnp.int32)],
        cost_estimate=cost(0, 4 * tokens * HEAD_WIDTH * 2),
        name="pack_kv",
    )(dest_replica, dest_slot, keys, values)
    kv_recv = route(kv_send)
    q_send, bias, block_of = pl.pallas_call(
        functools.partial(pack_q_kernel, cap),
        out_shape=(
            jax.ShapeDtypeStruct((packs, cap * size, width), bf16),
            jax.ShapeDtypeStruct((REACH + 1, blocks, HEAD_WIDTH), f32),
            jax.ShapeDtypeStruct((tokens, HEAD_WIDTH), bf16),
        ),
        in_specs=[SMEM, SMEM, VMEM, VMEM],
        out_specs=(VMEM, VMEM, VMEM),
        scratch_shapes=[counts],
        compiler_params=small,
        cost_estimate=cost(0, 2 * tokens * width * 2),
        name="pack_q",
    )(dest_replica, doc_lengths, tile_mask, queries)
    q_recv = route(q_send).reshape(tokens, width)
    piece = tokens * PIECE // 4
    early, rest, order = pl.pallas_call(
        functools.partial(place_kernel, cap),
        out_shape=(
            jax.ShapeDtypeStruct((piece, HEAD_WIDTH), bf16),
            jax.ShapeDtypeStruct((2 * tokens - piece, HEAD_WIDTH), bf16),
            jax.ShapeDtypeStruct((1, blocks), jnp.int32),
        ),
        in_specs=[VMEM],
        out_specs=(VMEM, VMEM, SMEM),
        scratch_shapes=[pltpu.VMEM((2 * tokens, HEAD_WIDTH), bf16)],
        compiler_params=small,
        cost_estimate=cost(0, 4 * tokens * HEAD_WIDTH * 2),
        name="place_kv",
    )(kv_recv)

    out_shape = jax.ShapeDtypeStruct((1, tokens, width), bf16)
    level_shape = jax.ShapeDtypeStruct((rows, HEAD_WIDTH), f32)
    sums_shape = jax.ShapeDtypeStruct((rows, 2 * HEAD_WIDTH), f32)
    stage = pltpu.VMEM((tokens, width), bf16)

    def attend_back(offset, early, rest, out, level, sums):
        last = offset == REACH
        return pl.pallas_call(
            functools.partial(hop_kernel, offset),
            out_shape=(out_shape, level_shape) + (() if last else (sums_shape,)),
            in_specs=[SMEM, SMEM] + [VMEM] * 5 + [ANY, VMEM, VMEM],
            out_specs=(ANY, VMEM) + (() if last else (VMEM,)),
            scratch_shapes=[stage, dma],
            input_output_aliases={7: 0, 8: 1},
            compiler_params=params,
            cost_estimate=cost(2 * 2 * rows * tokens * HEAD_WIDTH, 8 * tokens * width),
            name=f"attend_back_{offset}",
        )(order, doc_lengths, bias, block_of, q_recv, early, rest, out, level, sums)

    back_early = shifted(early, "ctx")
    back_rest = shifted(rest, "ctx")
    out, sums, level = pl.pallas_call(
        own_kernel,
        out_shape=(out_shape, sums_shape, level_shape),
        in_specs=[SMEM] + [VMEM] * 5,
        out_specs=(ANY, VMEM, VMEM),
        scratch_shapes=[stage, dma((blocks,))],
        compiler_params=params,
        cost_estimate=cost(2 * rows * tokens * HEAD_WIDTH, 8 * tokens * width),
        name="attend_own",
    )(order, bias, block_of, q_recv, early, rest)
    far_rest, out, sums, level = lax.optimization_barrier((back_rest, out, sums, level))
    far_early = shifted(back_early, "ctx")
    far_rest = shifted(far_rest, "ctx")
    out, level, sums = attend_back(1, back_early, back_rest, out, level, sums)
    return attend_back(2, far_early, far_rest, out, level, sums)[0]


def solution(mesh):
    return jax.shard_map(
        per_device,
        mesh=mesh,
        in_specs=(
            P("dp", "ctx", None),
            P("dp", "ctx", None),
            P("dp", "ctx", None),
            P("dp", "ctx"),
            P("dp", "ctx"),
            P("dp", None),
            P("dp", "ctx", None),
        ),
        out_specs=P("dp", "ctx", None),
        check_vma=False,
    )
```

```python
import functools

import jax
import jax.numpy as jnp
from jax import lax
from jax.experimental import pallas as pl
from jax.experimental.pallas import tpu as pltpu
from jax.sharding import PartitionSpec as P

HEAD_WIDTH = 128
QUERY_HEADS = 4
SCALE = HEAD_WIDTH ** (-0.5) * 1.4426950408889634
NEVER = -1e30
MOST = 1e30
CHUNK = 256
SLOT_ROWS = 16
REACH = 2
PIECE = 4
VMEM_LIMIT = 32 * 1024 * 1024
VMEM_SMALL = 8 * 1024 * 1024

ANY = pl.BlockSpec(memory_space=pl.ANY)
SMEM = pl.BlockSpec(memory_space=pltpu.SMEM)
VMEM = pl.BlockSpec(memory_space=pltpu.VMEM)


def shifted(value, axis):
    count = lax.axis_size(axis)
    return lax.ppermute(value, axis, [(source, source + 1) for source in range(count - 1)])


def pack_kv_kernel(cap, targets, slots, keys, values, send, counts, slot_of):
    packs = send.shape[0]
    blocks = targets.shape[1]
    size = keys.shape[1] // blocks
    half = cap * size
    for t in range(packs):
        counts[t] = 0
    for j in range(blocks):
        t = targets[0, j]
        rank = counts[t]
        counts[t] = rank + 1
        slot_of[t * cap + rank] = lax.rem(slots[0, j], blocks)
        rows = slice(j * size, (j + 1) * size)
        to = pl.multiple_of(rank * size, size)
        send[t, pl.ds(to, size), :] = keys[0, rows, :]
        send[t, pl.ds(to + half, size), :] = values[0, rows, :]
    row = lax.broadcasted_iota(jnp.int32, (SLOT_ROWS, HEAD_WIDTH), 0)
    for t in range(packs):
        listed = jnp.zeros(row.shape, jnp.int32)
        for i in range(cap):
            listed = jnp.where(row == i, slot_of[t * cap + i], listed)
        send[t, 2 * half:, :] = listed.astype(jnp.float32).astype(jnp.bfloat16)


def pack_q_kernel(cap, targets, lengths, tiles, queries, send, bias, block_of, counts):
    packs = send.shape[0]
    blocks = targets.shape[1]
    tokens = queries.shape[1]
    size = tokens // blocks
    place = lax.axis_index("ctx")
    for t in range(packs):
        counts[t] = 0
    for j in range(blocks):
        t = targets[0, j]
        rank = counts[t]
        counts[t] = rank + 1
        to = pl.multiple_of(rank * size, size)
        send[t, pl.ds(to, size), :] = queries[0, j * size:(j + 1) * size, :]

    block = lax.broadcasted_iota(jnp.int32, (tokens, HEAD_WIDTH), 1)
    of_key = lax.broadcasted_iota(jnp.int32, (tokens, HEAD_WIDTH), 0) // size
    block_of[...] = (block == of_key).astype(jnp.float32).astype(jnp.bfloat16)
    query_block = place * blocks + lax.broadcasted_iota(jnp.int32, (blocks, 1), 0)
    listed_tiles = tiles[0].astype(jnp.float32).astype(jnp.bfloat16)
    for offset in range(bias.shape[0]):
        low = (place - offset) * blocks
        key_block = low + lax.broadcasted_iota(jnp.int32, (1, HEAD_WIDTH), 1)
        key_doc = jnp.zeros((1, HEAD_WIDTH), jnp.int32)
        query_doc = jnp.zeros((blocks, 1), jnp.int32)
        end = jnp.int32(0)
        for j in range(lengths.shape[1]):
            end = end + lengths[0, j]
            key_doc = key_doc + (key_block >= end).astype(jnp.int32)
            query_doc = query_doc + (query_block >= end).astype(jnp.int32)
        spread = lax.broadcasted_iota(jnp.int32, (tiles.shape[2], HEAD_WIDTH), 0) == key_block
        listed = jnp.dot(
            listed_tiles, spread.astype(jnp.float32).astype(jnp.bfloat16),
            preferred_element_type=jnp.float32,
        )
        allowed = (query_doc == key_doc) & (key_block <= query_block) & (key_block >= 0)
        allowed = allowed & ((listed > 0.5) | (key_block == query_block))
        bias[offset] = jnp.where(allowed, 0.0, NEVER)


def place_kernel(cap, received, early, rest, order, placed):
    packs = received.shape[0]
    tokens = placed.shape[0] // 2
    size = tokens // (packs * cap)
    half = cap * size
    for s in range(packs):
        listed = received[s, 2 * half:, :].astype(jnp.float32).astype(jnp.int32)
        for i in range(cap):
            slot = listed[i, 0]
            order[0, slot] = s * cap + i
            to = pl.multiple_of(slot * size, size)
            placed[pl.ds(to, size), :] = received[s, i * size:(i + 1) * size, :]
            placed[pl.ds(to + tokens, size), :] = (
                received[s, half + i * size:half + (i + 1) * size, :]
            )
    early[...] = placed[:early.shape[0], :]
    rest[...] = placed[early.shape[0]:, :]


def first_document(lengths, position):
    start, end = jnp.int32(0), jnp.int32(0)
    total = jnp.int32(0)
    for j in range(lengths.shape[1]):
        after = total + lengths[0, j]
        inside = (total <= position) & (position < after)
        start = jnp.where(inside, total, start)
        end = jnp.where(inside, after, end)
        total = after
    return start, end


def reach_of(lengths, place, offset, blocks):
    start, end = first_document(lengths, place * blocks)
    low = (place - offset) * blocks
    rows = jnp.where(start < low + blocks, jnp.minimum(end - place * blocks, blocks), 0)
    return jnp.where(low >= 0, rows, 0), jnp.maximum(start - low, 0)


def keys_of(early, rest, low, high):
    half = early.shape[0]
    if high <= half:
        return early[low:high, :]
    if low >= half:
        return rest[low - half:high - half, :]
    return jnp.concatenate([early[low:, :], rest[:high - half, :]], axis=0)


def values_of(early, rest, low, high):
    values = (early.shape[0] + rest.shape[0]) // 2 - early.shape[0]
    return beside_ones(rest[values + low:values + high, :])


def beside_ones(values):
    return jnp.concatenate([values, jnp.ones(values.shape, values.dtype)], axis=1)


def query_rows(received, order, bias, i, size):
    source = pl.ds(pl.multiple_of(order[0, i] * size, size), size)
    barred = jnp.broadcast_to(bias[pl.ds(i, 1), :], (QUERY_HEADS * size, HEAD_WIDTH))
    return jnp.concatenate(
        [heads_as_rows(received[source, :]), barred.astype(jnp.bfloat16)], axis=1
    )


def score(rows, keys, block_of):
    return lax.dot_general(
        rows, jnp.concatenate([keys, block_of], axis=1), (((1,), (1,)), ((), ())),
        preferred_element_type=jnp.float32,
    )


def weigh(scores, level):
    return jnp.exp2(scores * SCALE - level).astype(jnp.bfloat16)


def largest(sums, so_far):
    parts = sums[:, HEAD_WIDTH:]
    return jnp.maximum(so_far, jnp.max(parts.reshape(-1, 8, HEAD_WIDTH), axis=0))


def divided(sums, size):
    return heads_as_columns(sums[:, :HEAD_WIDTH] / sums[:, HEAD_WIDTH:], size).astype(jnp.bfloat16)


def heads_as_rows(block):
    return jnp.concatenate(
        [block[:, h * HEAD_WIDTH:(h + 1) * HEAD_WIDTH] for h in range(QUERY_HEADS)], axis=0
    )


def heads_as_columns(rows, size):
    return jnp.concatenate(
        [rows[h * size:(h + 1) * size] for h in range(QUERY_HEADS)], axis=1
    )


def own_kernel(
    order, bias_in, block_of, received, early, rest,
    out, state, level,
    stage, sem,
):
    bias = bias_in.at[0]
    blocks = bias.shape[0]
    tokens = (early.shape[0] + rest.shape[0]) // 2
    size = tokens // blocks
    group = QUERY_HEADS * size
    row = lax.rem(lax.broadcasted_iota(jnp.int32, (group, 2 * size), 0), size)
    lane = lax.broadcasted_iota(jnp.int32, (group, 2 * size), 1)

    work = []
    for i in range(blocks):
        width = (i // 2 + 1) * 2 * size
        spans = [(low, min(low + CHUNK, width)) for low in range(0, width, CHUNK)]
        for n, span in enumerate(spans[-1:] + spans[:-1]):
            work.append((i, span, n == 0, n == len(spans) - 1))

    rows = {}

    def start(i, span):
        if i not in rows:
            rows[i] = query_rows(received, order, bias, i, size)
        return score(rows[i], keys_of(early, rest, *span), block_of[span[0]:span[1], :])

    worst = jnp.zeros((8, HEAD_WIDTH), jnp.float32)
    copies = []
    scores = start(*work[0][:2])
    for n, (i, span, opening, closing) in enumerate(work):
        ahead = start(*work[n + 1][:2]) if n + 1 < len(work) else None
        if opening:
            cut = span[1] - span[0] - 2 * size
            tail = jnp.where(lane - (i % 2) * size > row, NEVER, scores[:, cut:])
            scores = jnp.concatenate([scores[:, :cut], tail], axis=1) if cut else tail
            top = jnp.max(scores, axis=1, keepdims=True) * SCALE
            weights = []
            width = span[1]
        weights.append(weigh(scores, top))
        if closing:
            ordered = weights[1:] + weights[:1]
            joined = jnp.concatenate(ordered, axis=1) if len(ordered) > 1 else ordered[0]
            sums = jnp.dot(
                joined, values_of(early, rest, 0, width), preferred_element_type=jnp.float32
            )
            worst = largest(sums, worst)
            where = slice(i * group, (i + 1) * group)
            held = slice(i * size, (i + 1) * size)
            state[where, :] = sums
            level[where, :] = jnp.broadcast_to(top, (group, HEAD_WIDTH))
            stage[held, :] = divided(sums, size)
            copy = pltpu.make_async_copy(stage.at[held], out.at[0, held], sem.at[i])
            copy.start()
            copies.append(copy)
        scores = ahead
    for copy in copies:
        copy.wait()

    @pl.when(jnp.logical_not(jnp.max(worst) < MOST))
    def _():
        def again(i, carry):
            where = pl.ds(pl.multiple_of(i * group, group), group)
            held = pl.ds(pl.multiple_of(i * size, size), size)
            scores = score(
                query_rows(received, order, bias, i, size),
                keys_of(early, rest, 0, tokens), block_of[...],
            )
            query = i * size + lax.rem(lax.broadcasted_iota(jnp.int32, scores.shape, 0), size)
            key = lax.broadcasted_iota(jnp.int32, scores.shape, 1)
            scores = jnp.where(key > query, NEVER, scores)
            top = jnp.max(scores, axis=1, keepdims=True) * SCALE
            sums = jnp.dot(
                weigh(scores, top), values_of(early, rest, 0, tokens),
                preferred_element_type=jnp.float32,
            )
            state[where, :] = sums
            level[where, :] = jnp.broadcast_to(top, (group, HEAD_WIDTH))
            stage[held, :] = divided(sums, size)
            copy = pltpu.make_async_copy(stage.at[held], out.at[0, held], sem.at[0])
            copy.start()
            copy.wait()
            return carry

        lax.fori_loop(0, blocks, again, 0)


def hop_kernel(
    offset, order, lengths, bias_in, block_of, received, early, rest,
    out_in, level_in, state_in, *refs,
):
    stage, sem = refs[-2:]
    out, level = refs[0], refs[1]
    place = lax.axis_index("ctx")
    bias = bias_in.at[offset]
    blocks = bias.shape[0]
    tokens = (early.shape[0] + rest.shape[0]) // 2
    size = tokens // blocks
    group = QUERY_HEADS * size
    reads, first = reach_of(lengths, place, offset, blocks)

    def over(low, together, final):
        def keep(i, sums):
            if offset < REACH:
                refs[2][pl.ds(pl.multiple_of(i * group, group), group), :] = sums
            if final:
                stage[pl.ds(pl.multiple_of(i * size, size), size), :] = divided(sums, size)

        spans = [(at, at + CHUNK) for at in range(low, tokens, CHUNK)]
        work = [(u, span) for u in range(together) for span in spans]

        def opening(i):
            rows = query_rows(received, order, bias, jnp.minimum(i, blocks - 1), size)
            return score(rows, keys_of(early, rest, *spans[0]), block_of[low:low + CHUNK, :])

        def step(n, carry):
            worst, scores = carry
            i = n * together
            rows = {}

            def start(u, span):
                if u not in rows:
                    rows[u] = query_rows(received, order, bias, i + u, size)
                return score(rows[u], keys_of(early, rest, *span), block_of[span[0]:span[1], :])

            for m, (u, span) in enumerate(work):
                last = m + 1 == len(work)
                ahead = opening(i + together) if last else start(*work[m + 1])
                where = pl.ds(pl.multiple_of((i + u) * group, group), group)
                if span is spans[0]:
                    base = level_in[where, :]
                    base = jnp.concatenate([base] * (CHUNK // HEAD_WIDTH), axis=1)
                    weights = []
                weights.append(weigh(scores, base))
                if span is spans[-1]:
                    joined = jnp.concatenate(weights, axis=1) if len(weights) > 1 else weights[0]
                    sums = state_in[where, :] + jnp.dot(
                        joined, values_of(early, rest, low, tokens), preferred_element_type=jnp.float32
                    )
                    worst = jnp.where(i + u < reads, largest(sums, worst), worst)
                    keep(i + u, sums)
                scores = ahead
            if final:
                lax.fori_loop(i, jnp.minimum(i + together, reads), send, 0)
            return worst, scores

        def copy_of(i):
            held = pl.ds(pl.multiple_of(i * size, size), size)
            return pltpu.make_async_copy(stage.at[held], out.at[0, held], sem)

        def send(i, carry):
            copy_of(i).start()
            return carry

        def finish(i, carry):
            copy_of(i).wait()
            return carry

        steps = pl.cdiv(reads, together)
        worst = jnp.zeros((8, HEAD_WIDTH), jnp.float32)
        worst, _ = lax.fori_loop(0, steps, step, (worst, opening(0)))
        if final:
            lax.fori_loop(0, reads, finish, 0)

        @pl.when(jnp.logical_not(jnp.max(worst) < MOST))
        def _():
            def again(i, carry):
                where = pl.ds(pl.multiple_of(i * group, group), group)
                scores = score(
                    query_rows(received, order, bias, i, size),
                    keys_of(early, rest, 0, tokens), block_of[...],
                )
                before = level_in[where, :]
                top = jnp.max(scores, axis=1, keepdims=True) * SCALE
                now = jnp.maximum(before, top)
                factor = jnp.exp2(before - now)
                sums = jnp.concatenate([factor, factor], axis=1) * state_in[where, :] + jnp.dot(
                    weigh(scores, now[:, :1]), values_of(early, rest, 0, tokens),
                    preferred_element_type=jnp.float32,
                )
                level[where, :] = now
                keep(i, sums)
                if final:
                    copy_of(i).start()
                    copy_of(i).wait()
                return carry

            lax.fori_loop(0, reads, again, 0)

    part = first // (blocks // 4)
    more = jnp.int32(0)
    if offset < REACH:
        more, _ = reach_of(lengths, place, offset + 1, blocks)
        pl.when((reads > 0) & (more > 0))(functools.partial(over, 0, 4, False))
    for n, together in enumerate((4, 4, 8, 8)):
        pl.when((reads > 0) & (more == 0) & (part == n))(
            functools.partial(over, n * (tokens // 4), together, True)
        )


def near_kernel(
    order, lengths, bias, block_of, received, early, rest, back_early, back_rest,
    out, level, sums,
    stage, state, sems, sem,
):
    own_kernel(
        order, bias, block_of, received, early, rest, out, state, level, stage, sems
    )
    hop_kernel(
        1, order, lengths, bias, block_of, received, back_early, back_rest,
        out, level, state, out, level, sums, stage, sem,
    )


def per_device(queries, keys, values, dest_replica, dest_slot, doc_lengths, tile_mask):
    tokens = queries.shape[1]
    width = queries.shape[2]
    blocks = dest_replica.shape[1]
    size = tokens // blocks
    packs = lax.axis_size("dp")
    cap = blocks // packs
    bf16, f32 = jnp.bfloat16, jnp.float32
    rows = tokens * QUERY_HEADS
    params = pltpu.CompilerParams(vmem_limit_bytes=VMEM_LIMIT)
    small = pltpu.CompilerParams(vmem_limit_bytes=VMEM_SMALL)

    def cost(flops, moved):
        return pl.CostEstimate(flops=flops, bytes_accessed=moved, transcendentals=0)

    def route(sent):
        return lax.all_to_all(sent, "dp", split_axis=0, concat_axis=0, tiled=True)

    dma = pltpu.SemaphoreType.DMA
    counts = pltpu.SMEM((packs,), jnp.int32)
    kv_send = pl.pallas_call(
        functools.partial(pack_kv_kernel, cap),
        out_shape=jax.ShapeDtypeStruct((packs, 2 * cap * size + SLOT_ROWS, HEAD_WIDTH), bf16),
        in_specs=[SMEM, SMEM, VMEM, VMEM],
        out_specs=VMEM,
        scratch_shapes=[counts, pltpu.SMEM((blocks,), jnp.int32)],
        cost_estimate=cost(0, 4 * tokens * HEAD_WIDTH * 2),
        name="pack_kv",
    )(dest_replica, dest_slot, keys, values)
    kv_recv = route(kv_send)
    q_send, bias, block_of = pl.pallas_call(
        functools.partial(pack_q_kernel, cap),
        out_shape=(
            jax.ShapeDtypeStruct((packs, cap * size, width), bf16),
            jax.ShapeDtypeStruct((REACH + 1, blocks, HEAD_WIDTH), f32),
            jax.ShapeDtypeStruct((tokens, HEAD_WIDTH), bf16),
        ),
        in_specs=[SMEM, SMEM, VMEM, VMEM],
        out_specs=(VMEM, VMEM, VMEM),
        scratch_shapes=[counts],
        compiler_params=small,
        cost_estimate=cost(0, 2 * tokens * width * 2),
        name="pack_q",
    )(dest_replica, doc_lengths, tile_mask, queries)
    q_recv = route(q_send).reshape(tokens, width)
    piece = tokens * PIECE // 4
    early, rest, order = pl.pallas_call(
        functools.partial(place_kernel, cap),
        out_shape=(
            jax.ShapeDtypeStruct((piece, HEAD_WIDTH), bf16),
            jax.ShapeDtypeStruct((2 * tokens - piece, HEAD_WIDTH), bf16),
            jax.ShapeDtypeStruct((1, blocks), jnp.int32),
        ),
        in_specs=[VMEM],
        out_specs=(VMEM, VMEM, SMEM),
        scratch_shapes=[pltpu.VMEM((2 * tokens, HEAD_WIDTH), bf16)],
        compiler_params=small,
        cost_estimate=cost(0, 4 * tokens * HEAD_WIDTH * 2),
        name="place_kv",
    )(kv_recv)

    out_shape = jax.ShapeDtypeStruct((1, tokens, width), bf16)
    level_shape = jax.ShapeDtypeStruct((rows, HEAD_WIDTH), f32)
    sums_shape = jax.ShapeDtypeStruct((rows, 2 * HEAD_WIDTH), f32)
    stage = pltpu.VMEM((tokens, width), bf16)

    back_early = shifted(early, "ctx")
    back_rest = shifted(rest, "ctx")
    far_early = shifted(back_early, "ctx")
    far_rest = shifted(back_rest, "ctx")
    out, level, sums = pl.pallas_call(
        near_kernel,
        out_shape=(out_shape, level_shape, sums_shape),
        in_specs=[SMEM, SMEM] + [VMEM] * 7,
        out_specs=(ANY, VMEM, VMEM),
        scratch_shapes=[stage, pltpu.VMEM(sums_shape.shape, f32), dma((blocks,)), dma],
        compiler_params=params,
        cost_estimate=cost(2 * 3 * rows * tokens * HEAD_WIDTH, 8 * tokens * width),
        name="attend_near",
    )(order, doc_lengths, bias, block_of, q_recv, early, rest, back_early, back_rest)
    return pl.pallas_call(
        functools.partial(hop_kernel, REACH),
        out_shape=(out_shape, level_shape),
        in_specs=[SMEM, SMEM] + [VMEM] * 5 + [ANY, VMEM, VMEM],
        out_specs=(ANY, VMEM),
        scratch_shapes=[stage, dma],
        input_output_aliases={7: 0, 8: 1},
        compiler_params=params,
        cost_estimate=cost(2 * 2 * rows * tokens * HEAD_WIDTH, 8 * tokens * width),
        name="attend_far",
    )(order, doc_lengths, bias, block_of, q_recv, far_early, far_rest, out, level, sums)[0]


def solution(mesh):
    return jax.shard_map(
        per_device,
        mesh=mesh,
        in_specs=(
            P("dp", "ctx", None),
            P("dp", "ctx", None),
            P("dp", "ctx", None),
            P("dp", "ctx"),
            P("dp", "ctx"),
            P("dp", None),
            P("dp", "ctx", None),
        ),
        out_specs=P("dp", "ctx", None),
        check_vma=False,
    )
```

```python
import functools

import jax
import jax.numpy as jnp
from jax import lax
from jax.experimental import pallas as pl
from jax.experimental.pallas import tpu as pltpu
from jax.sharding import PartitionSpec as P

HEAD_WIDTH = 128
QUERY_HEADS = 4
SCALE = HEAD_WIDTH ** (-0.5) * 1.4426950408889634
NEVER = -1e30
MOST = 1e30
CHUNK = 256
SLOT_ROWS = 16
REACH = 2
PIECE = 4
VMEM_LIMIT = 32 * 1024 * 1024
VMEM_SMALL = 8 * 1024 * 1024

ANY = pl.BlockSpec(memory_space=pl.ANY)
SMEM = pl.BlockSpec(memory_space=pltpu.SMEM)
VMEM = pl.BlockSpec(memory_space=pltpu.VMEM)


def shifted(value, axis):
    count = lax.axis_size(axis)
    return lax.ppermute(value, axis, [(source, source + 1) for source in range(count - 1)])


def pack_kv_kernel(cap, targets, slots, keys, values, send, counts, slot_of):
    packs = send.shape[0]
    blocks = targets.shape[1]
    size = keys.shape[1] // blocks
    half = cap * size
    for t in range(packs):
        counts[t] = 0
    for j in range(blocks):
        t = targets[0, j]
        rank = counts[t]
        counts[t] = rank + 1
        slot_of[t * cap + rank] = lax.rem(slots[0, j], blocks)
        rows = slice(j * size, (j + 1) * size)
        to = pl.multiple_of(rank * size, size)
        send[t, pl.ds(to, size), :] = keys[0, rows, :]
        send[t, pl.ds(to + half, size), :] = values[0, rows, :]
    row = lax.broadcasted_iota(jnp.int32, (SLOT_ROWS, HEAD_WIDTH), 0)
    for t in range(packs):
        listed = jnp.zeros(row.shape, jnp.int32)
        for i in range(cap):
            listed = jnp.where(row == i, slot_of[t * cap + i], listed)
        send[t, 2 * half:, :] = listed.astype(jnp.float32).astype(jnp.bfloat16)


def pack_q_kernel(cap, targets, lengths, tiles, queries, send, bias, block_of, counts):
    packs = send.shape[0]
    blocks = targets.shape[1]
    tokens = queries.shape[1]
    size = tokens // blocks
    place = lax.axis_index("ctx")
    for t in range(packs):
        counts[t] = 0
    for j in range(blocks):
        t = targets[0, j]
        rank = counts[t]
        counts[t] = rank + 1
        to = pl.multiple_of(rank * size, size)
        send[t, pl.ds(to, size), :] = queries[0, j * size:(j + 1) * size, :]

    block = lax.broadcasted_iota(jnp.int32, (tokens, HEAD_WIDTH), 1)
    of_key = lax.broadcasted_iota(jnp.int32, (tokens, HEAD_WIDTH), 0) // size
    block_of[...] = (block == of_key).astype(jnp.float32).astype(jnp.bfloat16)
    query_block = place * blocks + lax.broadcasted_iota(jnp.int32, (blocks, 1), 0)
    listed_tiles = tiles[0].astype(jnp.float32).astype(jnp.bfloat16)
    for offset in range(bias.shape[0]):
        low = (place - offset) * blocks
        key_block = low + lax.broadcasted_iota(jnp.int32, (1, HEAD_WIDTH), 1)
        key_doc = jnp.zeros((1, HEAD_WIDTH), jnp.int32)
        query_doc = jnp.zeros((blocks, 1), jnp.int32)
        end = jnp.int32(0)
        for j in range(lengths.shape[1]):
            end = end + lengths[0, j]
            key_doc = key_doc + (key_block >= end).astype(jnp.int32)
            query_doc = query_doc + (query_block >= end).astype(jnp.int32)
        spread = lax.broadcasted_iota(jnp.int32, (tiles.shape[2], HEAD_WIDTH), 0) == key_block
        listed = jnp.dot(
            listed_tiles, spread.astype(jnp.float32).astype(jnp.bfloat16),
            preferred_element_type=jnp.float32,
        )
        allowed = (query_doc == key_doc) & (key_block <= query_block) & (key_block >= 0)
        allowed = allowed & ((listed > 0.5) | (key_block == query_block))
        bias[offset] = jnp.where(allowed, 0.0, NEVER)


def place_kernel(cap, received, early, rest, order, placed):
    packs = received.shape[0]
    tokens = placed.shape[0] // 2
    size = tokens // (packs * cap)
    half = cap * size
    for s in range(packs):
        listed = received[s, 2 * half:, :].astype(jnp.float32).astype(jnp.int32)
        for i in range(cap):
            slot = listed[i, 0]
            order[0, slot] = s * cap + i
            to = pl.multiple_of(slot * size, size)
            placed[pl.ds(to, size), :] = received[s, i * size:(i + 1) * size, :]
            placed[pl.ds(to + tokens, size), :] = (
                received[s, half + i * size:half + (i + 1) * size, :]
            )
    early[...] = placed[:early.shape[0], :]
    rest[...] = placed[early.shape[0]:, :]


def first_document(lengths, position):
    start, end = jnp.int32(0), jnp.int32(0)
    total = jnp.int32(0)
    for j in range(lengths.shape[1]):
        after = total + lengths[0, j]
        inside = (total <= position) & (position < after)
        start = jnp.where(inside, total, start)
        end = jnp.where(inside, after, end)
        total = after
    return start, end


def reach_of(lengths, place, offset, blocks):
    start, end = first_document(lengths, place * blocks)
    low = (place - offset) * blocks
    rows = jnp.where(start < low + blocks, jnp.minimum(end - place * blocks, blocks), 0)
    return jnp.where(low >= 0, rows, 0), jnp.maximum(start - low, 0)


def keys_of(early, rest, low, high):
    half = early.shape[0]
    if high <= half:
        return early[low:high, :]
    if low >= half:
        return rest[low - half:high - half, :]
    return jnp.concatenate([early[low:, :], rest[:high - half, :]], axis=0)


def values_of(early, rest, low, high):
    values = (early.shape[0] + rest.shape[0]) // 2 - early.shape[0]
    return beside_ones(rest[values + low:values + high, :])


def beside_ones(values):
    return jnp.concatenate([values, jnp.ones(values.shape, values.dtype)], axis=1)


def query_rows(received, order, bias, i, size):
    source = pl.ds(pl.multiple_of(order[0, i] * size, size), size)
    barred = jnp.broadcast_to(bias[pl.ds(i, 1), :], (QUERY_HEADS * size, HEAD_WIDTH))
    return jnp.concatenate(
        [heads_as_rows(received[source, :]), barred.astype(jnp.bfloat16)], axis=1
    )


def pair_rows(received, order, bias, i, size):
    return jnp.concatenate(
        [query_rows(received, order, bias, i + u, size) for u in range(2)], axis=0
    )


def score(rows, keys, block_of):
    return lax.dot_general(
        rows, jnp.concatenate([keys, block_of], axis=1), (((1,), (1,)), ((), ())),
        preferred_element_type=jnp.float32,
    )


def weigh(scores, level):
    return jnp.exp2(scores * SCALE - level).astype(jnp.bfloat16)


def largest(sums, so_far):
    parts = sums[:, HEAD_WIDTH:]
    return jnp.maximum(so_far, jnp.max(parts.reshape(-1, 8, HEAD_WIDTH), axis=0))


def divided(sums, size):
    ratio = sums[:, :HEAD_WIDTH] / sums[:, HEAD_WIDTH:]
    group = QUERY_HEADS * size
    return jnp.concatenate(
        [heads_as_columns(ratio[u:u + group], size) for u in range(0, ratio.shape[0], group)],
        axis=0,
    ).astype(jnp.bfloat16)


def heads_as_rows(block):
    return jnp.concatenate(
        [block[:, h * HEAD_WIDTH:(h + 1) * HEAD_WIDTH] for h in range(QUERY_HEADS)], axis=0
    )


def heads_as_columns(rows, size):
    return jnp.concatenate(
        [rows[h * size:(h + 1) * size] for h in range(QUERY_HEADS)], axis=1
    )


def own_kernel(
    order, bias_in, block_of, received, early, rest,
    out, state, level,
    stage, sem,
):
    bias = bias_in.at[0]
    blocks = bias.shape[0]
    tokens = (early.shape[0] + rest.shape[0]) // 2
    size = tokens // blocks
    group = QUERY_HEADS * size
    row = lax.broadcasted_iota(jnp.int32, (2 * group, 2 * size), 0)
    lane = lax.broadcasted_iota(jnp.int32, (2 * group, 2 * size), 1)
    later = lane - (row // group) * size > lax.rem(row, size)

    work = []
    for i in range(0, blocks, 2):
        width = (i + 2) * size
        spans = [(low, min(low + CHUNK, width)) for low in range(0, width, CHUNK)]
        for n, span in enumerate(spans[-1:] + spans[:-1]):
            work.append((i, span, n == 0, n == len(spans) - 1))

    rows = {}

    def start(i, span):
        if i not in rows:
            rows[i] = pair_rows(received, order, bias, i, size)
        return score(rows[i], keys_of(early, rest, *span), block_of[span[0]:span[1], :])

    worst = jnp.zeros((8, HEAD_WIDTH), jnp.float32)
    copies = []
    scores = start(*work[0][:2])
    for n, (i, span, opening, closing) in enumerate(work):
        ahead = start(*work[n + 1][:2]) if n + 1 < len(work) else None
        if opening:
            cut = span[1] - span[0] - 2 * size
            tail = jnp.where(later, NEVER, scores[:, cut:])
            scores = jnp.concatenate([scores[:, :cut], tail], axis=1) if cut else tail
            top = jnp.max(scores, axis=1, keepdims=True) * SCALE
            weights = []
            width = span[1]
        weights.append(weigh(scores, top))
        if closing:
            ordered = weights[1:] + weights[:1]
            joined = jnp.concatenate(ordered, axis=1) if len(ordered) > 1 else ordered[0]
            sums = jnp.dot(
                joined, values_of(early, rest, 0, width), preferred_element_type=jnp.float32
            )
            worst = largest(sums, worst)
            where = slice(i * group, (i + 2) * group)
            held = slice(i * size, (i + 2) * size)
            state[where, :] = sums
            level[where, :] = jnp.broadcast_to(top, (2 * group, HEAD_WIDTH))
            stage[held, :] = divided(sums, size)
            copy = pltpu.make_async_copy(stage.at[held], out.at[0, held], sem.at[i])
            copy.start()
            copies.append(copy)
        scores = ahead
    for copy in copies:
        copy.wait()

    @pl.when(jnp.logical_not(jnp.max(worst) < MOST))
    def _():
        def again(i, carry):
            where = pl.ds(pl.multiple_of(i * group, group), group)
            held = pl.ds(pl.multiple_of(i * size, size), size)
            scores = score(
                query_rows(received, order, bias, i, size),
                keys_of(early, rest, 0, tokens), block_of[...],
            )
            query = i * size + lax.rem(lax.broadcasted_iota(jnp.int32, scores.shape, 0), size)
            key = lax.broadcasted_iota(jnp.int32, scores.shape, 1)
            scores = jnp.where(key > query, NEVER, scores)
            top = jnp.max(scores, axis=1, keepdims=True) * SCALE
            sums = jnp.dot(
                weigh(scores, top), values_of(early, rest, 0, tokens),
                preferred_element_type=jnp.float32,
            )
            state[where, :] = sums
            level[where, :] = jnp.broadcast_to(top, (group, HEAD_WIDTH))
            stage[held, :] = divided(sums, size)
            copy = pltpu.make_async_copy(stage.at[held], out.at[0, held], sem.at[0])
            copy.start()
            copy.wait()
            return carry

        lax.fori_loop(0, blocks, again, 0)


def hop_kernel(
    offset, order, lengths, bias_in, block_of, received, early, rest,
    out_in, level_in, state_in, *refs,
):
    stage, sem = refs[-2:]
    out, level = refs[0], refs[1]
    place = lax.axis_index("ctx")
    bias = bias_in.at[offset]
    blocks = bias.shape[0]
    tokens = (early.shape[0] + rest.shape[0]) // 2
    size = tokens // blocks
    group = QUERY_HEADS * size
    reads, first = reach_of(lengths, place, offset, blocks)

    def over(low, together, final):
        def keep(i, sums):
            count = sums.shape[0]
            if offset < REACH:
                refs[2][pl.ds(pl.multiple_of(i * group, group), count), :] = sums
            if final:
                held = pl.ds(pl.multiple_of(i * size, size), count // QUERY_HEADS)
                stage[held, :] = divided(sums, size)

        spans = [(at, at + CHUNK) for at in range(low, tokens, CHUNK)]
        work = [(u, span) for u in range(0, together, 2) for span in spans]

        def step(n, worst):
            i = n * together
            rows = {}

            def start(u, span):
                if u not in rows:
                    rows[u] = pair_rows(received, order, bias, i + u, size)
                return score(rows[u], keys_of(early, rest, *span), block_of[span[0]:span[1], :])

            scores = start(*work[0])
            for m, (u, span) in enumerate(work):
                ahead = start(*work[m + 1]) if m + 1 < len(work) else None
                where = pl.ds(pl.multiple_of((i + u) * group, group), 2 * group)
                if span is spans[0]:
                    base = level_in[where, :]
                    base = jnp.concatenate([base] * (CHUNK // HEAD_WIDTH), axis=1)
                    weights = []
                weights.append(weigh(scores, base))
                if span is spans[-1]:
                    joined = jnp.concatenate(weights, axis=1) if len(weights) > 1 else weights[0]
                    sums = state_in[where, :] + jnp.dot(
                        joined, values_of(early, rest, low, tokens), preferred_element_type=jnp.float32
                    )
                    worst = jnp.where(i + u < reads, largest(sums, worst), worst)
                    keep(i + u, sums)
                scores = ahead
            if final:
                lax.fori_loop(i, jnp.minimum(i + together, reads), send, 0)
            return worst

        def copy_of(i):
            held = pl.ds(pl.multiple_of(i * size, size), size)
            return pltpu.make_async_copy(stage.at[held], out.at[0, held], sem)

        def send(i, carry):
            copy_of(i).start()
            return carry

        def finish(i, carry):
            copy_of(i).wait()
            return carry

        steps = pl.cdiv(reads, together)
        worst = lax.fori_loop(0, steps, step, jnp.zeros((8, HEAD_WIDTH), jnp.float32))
        if final:
            lax.fori_loop(0, reads, finish, 0)

        @pl.when(jnp.logical_not(jnp.max(worst) < MOST))
        def _():
            def again(i, carry):
                where = pl.ds(pl.multiple_of(i * group, group), group)
                scores = score(
                    query_rows(received, order, bias, i, size),
                    keys_of(early, rest, 0, tokens), block_of[...],
                )
                before = level_in[where, :]
                top = jnp.max(scores, axis=1, keepdims=True) * SCALE
                now = jnp.maximum(before, top)
                factor = jnp.exp2(before - now)
                sums = jnp.concatenate([factor, factor], axis=1) * state_in[where, :] + jnp.dot(
                    weigh(scores, now[:, :1]), values_of(early, rest, 0, tokens),
                    preferred_element_type=jnp.float32,
                )
                level[where, :] = now
                keep(i, sums)
                if final:
                    copy_of(i).start()
                    copy_of(i).wait()
                return carry

            lax.fori_loop(0, reads, again, 0)

    part = first // (blocks // 4)
    more = jnp.int32(0)
    if offset < REACH:
        more, _ = reach_of(lengths, place, offset + 1, blocks)
        pl.when((reads > 0) & (more > 0))(functools.partial(over, 0, 4, False))
    for n, together in enumerate((4, 4, 8, 8)):
        pl.when((reads > 0) & (more == 0) & (part == n))(
            functools.partial(over, n * (tokens // 4), together, True)
        )


def per_device(queries, keys, values, dest_replica, dest_slot, doc_lengths, tile_mask):
    tokens = queries.shape[1]
    width = queries.shape[2]
    blocks = dest_replica.shape[1]
    size = tokens // blocks
    packs = lax.axis_size("dp")
    cap = blocks // packs
    bf16, f32 = jnp.bfloat16, jnp.float32
    rows = tokens * QUERY_HEADS
    params = pltpu.CompilerParams(vmem_limit_bytes=VMEM_LIMIT)
    small = pltpu.CompilerParams(vmem_limit_bytes=VMEM_SMALL)

    def cost(flops, moved):
        return pl.CostEstimate(flops=flops, bytes_accessed=moved, transcendentals=0)

    def route(sent):
        return lax.all_to_all(sent, "dp", split_axis=0, concat_axis=0, tiled=True)

    dma = pltpu.SemaphoreType.DMA
    counts = pltpu.SMEM((packs,), jnp.int32)
    kv_send = pl.pallas_call(
        functools.partial(pack_kv_kernel, cap),
        out_shape=jax.ShapeDtypeStruct((packs, 2 * cap * size + SLOT_ROWS, HEAD_WIDTH), bf16),
        in_specs=[SMEM, SMEM, VMEM, VMEM],
        out_specs=VMEM,
        scratch_shapes=[counts, pltpu.SMEM((blocks,), jnp.int32)],
        cost_estimate=cost(0, 4 * tokens * HEAD_WIDTH * 2),
        name="pack_kv",
    )(dest_replica, dest_slot, keys, values)
    kv_recv = route(kv_send)
    q_send, bias, block_of = pl.pallas_call(
        functools.partial(pack_q_kernel, cap),
        out_shape=(
            jax.ShapeDtypeStruct((packs, cap * size, width), bf16),
            jax.ShapeDtypeStruct((REACH + 1, blocks, HEAD_WIDTH), f32),
            jax.ShapeDtypeStruct((tokens, HEAD_WIDTH), bf16),
        ),
        in_specs=[SMEM, SMEM, VMEM, VMEM],
        out_specs=(VMEM, VMEM, VMEM),
        scratch_shapes=[counts],
        compiler_params=small,
        cost_estimate=cost(0, 2 * tokens * width * 2),
        name="pack_q",
    )(dest_replica, doc_lengths, tile_mask, queries)
    q_recv = route(q_send).reshape(tokens, width)
    piece = tokens * PIECE // 4
    early, rest, order = pl.pallas_call(
        functools.partial(place_kernel, cap),
        out_shape=(
            jax.ShapeDtypeStruct((piece, HEAD_WIDTH), bf16),
            jax.ShapeDtypeStruct((2 * tokens - piece, HEAD_WIDTH), bf16),
            jax.ShapeDtypeStruct((1, blocks), jnp.int32),
        ),
        in_specs=[VMEM],
        out_specs=(VMEM, VMEM, SMEM),
        scratch_shapes=[pltpu.VMEM((2 * tokens, HEAD_WIDTH), bf16)],
        compiler_params=small,
        cost_estimate=cost(0, 4 * tokens * HEAD_WIDTH * 2),
        name="place_kv",
    )(kv_recv)

    out_shape = jax.ShapeDtypeStruct((1, tokens, width), bf16)
    level_shape = jax.ShapeDtypeStruct((rows, HEAD_WIDTH), f32)
    sums_shape = jax.ShapeDtypeStruct((rows, 2 * HEAD_WIDTH), f32)
    stage = pltpu.VMEM((tokens, width), bf16)

    def attend_back(offset, early, rest, out, level, sums):
        last = offset == REACH
        return pl.pallas_call(
            functools.partial(hop_kernel, offset),
            out_shape=(out_shape, level_shape) + (() if last else (sums_shape,)),
            in_specs=[SMEM, SMEM] + [VMEM] * 5 + [ANY, VMEM, VMEM],
            out_specs=(ANY, VMEM) + (() if last else (VMEM,)),
            scratch_shapes=[stage, dma],
            input_output_aliases={7: 0, 8: 1},
            compiler_params=params,
            cost_estimate=cost(2 * 2 * rows * tokens * HEAD_WIDTH, 8 * tokens * width),
            name=f"attend_back_{offset}",
        )(order, doc_lengths, bias, block_of, q_recv, early, rest, out, level, sums)

    back_early = shifted(early, "ctx")
    back_rest = shifted(rest, "ctx")
    out, sums, level = pl.pallas_call(
        own_kernel,
        out_shape=(out_shape, sums_shape, level_shape),
        in_specs=[SMEM] + [VMEM] * 5,
        out_specs=(ANY, VMEM, VMEM),
        scratch_shapes=[stage, dma((blocks,))],
        compiler_params=params,
        cost_estimate=cost(2 * rows * tokens * HEAD_WIDTH, 8 * tokens * width),
        name="attend_own",
    )(order, bias, block_of, q_recv, early, rest)
    far_rest, out, sums, level = lax.optimization_barrier((back_rest, out, sums, level))
    far_early = shifted(back_early, "ctx")
    far_rest = shifted(far_rest, "ctx")
    out, level, sums = attend_back(1, back_early, back_rest, out, level, sums)
    return attend_back(2, far_early, far_rest, out, level, sums)[0]


def solution(mesh):
    return jax.shard_map(
        per_device,
        mesh=mesh,
        in_specs=(
            P("dp", "ctx", None),
            P("dp", "ctx", None),
            P("dp", "ctx", None),
            P("dp", "ctx"),
            P("dp", "ctx"),
            P("dp", None),
            P("dp", "ctx", None),
        ),
        out_specs=P("dp", "ctx", None),
        check_vma=False,
    )
```

```python
import functools

import jax
import jax.numpy as jnp
from jax import lax
from jax.experimental import pallas as pl
from jax.experimental.pallas import tpu as pltpu
from jax.sharding import PartitionSpec as P

HEAD_WIDTH = 128
QUERY_HEADS = 4
SCALE = HEAD_WIDTH ** (-0.5) * 1.4426950408889634
NEVER = -1e30
MOST = 1e30
CHUNK = 256
SLOT_ROWS = 16
REACH = 2
PIECE = 3
VMEM_LIMIT = 32 * 1024 * 1024
VMEM_SMALL = 8 * 1024 * 1024

ANY = pl.BlockSpec(memory_space=pl.ANY)
SMEM = pl.BlockSpec(memory_space=pltpu.SMEM)
VMEM = pl.BlockSpec(memory_space=pltpu.VMEM)


def shifted(value, axis):
    count = lax.axis_size(axis)
    return lax.ppermute(value, axis, [(source, source + 1) for source in range(count - 1)])


def pack_kv_kernel(cap, targets, slots, keys, values, send, counts, slot_of):
    packs = send.shape[0]
    blocks = targets.shape[1]
    size = keys.shape[1] // blocks
    half = cap * size
    for t in range(packs):
        counts[t] = 0
    for j in range(blocks):
        t = targets[0, j]
        rank = counts[t]
        counts[t] = rank + 1
        slot_of[t * cap + rank] = lax.rem(slots[0, j], blocks)
        rows = slice(j * size, (j + 1) * size)
        to = pl.multiple_of(rank * size, size)
        send[t, pl.ds(to, size), :] = keys[0, rows, :]
        send[t, pl.ds(to + half, size), :] = values[0, rows, :]
    row = lax.broadcasted_iota(jnp.int32, (SLOT_ROWS, HEAD_WIDTH), 0)
    for t in range(packs):
        listed = jnp.zeros(row.shape, jnp.int32)
        for i in range(cap):
            listed = jnp.where(row == i, slot_of[t * cap + i], listed)
        send[t, 2 * half:, :] = listed.astype(jnp.float32).astype(jnp.bfloat16)


def pack_q_kernel(cap, targets, lengths, tiles, queries, send, bias, block_of, counts):
    packs = send.shape[0]
    blocks = targets.shape[1]
    tokens = queries.shape[1]
    size = tokens // blocks
    place = lax.axis_index("ctx")
    for t in range(packs):
        counts[t] = 0
    for j in range(blocks):
        t = targets[0, j]
        rank = counts[t]
        counts[t] = rank + 1
        to = pl.multiple_of(rank * size, size)
        send[t, pl.ds(to, size), :] = queries[0, j * size:(j + 1) * size, :]

    block = lax.broadcasted_iota(jnp.int32, (tokens, HEAD_WIDTH), 1)
    of_key = lax.broadcasted_iota(jnp.int32, (tokens, HEAD_WIDTH), 0) // size
    block_of[...] = (block == of_key).astype(jnp.float32).astype(jnp.bfloat16)
    query_block = place * blocks + lax.broadcasted_iota(jnp.int32, (blocks, 1), 0)
    listed_tiles = tiles[0].astype(jnp.float32).astype(jnp.bfloat16)
    for offset in range(bias.shape[0]):
        low = (place - offset) * blocks
        key_block = low + lax.broadcasted_iota(jnp.int32, (1, HEAD_WIDTH), 1)
        key_doc = jnp.zeros((1, HEAD_WIDTH), jnp.int32)
        query_doc = jnp.zeros((blocks, 1), jnp.int32)
        end = jnp.int32(0)
        for j in range(lengths.shape[1]):
            end = end + lengths[0, j]
            key_doc = key_doc + (key_block >= end).astype(jnp.int32)
            query_doc = query_doc + (query_block >= end).astype(jnp.int32)
        spread = lax.broadcasted_iota(jnp.int32, (tiles.shape[2], HEAD_WIDTH), 0) == key_block
        listed = jnp.dot(
            listed_tiles, spread.astype(jnp.float32).astype(jnp.bfloat16),
            preferred_element_type=jnp.float32,
        )
        allowed = (query_doc == key_doc) & (key_block <= query_block) & (key_block >= 0)
        allowed = allowed & ((listed > 0.5) | (key_block == query_block))
        bias[offset] = jnp.where(allowed, 0.0, NEVER)


def place_kernel(cap, received, early, rest, order, placed):
    packs = received.shape[0]
    tokens = placed.shape[0] // 2
    size = tokens // (packs * cap)
    half = cap * size
    for s in range(packs):
        listed = received[s, 2 * half:, :].astype(jnp.float32).astype(jnp.int32)
        for i in range(cap):
            slot = listed[i, 0]
            order[0, slot] = s * cap + i
            to = pl.multiple_of(slot * size, size)
            placed[pl.ds(to, size), :] = received[s, i * size:(i + 1) * size, :]
            placed[pl.ds(to + tokens, size), :] = (
                received[s, half + i * size:half + (i + 1) * size, :]
            )
    early[...] = placed[:early.shape[0], :]
    rest[...] = placed[early.shape[0]:, :]


def first_document(lengths, position):
    start, end = jnp.int32(0), jnp.int32(0)
    total = jnp.int32(0)
    for j in range(lengths.shape[1]):
        after = total + lengths[0, j]
        inside = (total <= position) & (position < after)
        start = jnp.where(inside, total, start)
        end = jnp.where(inside, after, end)
        total = after
    return start, end


def reach_of(lengths, place, offset, blocks):
    start, end = first_document(lengths, place * blocks)
    low = (place - offset) * blocks
    rows = jnp.where(start < low + blocks, jnp.minimum(end - place * blocks, blocks), 0)
    return jnp.where(low >= 0, rows, 0), jnp.maximum(start - low, 0)


def keys_of(early, rest, low, high):
    half = early.shape[0]
    if high <= half:
        return early[low:high, :]
    if low >= half:
        return rest[low - half:high - half, :]
    return jnp.concatenate([early[low:, :], rest[:high - half, :]], axis=0)


def values_of(early, rest, low, high):
    values = (early.shape[0] + rest.shape[0]) // 2 - early.shape[0]
    return beside_ones(rest[values + low:values + high, :])


def beside_ones(values):
    return jnp.concatenate([values, jnp.ones(values.shape, values.dtype)], axis=1)


def query_rows(received, order, bias, i, size):
    source = pl.ds(pl.multiple_of(order[0, i] * size, size), size)
    barred = jnp.broadcast_to(bias[pl.ds(i, 1), :], (QUERY_HEADS * size, HEAD_WIDTH))
    return jnp.concatenate(
        [heads_as_rows(received[source, :]), barred.astype(jnp.bfloat16)], axis=1
    )


def pair_rows(received, order, bias, i, size):
    return jnp.concatenate(
        [query_rows(received, order, bias, i + u, size) for u in range(2)], axis=0
    )


def score(rows, keys, block_of):
    return lax.dot_general(
        rows, jnp.concatenate([keys, block_of], axis=1), (((1,), (1,)), ((), ())),
        preferred_element_type=jnp.float32,
    )


def weigh(scores, level):
    return jnp.exp2(scores * SCALE - level).astype(jnp.bfloat16)


def largest(sums, so_far):
    parts = sums[:, HEAD_WIDTH:]
    return jnp.maximum(so_far, jnp.max(parts.reshape(-1, 8, HEAD_WIDTH), axis=0))


def divided(sums, size):
    ratio = sums[:, :HEAD_WIDTH] / sums[:, HEAD_WIDTH:]
    group = QUERY_HEADS * size
    return jnp.concatenate(
        [heads_as_columns(ratio[u:u + group], size) for u in range(0, ratio.shape[0], group)],
        axis=0,
    ).astype(jnp.bfloat16)


def heads_as_rows(block):
    return jnp.concatenate(
        [block[:, h * HEAD_WIDTH:(h + 1) * HEAD_WIDTH] for h in range(QUERY_HEADS)], axis=0
    )


def heads_as_columns(rows, size):
    return jnp.concatenate(
        [rows[h * size:(h + 1) * size] for h in range(QUERY_HEADS)], axis=1
    )


def own_kernel(
    order, bias_in, block_of, received, early, rest,
    out, state, level,
    stage, sem,
):
    bias = bias_in.at[0]
    blocks = bias.shape[0]
    tokens = (early.shape[0] + rest.shape[0]) // 2
    size = tokens // blocks
    group = QUERY_HEADS * size
    row = lax.broadcasted_iota(jnp.int32, (2 * group, 2 * size), 0)
    lane = lax.broadcasted_iota(jnp.int32, (2 * group, 2 * size), 1)
    later = lane - (row // group) * size > lax.rem(row, size)

    work = []
    for i in range(0, blocks, 2):
        width = (i + 2) * size
        spans = [(low, min(low + CHUNK, width)) for low in range(0, width, CHUNK)]
        for n, span in enumerate(spans[-1:] + spans[:-1]):
            work.append((i, span, n == 0, n == len(spans) - 1))

    rows = {}

    def start(i, span):
        if i not in rows:
            rows[i] = pair_rows(received, order, bias, i, size)
        return score(rows[i], keys_of(early, rest, *span), block_of[span[0]:span[1], :])

    worst = jnp.zeros((8, HEAD_WIDTH), jnp.float32)
    copies = []
    scores = start(*work[0][:2])
    for n, (i, span, opening, closing) in enumerate(work):
        ahead = start(*work[n + 1][:2]) if n + 1 < len(work) else None
        if opening:
            cut = span[1] - span[0] - 2 * size
            tail = jnp.where(later, NEVER, scores[:, cut:])
            scores = jnp.concatenate([scores[:, :cut], tail], axis=1) if cut else tail
            top = jnp.max(scores, axis=1, keepdims=True) * SCALE
            weights = []
            width = span[1]
        weights.append(weigh(scores, top))
        if closing:
            ordered = weights[1:] + weights[:1]
            joined = jnp.concatenate(ordered, axis=1) if len(ordered) > 1 else ordered[0]
            sums = jnp.dot(
                joined, values_of(early, rest, 0, width), preferred_element_type=jnp.float32
            )
            worst = largest(sums, worst)
            where = slice(i * group, (i + 2) * group)
            held = slice(i * size, (i + 2) * size)
            state[where, :] = sums
            level[where, :] = jnp.broadcast_to(top, (2 * group, HEAD_WIDTH))
            stage[held, :] = divided(sums, size)
            copy = pltpu.make_async_copy(stage.at[held], out.at[0, held], sem.at[i])
            copy.start()
            copies.append(copy)
        scores = ahead
    for copy in copies:
        copy.wait()

    @pl.when(jnp.logical_not(jnp.max(worst) < MOST))
    def _():
        def again(i, carry):
            where = pl.ds(pl.multiple_of(i * group, group), group)
            held = pl.ds(pl.multiple_of(i * size, size), size)
            scores = score(
                query_rows(received, order, bias, i, size),
                keys_of(early, rest, 0, tokens), block_of[...],
            )
            query = i * size + lax.rem(lax.broadcasted_iota(jnp.int32, scores.shape, 0), size)
            key = lax.broadcasted_iota(jnp.int32, scores.shape, 1)
            scores = jnp.where(key > query, NEVER, scores)
            top = jnp.max(scores, axis=1, keepdims=True) * SCALE
            sums = jnp.dot(
                weigh(scores, top), values_of(early, rest, 0, tokens),
                preferred_element_type=jnp.float32,
            )
            state[where, :] = sums
            level[where, :] = jnp.broadcast_to(top, (group, HEAD_WIDTH))
            stage[held, :] = divided(sums, size)
            copy = pltpu.make_async_copy(stage.at[held], out.at[0, held], sem.at[0])
            copy.start()
            copy.wait()
            return carry

        lax.fori_loop(0, blocks, again, 0)


def hop_kernel(
    offset, order, lengths, bias_in, block_of, received, early, rest,
    out_in, level_in, state_in, *refs,
):
    stage, sem = refs[-2:]
    out, level = refs[0], refs[1]
    place = lax.axis_index("ctx")
    bias = bias_in.at[offset]
    blocks = bias.shape[0]
    tokens = (early.shape[0] + rest.shape[0]) // 2
    size = tokens // blocks
    group = QUERY_HEADS * size
    reads, first = reach_of(lengths, place, offset, blocks)

    def over(low, together, final):
        def keep(i, sums):
            count = sums.shape[0]
            if offset < REACH:
                refs[2][pl.ds(pl.multiple_of(i * group, group), count), :] = sums
            if final:
                held = pl.ds(pl.multiple_of(i * size, size), count // QUERY_HEADS)
                stage[held, :] = divided(sums, size)

        spans = [(at, at + CHUNK) for at in range(low, tokens, CHUNK)]
        work = [(u, span) for u in range(0, together, 2) for span in spans]

        def step(n, worst):
            i = n * together
            rows = {}

            def start(u, span):
                if u not in rows:
                    rows[u] = pair_rows(received, order, bias, i + u, size)
                return score(rows[u], keys_of(early, rest, *span), block_of[span[0]:span[1], :])

            scores = start(*work[0])
            for m, (u, span) in enumerate(work):
                ahead = start(*work[m + 1]) if m + 1 < len(work) else None
                where = pl.ds(pl.multiple_of((i + u) * group, group), 2 * group)
                if span is spans[0]:
                    base = level_in[where, :]
                    base = jnp.concatenate([base] * (CHUNK // HEAD_WIDTH), axis=1)
                    weights = []
                weights.append(weigh(scores, base))
                if span is spans[-1]:
                    joined = jnp.concatenate(weights, axis=1) if len(weights) > 1 else weights[0]
                    sums = state_in[where, :] + jnp.dot(
                        joined, values_of(early, rest, low, tokens), preferred_element_type=jnp.float32
                    )
                    worst = jnp.where(i + u < reads, largest(sums, worst), worst)
                    keep(i + u, sums)
                scores = ahead
            if final:
                lax.fori_loop(i, jnp.minimum(i + together, reads), send, 0)
            return worst

        def copy_of(i):
            held = pl.ds(pl.multiple_of(i * size, size), size)
            return pltpu.make_async_copy(stage.at[held], out.at[0, held], sem)

        def send(i, carry):
            copy_of(i).start()
            return carry

        def finish(i, carry):
            copy_of(i).wait()
            return carry

        steps = pl.cdiv(reads, together)
        worst = lax.fori_loop(0, steps, step, jnp.zeros((8, HEAD_WIDTH), jnp.float32))
        if final:
            lax.fori_loop(0, reads, finish, 0)

        @pl.when(jnp.logical_not(jnp.max(worst) < MOST))
        def _():
            def again(i, carry):
                where = pl.ds(pl.multiple_of(i * group, group), group)
                scores = score(
                    query_rows(received, order, bias, i, size),
                    keys_of(early, rest, 0, tokens), block_of[...],
                )
                before = level_in[where, :]
                top = jnp.max(scores, axis=1, keepdims=True) * SCALE
                now = jnp.maximum(before, top)
                factor = jnp.exp2(before - now)
                sums = jnp.concatenate([factor, factor], axis=1) * state_in[where, :] + jnp.dot(
                    weigh(scores, now[:, :1]), values_of(early, rest, 0, tokens),
                    preferred_element_type=jnp.float32,
                )
                level[where, :] = now
                keep(i, sums)
                if final:
                    copy_of(i).start()
                    copy_of(i).wait()
                return carry

            lax.fori_loop(0, reads, again, 0)

    part = first // (blocks // 4)
    more = jnp.int32(0)
    if offset < REACH:
        more, _ = reach_of(lengths, place, offset + 1, blocks)
        pl.when((reads > 0) & (more > 0))(functools.partial(over, 0, 4, False))
    for n, together in enumerate((4, 4, 8, 8)):
        pl.when((reads > 0) & (more == 0) & (part == n))(
            functools.partial(over, n * (tokens // 4), together, True)
        )


def per_device(queries, keys, values, dest_replica, dest_slot, doc_lengths, tile_mask):
    tokens = queries.shape[1]
    width = queries.shape[2]
    blocks = dest_replica.shape[1]
    size = tokens // blocks
    packs = lax.axis_size("dp")
    cap = blocks // packs
    bf16, f32 = jnp.bfloat16, jnp.float32
    rows = tokens * QUERY_HEADS
    params = pltpu.CompilerParams(vmem_limit_bytes=VMEM_LIMIT)
    small = pltpu.CompilerParams(vmem_limit_bytes=VMEM_SMALL)

    def cost(flops, moved):
        return pl.CostEstimate(flops=flops, bytes_accessed=moved, transcendentals=0)

    def route(sent):
        return lax.all_to_all(sent, "dp", split_axis=0, concat_axis=0, tiled=True)

    dma = pltpu.SemaphoreType.DMA
    counts = pltpu.SMEM((packs,), jnp.int32)
    kv_send = pl.pallas_call(
        functools.partial(pack_kv_kernel, cap),
        out_shape=jax.ShapeDtypeStruct((packs, 2 * cap * size + SLOT_ROWS, HEAD_WIDTH), bf16),
        in_specs=[SMEM, SMEM, VMEM, VMEM],
        out_specs=VMEM,
        scratch_shapes=[counts, pltpu.SMEM((blocks,), jnp.int32)],
        cost_estimate=cost(0, 4 * tokens * HEAD_WIDTH * 2),
        name="pack_kv",
    )(dest_replica, dest_slot, keys, values)
    kv_recv = route(kv_send)
    q_send, bias, block_of = pl.pallas_call(
        functools.partial(pack_q_kernel, cap),
        out_shape=(
            jax.ShapeDtypeStruct((packs, cap * size, width), bf16),
            jax.ShapeDtypeStruct((REACH + 1, blocks, HEAD_WIDTH), f32),
            jax.ShapeDtypeStruct((tokens, HEAD_WIDTH), bf16),
        ),
        in_specs=[SMEM, SMEM, VMEM, VMEM],
        out_specs=(VMEM, VMEM, VMEM),
        scratch_shapes=[counts],
        compiler_params=small,
        cost_estimate=cost(0, 2 * tokens * width * 2),
        name="pack_q",
    )(dest_replica, doc_lengths, tile_mask, queries)
    q_recv = route(q_send).reshape(tokens, width)
    piece = tokens * PIECE // 4
    early, rest, order = pl.pallas_call(
        functools.partial(place_kernel, cap),
        out_shape=(
            jax.ShapeDtypeStruct((piece, HEAD_WIDTH), bf16),
            jax.ShapeDtypeStruct((2 * tokens - piece, HEAD_WIDTH), bf16),
            jax.ShapeDtypeStruct((1, blocks), jnp.int32),
        ),
        in_specs=[VMEM],
        out_specs=(VMEM, VMEM, SMEM),
        scratch_shapes=[pltpu.VMEM((2 * tokens, HEAD_WIDTH), bf16)],
        compiler_params=small,
        cost_estimate=cost(0, 4 * tokens * HEAD_WIDTH * 2),
        name="place_kv",
    )(kv_recv)

    out_shape = jax.ShapeDtypeStruct((1, tokens, width), bf16)
    level_shape = jax.ShapeDtypeStruct((rows, HEAD_WIDTH), f32)
    sums_shape = jax.ShapeDtypeStruct((rows, 2 * HEAD_WIDTH), f32)
    stage = pltpu.VMEM((tokens, width), bf16)

    def attend_back(offset, early, rest, out, level, sums):
        last = offset == REACH
        return pl.pallas_call(
            functools.partial(hop_kernel, offset),
            out_shape=(out_shape, level_shape) + (() if last else (sums_shape,)),
            in_specs=[SMEM, SMEM] + [VMEM] * 5 + [ANY, VMEM, VMEM],
            out_specs=(ANY, VMEM) + (() if last else (VMEM,)),
            scratch_shapes=[stage, dma],
            input_output_aliases={7: 0, 8: 1},
            compiler_params=params,
            cost_estimate=cost(2 * 2 * rows * tokens * HEAD_WIDTH, 8 * tokens * width),
            name=f"attend_back_{offset}",
        )(order, doc_lengths, bias, block_of, q_recv, early, rest, out, level, sums)

    back_early = shifted(early, "ctx")
    back_rest = shifted(rest, "ctx")
    out, sums, level = pl.pallas_call(
        own_kernel,
        out_shape=(out_shape, sums_shape, level_shape),
        in_specs=[SMEM] + [VMEM] * 5,
        out_specs=(ANY, VMEM, VMEM),
        scratch_shapes=[stage, dma((blocks,))],
        compiler_params=params,
        cost_estimate=cost(2 * rows * tokens * HEAD_WIDTH, 8 * tokens * width),
        name="attend_own",
    )(order, bias, block_of, q_recv, early, rest)
    far_rest, out, sums, level = lax.optimization_barrier((back_rest, out, sums, level))
    far_early = shifted(back_early, "ctx")
    far_rest = shifted(far_rest, "ctx")
    out, level, sums = attend_back(1, back_early, back_rest, out, level, sums)
    return attend_back(2, far_early, far_rest, out, level, sums)[0]


def solution(mesh):
    return jax.shard_map(
        per_device,
        mesh=mesh,
        in_specs=(
            P("dp", "ctx", None),
            P("dp", "ctx", None),
            P("dp", "ctx", None),
            P("dp", "ctx"),
            P("dp", "ctx"),
            P("dp", None),
            P("dp", "ctx", None),
        ),
        out_specs=P("dp", "ctx", None),
        check_vma=False,
    )
```

```python
import functools

import jax
import jax.numpy as jnp
from jax import lax
from jax.experimental import pallas as pl
from jax.experimental.pallas import tpu as pltpu
from jax.sharding import PartitionSpec as P

HEAD_WIDTH = 128
QUERY_HEADS = 4
SCALE = HEAD_WIDTH ** (-0.5) * 1.4426950408889634
NEVER = -1e30
MOST = 1e30
CHUNK = 256
SLOT_ROWS = 16
REACH = 2
PIECE = 4
VMEM_LIMIT = 32 * 1024 * 1024
VMEM_SMALL = 8 * 1024 * 1024

ANY = pl.BlockSpec(memory_space=pl.ANY)
SMEM = pl.BlockSpec(memory_space=pltpu.SMEM)
VMEM = pl.BlockSpec(memory_space=pltpu.VMEM)


def shifted(value, axis):
    count = lax.axis_size(axis)
    return lax.ppermute(value, axis, [(source, source + 1) for source in range(count - 1)])


def pack_kv_kernel(cap, targets, slots, keys, values, send, counts, slot_of):
    packs = send.shape[0]
    blocks = targets.shape[1]
    size = keys.shape[1] // blocks
    half = cap * size
    for t in range(packs):
        counts[t] = 0
    for j in range(blocks):
        t = targets[0, j]
        rank = counts[t]
        counts[t] = rank + 1
        slot_of[t * cap + rank] = lax.rem(slots[0, j], blocks)
        rows = slice(j * size, (j + 1) * size)
        to = pl.multiple_of(rank * size, size)
        send[t, pl.ds(to, size), :] = keys[0, rows, :]
        send[t, pl.ds(to + half, size), :] = values[0, rows, :]
    row = lax.broadcasted_iota(jnp.int32, (SLOT_ROWS, HEAD_WIDTH), 0)
    for t in range(packs):
        listed = jnp.zeros(row.shape, jnp.int32)
        for i in range(cap):
            listed = jnp.where(row == i, slot_of[t * cap + i], listed)
        send[t, 2 * half:, :] = listed.astype(jnp.float32).astype(jnp.bfloat16)


def pack_q_kernel(cap, targets, lengths, tiles, queries, send, bias, block_of, counts):
    packs = send.shape[0]
    blocks = targets.shape[1]
    tokens = queries.shape[1]
    size = tokens // blocks
    place = lax.axis_index("ctx")
    for t in range(packs):
        counts[t] = 0
    for j in range(blocks):
        t = targets[0, j]
        rank = counts[t]
        counts[t] = rank + 1
        to = pl.multiple_of(rank * size, size)
        send[t, pl.ds(to, size), :] = queries[0, j * size:(j + 1) * size, :]

    block = lax.broadcasted_iota(jnp.int32, (tokens, HEAD_WIDTH), 1)
    of_key = lax.broadcasted_iota(jnp.int32, (tokens, HEAD_WIDTH), 0) // size
    block_of[...] = (block == of_key).astype(jnp.float32).astype(jnp.bfloat16)
    query_block = place * blocks + lax.broadcasted_iota(jnp.int32, (blocks, 1), 0)
    listed_tiles = tiles[0].astype(jnp.float32).astype(jnp.bfloat16)
    for offset in range(bias.shape[0]):
        low = (place - offset) * blocks
        key_block = low + lax.broadcasted_iota(jnp.int32, (1, HEAD_WIDTH), 1)
        key_doc = jnp.zeros((1, HEAD_WIDTH), jnp.int32)
        query_doc = jnp.zeros((blocks, 1), jnp.int32)
        end = jnp.int32(0)
        for j in range(lengths.shape[1]):
            end = end + lengths[0, j]
            key_doc = key_doc + (key_block >= end).astype(jnp.int32)
            query_doc = query_doc + (query_block >= end).astype(jnp.int32)
        spread = lax.broadcasted_iota(jnp.int32, (tiles.shape[2], HEAD_WIDTH), 0) == key_block
        listed = jnp.dot(
            listed_tiles, spread.astype(jnp.float32).astype(jnp.bfloat16),
            preferred_element_type=jnp.float32,
        )
        allowed = (query_doc == key_doc) & (key_block <= query_block) & (key_block >= 0)
        allowed = allowed & ((listed > 0.5) | (key_block == query_block))
        bias[offset] = jnp.where(allowed, 0.0, NEVER)


def place_kernel(cap, received, early, rest, order, placed):
    packs = received.shape[0]
    tokens = placed.shape[0] // 2
    size = tokens // (packs * cap)
    half = cap * size
    for s in range(packs):
        listed = received[s, 2 * half:, :].astype(jnp.float32).astype(jnp.int32)
        for i in range(cap):
            slot = listed[i, 0]
            order[0, slot] = s * cap + i
            to = pl.multiple_of(slot * size, size)
            placed[pl.ds(to, size), :] = received[s, i * size:(i + 1) * size, :]
            placed[pl.ds(to + tokens, size), :] = (
                received[s, half + i * size:half + (i + 1) * size, :]
            )
    early[...] = placed[:early.shape[0], :]
    rest[...] = placed[early.shape[0]:, :]


def first_document(lengths, position):
    start, end = jnp.int32(0), jnp.int32(0)
    total = jnp.int32(0)
    for j in range(lengths.shape[1]):
        after = total + lengths[0, j]
        inside = (total <= position) & (position < after)
        start = jnp.where(inside, total, start)
        end = jnp.where(inside, after, end)
        total = after
    return start, end


def reach_of(lengths, place, offset, blocks):
    start, end = first_document(lengths, place * blocks)
    low = (place - offset) * blocks
    rows = jnp.where(start < low + blocks, jnp.minimum(end - place * blocks, blocks), 0)
    return jnp.where(low >= 0, rows, 0), jnp.maximum(start - low, 0)


def keys_of(early, rest, low, high):
    half = early.shape[0]
    if high <= half:
        return early[low:high, :]
    if low >= half:
        return rest[low - half:high - half, :]
    return jnp.concatenate([early[low:, :], rest[:high - half, :]], axis=0)


def values_of(early, rest, low, high):
    values = (early.shape[0] + rest.shape[0]) // 2 - early.shape[0]
    return beside_ones(rest[values + low:values + high, :])


def beside_ones(values):
    return jnp.concatenate([values, jnp.ones(values.shape, values.dtype)], axis=1)


def query_rows(received, order, bias, i, size):
    source = pl.ds(pl.multiple_of(order[0, i] * size, size), size)
    barred = jnp.broadcast_to(bias[pl.ds(i, 1), :], (QUERY_HEADS * size, HEAD_WIDTH))
    return jnp.concatenate(
        [heads_as_rows(received[source, :]), barred.astype(jnp.bfloat16)], axis=1
    )


def pair_rows(received, order, bias, i, size):
    return jnp.concatenate(
        [query_rows(received, order, bias, i + u, size) for u in range(2)], axis=0
    )


def score(rows, keys, block_of):
    return lax.dot_general(
        rows, jnp.concatenate([keys, block_of], axis=1), (((1,), (1,)), ((), ())),
        preferred_element_type=jnp.float32,
    )


def weigh(scores, level):
    return jnp.exp2(scores * SCALE - level).astype(jnp.bfloat16)


def largest(sums, so_far):
    parts = sums[:, HEAD_WIDTH:]
    return jnp.maximum(so_far, jnp.max(parts.reshape(-1, 8, HEAD_WIDTH), axis=0))


def divided(sums, size):
    ratio = sums[:, :HEAD_WIDTH] / sums[:, HEAD_WIDTH:]
    group = QUERY_HEADS * size
    return jnp.concatenate(
        [heads_as_columns(ratio[u:u + group], size) for u in range(0, ratio.shape[0], group)],
        axis=0,
    ).astype(jnp.bfloat16)


def heads_as_rows(block):
    return jnp.concatenate(
        [block[:, h * HEAD_WIDTH:(h + 1) * HEAD_WIDTH] for h in range(QUERY_HEADS)], axis=0
    )


def heads_as_columns(rows, size):
    return jnp.concatenate(
        [rows[h * size:(h + 1) * size] for h in range(QUERY_HEADS)], axis=1
    )


def own_kernel(
    order, bias_in, block_of, received, early, rest,
    out, state, level,
    stage, sem,
):
    bias = bias_in.at[0]
    blocks = bias.shape[0]
    tokens = (early.shape[0] + rest.shape[0]) // 2
    size = tokens // blocks
    group = QUERY_HEADS * size
    row = lax.broadcasted_iota(jnp.int32, (2 * group, 2 * size), 0)
    lane = lax.broadcasted_iota(jnp.int32, (2 * group, 2 * size), 1)
    later = lane - (row // group) * size > lax.rem(row, size)

    work = []
    for i in range(0, blocks, 2):
        width = (i + 2) * size
        spans = [(low, min(low + CHUNK, width)) for low in range(0, width, CHUNK)]
        for n, span in enumerate(spans[-1:] + spans[:-1]):
            work.append((i, span, n == 0, n == len(spans) - 1))

    rows = {}

    def start(i, span):
        if i not in rows:
            rows[i] = pair_rows(received, order, bias, i, size)
        return score(rows[i], keys_of(early, rest, *span), block_of[span[0]:span[1], :])

    worst = jnp.zeros((8, HEAD_WIDTH), jnp.float32)
    copies = []
    scores = start(*work[0][:2])
    for n, (i, span, opening, closing) in enumerate(work):
        ahead = start(*work[n + 1][:2]) if n + 1 < len(work) else None
        if opening:
            cut = span[1] - span[0] - 2 * size
            tail = jnp.where(later, NEVER, scores[:, cut:])
            scores = jnp.concatenate([scores[:, :cut], tail], axis=1) if cut else tail
            top = jnp.max(scores, axis=1, keepdims=True) * SCALE
            weights = []
            width = span[1]
        weights.append(weigh(scores, top))
        if closing:
            ordered = weights[1:] + weights[:1]
            joined = jnp.concatenate(ordered, axis=1) if len(ordered) > 1 else ordered[0]
            sums = jnp.dot(
                joined, values_of(early, rest, 0, width), preferred_element_type=jnp.float32
            )
            worst = largest(sums, worst)
            where = slice(i * group, (i + 2) * group)
            held = slice(i * size, (i + 2) * size)
            state[where, :] = sums
            level[where, :] = jnp.broadcast_to(top, (2 * group, HEAD_WIDTH))
            stage[held, :] = divided(sums, size)
            copy = pltpu.make_async_copy(stage.at[held], out.at[0, held], sem.at[i])
            copy.start()
            copies.append(copy)
        scores = ahead
    for copy in copies:
        copy.wait()

    @pl.when(jnp.logical_not(jnp.max(worst) < MOST))
    def _():
        def again(i, carry):
            where = pl.ds(pl.multiple_of(i * group, group), group)
            held = pl.ds(pl.multiple_of(i * size, size), size)
            scores = score(
                query_rows(received, order, bias, i, size),
                keys_of(early, rest, 0, tokens), block_of[...],
            )
            query = i * size + lax.rem(lax.broadcasted_iota(jnp.int32, scores.shape, 0), size)
            key = lax.broadcasted_iota(jnp.int32, scores.shape, 1)
            scores = jnp.where(key > query, NEVER, scores)
            top = jnp.max(scores, axis=1, keepdims=True) * SCALE
            sums = jnp.dot(
                weigh(scores, top), values_of(early, rest, 0, tokens),
                preferred_element_type=jnp.float32,
            )
            state[where, :] = sums
            level[where, :] = jnp.broadcast_to(top, (group, HEAD_WIDTH))
            stage[held, :] = divided(sums, size)
            copy = pltpu.make_async_copy(stage.at[held], out.at[0, held], sem.at[0])
            copy.start()
            copy.wait()
            return carry

        lax.fori_loop(0, blocks, again, 0)


def hop_kernel(
    offset, order, lengths, bias_in, block_of, received, early, rest,
    out_in, level_in, state_in, *refs,
):
    stage, sem = refs[-2:]
    out, level = refs[0], refs[1]
    place = lax.axis_index("ctx")
    bias = bias_in.at[offset]
    blocks = bias.shape[0]
    tokens = (early.shape[0] + rest.shape[0]) // 2
    size = tokens // blocks
    group = QUERY_HEADS * size
    reads, first = reach_of(lengths, place, offset, blocks)

    def over(low, together, final):
        def keep(i, sums):
            count = sums.shape[0]
            if offset < REACH:
                refs[2][pl.ds(pl.multiple_of(i * group, group), count), :] = sums
            if final:
                held = pl.ds(pl.multiple_of(i * size, size), count // QUERY_HEADS)
                stage[held, :] = divided(sums, size)

        spans = [(at, at + CHUNK) for at in range(low, tokens, CHUNK)]
        work = [(u, span) for u in range(0, together, 2) for span in spans]

        def step(n, worst):
            i = n * together
            rows = {}

            def start(u, span):
                if u not in rows:
                    rows[u] = pair_rows(received, order, bias, i + u, size)
                return score(rows[u], keys_of(early, rest, *span), block_of[span[0]:span[1], :])

            scores = start(*work[0])
            for m, (u, span) in enumerate(work):
                ahead = start(*work[m + 1]) if m + 1 < len(work) else None
                where = pl.ds(pl.multiple_of((i + u) * group, group), 2 * group)
                if span is spans[0]:
                    base = level_in[where, :]
                    base = jnp.concatenate([base] * (CHUNK // HEAD_WIDTH), axis=1)
                    weights = []
                weights.append(weigh(scores, base))
                if span is spans[-1]:
                    joined = jnp.concatenate(weights, axis=1) if len(weights) > 1 else weights[0]
                    sums = state_in[where, :] + jnp.dot(
                        joined, values_of(early, rest, low, tokens), preferred_element_type=jnp.float32
                    )
                    worst = jnp.where(i + u < reads, largest(sums, worst), worst)
                    keep(i + u, sums)
                scores = ahead
            if final:
                lax.fori_loop(i, jnp.minimum(i + together, reads), send, 0)
            return worst

        def copy_of(i):
            held = pl.ds(pl.multiple_of(i * size, size), size)
            return pltpu.make_async_copy(stage.at[held], out.at[0, held], sem)

        def send(i, carry):
            copy_of(i).start()
            return carry

        def finish(i, carry):
            copy_of(i).wait()
            return carry

        steps = pl.cdiv(reads, together)
        worst = lax.fori_loop(0, steps, step, jnp.zeros((8, HEAD_WIDTH), jnp.float32))
        if final:
            lax.fori_loop(0, reads, finish, 0)

        @pl.when(jnp.logical_not(jnp.max(worst) < MOST))
        def _():
            def again(i, carry):
                where = pl.ds(pl.multiple_of(i * group, group), group)
                scores = score(
                    query_rows(received, order, bias, i, size),
                    keys_of(early, rest, 0, tokens), block_of[...],
                )
                before = level_in[where, :]
                top = jnp.max(scores, axis=1, keepdims=True) * SCALE
                now = jnp.maximum(before, top)
                factor = jnp.exp2(before - now)
                sums = jnp.concatenate([factor, factor], axis=1) * state_in[where, :] + jnp.dot(
                    weigh(scores, now[:, :1]), values_of(early, rest, 0, tokens),
                    preferred_element_type=jnp.float32,
                )
                level[where, :] = now
                keep(i, sums)
                if final:
                    copy_of(i).start()
                    copy_of(i).wait()
                return carry

            lax.fori_loop(0, reads, again, 0)

    part = first // (blocks // 4)
    more = jnp.int32(0)
    if offset < REACH:
        more, _ = reach_of(lengths, place, offset + 1, blocks)
        pl.when((reads > 0) & (more > 0))(functools.partial(over, 0, 4, False))
    for n, together in enumerate((8 if offset < REACH else 4, 4, 8, 8)):
        pl.when((reads > 0) & (more == 0) & (part == n))(
            functools.partial(over, n * (tokens // 4), together, True)
        )


def per_device(queries, keys, values, dest_replica, dest_slot, doc_lengths, tile_mask):
    tokens = queries.shape[1]
    width = queries.shape[2]
    blocks = dest_replica.shape[1]
    size = tokens // blocks
    packs = lax.axis_size("dp")
    cap = blocks // packs
    bf16, f32 = jnp.bfloat16, jnp.float32
    rows = tokens * QUERY_HEADS
    params = pltpu.CompilerParams(vmem_limit_bytes=VMEM_LIMIT)
    small = pltpu.CompilerParams(vmem_limit_bytes=VMEM_SMALL)

    def cost(flops, moved):
        return pl.CostEstimate(flops=flops, bytes_accessed=moved, transcendentals=0)

    def route(sent):
        return lax.all_to_all(sent, "dp", split_axis=0, concat_axis=0, tiled=True)

    dma = pltpu.SemaphoreType.DMA
    counts = pltpu.SMEM((packs,), jnp.int32)
    kv_send = pl.pallas_call(
        functools.partial(pack_kv_kernel, cap),
        out_shape=jax.ShapeDtypeStruct((packs, 2 * cap * size + SLOT_ROWS, HEAD_WIDTH), bf16),
        in_specs=[SMEM, SMEM, VMEM, VMEM],
        out_specs=VMEM,
        scratch_shapes=[counts, pltpu.SMEM((blocks,), jnp.int32)],
        cost_estimate=cost(0, 4 * tokens * HEAD_WIDTH * 2),
        name="pack_kv",
    )(dest_replica, dest_slot, keys, values)
    kv_recv = route(kv_send)
    q_send, bias, block_of = pl.pallas_call(
        functools.partial(pack_q_kernel, cap),
        out_shape=(
            jax.ShapeDtypeStruct((packs, cap * size, width), bf16),
            jax.ShapeDtypeStruct((REACH + 1, blocks, HEAD_WIDTH), f32),
            jax.ShapeDtypeStruct((tokens, HEAD_WIDTH), bf16),
        ),
        in_specs=[SMEM, SMEM, VMEM, VMEM],
        out_specs=(VMEM, VMEM, VMEM),
        scratch_shapes=[counts],
        compiler_params=small,
        cost_estimate=cost(0, 2 * tokens * width * 2),
        name="pack_q",
    )(dest_replica, doc_lengths, tile_mask, queries)
    q_recv = route(q_send).reshape(tokens, width)
    piece = tokens * PIECE // 4
    early, rest, order = pl.pallas_call(
        functools.partial(place_kernel, cap),
        out_shape=(
            jax.ShapeDtypeStruct((piece, HEAD_WIDTH), bf16),
            jax.ShapeDtypeStruct((2 * tokens - piece, HEAD_WIDTH), bf16),
            jax.ShapeDtypeStruct((1, blocks), jnp.int32),
        ),
        in_specs=[VMEM],
        out_specs=(VMEM, VMEM, SMEM),
        scratch_shapes=[pltpu.VMEM((2 * tokens, HEAD_WIDTH), bf16)],
        compiler_params=small,
        cost_estimate=cost(0, 4 * tokens * HEAD_WIDTH * 2),
        name="place_kv",
    )(kv_recv)

    out_shape = jax.ShapeDtypeStruct((1, tokens, width), bf16)
    level_shape = jax.ShapeDtypeStruct((rows, HEAD_WIDTH), f32)
    sums_shape = jax.ShapeDtypeStruct((rows, 2 * HEAD_WIDTH), f32)
    stage = pltpu.VMEM((tokens, width), bf16)

    def attend_back(offset, early, rest, out, level, sums):
        last = offset == REACH
        return pl.pallas_call(
            functools.partial(hop_kernel, offset),
            out_shape=(out_shape, level_shape) + (() if last else (sums_shape,)),
            in_specs=[SMEM, SMEM] + [VMEM] * 5 + [ANY, VMEM, VMEM],
            out_specs=(ANY, VMEM) + (() if last else (VMEM,)),
            scratch_shapes=[stage, dma],
            input_output_aliases={7: 0, 8: 1},
            compiler_params=params,
            cost_estimate=cost(2 * 2 * rows * tokens * HEAD_WIDTH, 8 * tokens * width),
            name=f"attend_back_{offset}",
        )(order, doc_lengths, bias, block_of, q_recv, early, rest, out, level, sums)

    back_early = shifted(early, "ctx")
    back_rest = shifted(rest, "ctx")
    out, sums, level = pl.pallas_call(
        own_kernel,
        out_shape=(out_shape, sums_shape, level_shape),
        in_specs=[SMEM] + [VMEM] * 5,
        out_specs=(ANY, VMEM, VMEM),
        scratch_shapes=[stage, dma((blocks,))],
        compiler_params=params,
        cost_estimate=cost(2 * rows * tokens * HEAD_WIDTH, 8 * tokens * width),
        name="attend_own",
    )(order, bias, block_of, q_recv, early, rest)
    far_rest, out, sums, level = lax.optimization_barrier((back_rest, out, sums, level))
    far_early = shifted(back_early, "ctx")
    far_rest = shifted(far_rest, "ctx")
    out, level, sums = attend_back(1, back_early, back_rest, out, level, sums)
    return attend_back(2, far_early, far_rest, out, level, sums)[0]


def solution(mesh):
    return jax.shard_map(
        per_device,
        mesh=mesh,
        in_specs=(
            P("dp", "ctx", None),
            P("dp", "ctx", None),
            P("dp", "ctx", None),
            P("dp", "ctx"),
            P("dp", "ctx"),
            P("dp", None),
            P("dp", "ctx", None),
        ),
        out_specs=P("dp", "ctx", None),
        check_vma=False,
    )
```
